256 devices in a mesh: tower: 8 (over y, x_hi), seq: 16 (over x_lo, z), dp: 2 (over core).
Axes of the slice: x: 4 (x_hi: 2, x_lo: 2; x = x_hi * 2 + x_lo), y: 4, z: 8, core: 2. Of those that a mesh axis runs over, the one named last changes fastest.
Arguments:
- video_query: bfloat16 [2, 8192, 3072], P('dp', 'seq', 'tower'), may hold values from -8 to 8
- audio_key: bfloat16 [2, 1024, 3072], P('dp', 'seq', 'tower'), may hold values from -8 to 8
- audio_value: bfloat16 [2, 1024, 3072], P('dp', 'seq', 'tower'), may hold values from -6 to 6
- audio_query: bfloat16 [2, 1024, 3072], P('dp', 'seq', 'tower'), may hold values from -8 to 8
- video_key: bfloat16 [2, 8192, 3072], P('dp', 'seq', 'tower'), may hold values from -8 to 8
- video_value_rows: bfloat16 [2, 8192, 3072], P('dp', 'seq', 'tower'), may hold values from -6 to 6
- video_upstream: bfloat16 [2, 8192, 3072], P('dp', 'seq', 'tower'), may hold values from -6 to 6
- audio_output_gradient: bfloat16 [2, 1024, 3072], P('dp', 'seq', 'tower'), may hold values from -6 to 6
- gains: float32 [4, 3072], P(None, 'tower'), may hold values from 0.1 to 1.9
- video_lengths: int32 [2], P('dp'), may hold values from 2048 to 8192, as said below
- audio_lengths: int32 [2], P('dp'), may hold values from 256 to 1024, as said below
Outputs:
- video_output: bfloat16 [2, 8192, 3072], P('dp', 'seq', 'tower')
- audio_cross_output: bfloat16 [2, 1024, 3072], P('dp', 'seq', 'tower')
- video_query_grad: bfloat16 [2, 8192, 3072], P('dp', 'seq', 'tower')
- audio_key_grad: bfloat16 [2, 1024, 3072], P('dp', 'seq', 'tower')
- audio_value_grad: bfloat16 [2, 1024, 3072], P('dp', 'seq', 'tower')
- audio_query_grad: bfloat16 [2, 1024, 3072], P('dp', 'seq', 'tower')
- video_key_grad: bfloat16 [2, 8192, 3072], P('dp', 'seq', 'tower')
- video_value_grad: bfloat16 [2, 8192, 3072], P('dp', 'seq', 'tower')
- gain_grads: float32 [4, 3072], P(None, 'tower')
The draws below stay inside these ranges and needn't reach their ends.
Inputs may be any that keep to these rules, and one draw needn't show every extreme that they name: `video_lengths`: some clip has all 8192 video tokens live. `audio_lengths`: some clip has all 1024 audio tokens live.
All inputs are finite; a program needn't handle non-finite values.
Results may differ from the reference program's by a relative error of at most 0.04.
Values may be sent and summed in bfloat16 or wider, within the bound.
A program may use at most 128 MiB of HBM per device.

```python
import math
import jax
import jax.numpy as jnp
from jax import lax

HEADS = 24
HD = 128
D = 3072
CLIPS = 2
VTOK = 8192
ATOK = 1024


def common_pattern(key):
    return jnp.where(jax.random.bernoulli(jax.random.fold_in(key, 7), 0.5, (CLIPS, HD)), 1.0, -1.0)


def drawn_field(key, rows):
    return jnp.clip(jax.random.normal(key, (CLIPS, rows, D), jnp.float32), -8.0, 8.0)


def plant_queries(field, sign_pattern):
    strengths = jnp.array([8.0, 6.0, 4.0, 3.0], jnp.float32)
    planted = strengths[None, :, None] * sign_pattern[:, None, :]
    field = field.at[:, 0:4, :].multiply(0.25)
    return field.at[:, 0:4, 0:HD].set(planted)


def plant_keys(field, sign_pattern):
    first_row = 8.0 * sign_pattern
    second_row = first_row.at[:, 0].set(0.0)
    field = field.at[:, 0:2, :].multiply(0.25)
    field = field.at[:, 0, 0:HD].set(first_row)
    return field.at[:, 1, 0:HD].set(second_row)


def draw_video_query(key, part):
    sign_pattern = common_pattern(key)
    key = jax.random.fold_in(key, 11)
    field = drawn_field(key, VTOK)
    return plant_queries(field, sign_pattern).astype(jnp.bfloat16)


def draw_audio_key(key, part):
    sign_pattern = common_pattern(key)
    key = jax.random.fold_in(key, 12)
    field = drawn_field(key, ATOK)
    return plant_keys(field, sign_pattern).astype(jnp.bfloat16)


def draw_audio_query(key, part):
    sign_pattern = common_pattern(key)
    key = jax.random.fold_in(key, 13)
    field = drawn_field(key, ATOK)
    return plant_queries(field, sign_pattern).astype(jnp.bfloat16)


def draw_video_key(key, part):
    sign_pattern = common_pattern(key)
    key = jax.random.fold_in(key, 14)
    field = drawn_field(key, VTOK)
    return plant_keys(field, sign_pattern).astype(jnp.bfloat16)


def draw_video_lengths(key, part):
    key = jax.random.fold_in(key, 31)
    former, latter = jax.random.split(key)
    lengths = jax.random.randint(former, (CLIPS,), VTOK // 4, VTOK)
    full_clip = jax.random.randint(latter, (), 0, CLIPS)
    return jnp.where(jnp.arange(CLIPS) == full_clip, VTOK, lengths).astype(jnp.int32)


def draw_audio_lengths(key, part):
    key = jax.random.fold_in(key, 32)
    former, latter = jax.random.split(key)
    lengths = jax.random.randint(former, (CLIPS,), ATOK // 4, ATOK)
    full_clip = jax.random.randint(latter, (), 0, CLIPS)
    return jnp.where(jnp.arange(CLIPS) == full_clip, ATOK, lengths).astype(jnp.int32)


def block_levels(key, shape, pieces, least, top_value):
    level, own = 1.0, jax.random.fold_in(key, 6)
    for axis_at, shards_of in pieces:
        steps = jnp.exp(jax.random.uniform(jax.random.fold_in(own, axis_at), (shards_of,), jnp.float32, least / len(pieces), top_value / len(pieces)))
        level = level * jnp.repeat(steps, shape[axis_at] // shards_of).reshape([-1 if axis == axis_at else 1 for axis in range(len(shape))])
    return level


def centred(rng, dims, width, bound, cuts=(), kind=jnp.bfloat16):
    level = block_levels(rng, dims, cuts, -0.22, 0.18) if cuts else 1.0
    drawn = jax.random.normal(rng, dims, jnp.float32) * width * level
    return jnp.minimum(jnp.maximum(drawn, -bound), bound).astype(kind)


def setup_inputs(seed: int = 0) -> dict:
    streams_of = jax.random.split(jax.random.key(seed), 12)
    return {
        "video_query": draw_video_query(jax.random.fold_in(streams_of[11], 71), 0),
        "audio_key": draw_audio_key(jax.random.fold_in(streams_of[11], 71), 0),
        "audio_value": centred(streams_of[2], (CLIPS, ATOK, D), 1.0, 6.0, ((0, 2), (1, 16), (2, 8))),
        "audio_query": draw_audio_query(jax.random.fold_in(streams_of[11], 71), 0),
        "video_key": draw_video_key(jax.random.fold_in(streams_of[11], 71), 0),
        "video_value_rows": centred(streams_of[5], (CLIPS, VTOK, D), 1.0, 6.0, ((0, 2), (1, 16), (2, 8))),
        "video_upstream": centred(streams_of[6], (CLIPS, VTOK, D), 1.0, 6.0, ((0, 2), (1, 16), (2, 8))),
        "audio_output_gradient": centred(streams_of[7], (CLIPS, ATOK, D), 1.0, 6.0, ((0, 2), (1, 16), (2, 8))),
        "gains": jnp.clip(1.0 + 0.18 * jax.random.normal(streams_of[8], (4, D), jnp.float32), 0.1, 1.9),
        "video_lengths": draw_video_lengths(jax.random.fold_in(streams_of[11], 71), 0),
        "audio_lengths": draw_audio_lengths(jax.random.fold_in(streams_of[11], 71), 0),
    }


epsilon = 1e-06
masked_score = -1e+30

def rms_factors(tensor):
    widened = tensor.astype(jnp.float32)
    return lax.rsqrt(lax.optimization_barrier(jnp.sum(widened * widened, axis=-1)) / D + epsilon)

def normalize(tensor, factors, gain):
    return (tensor.astype(jnp.float32) * factors[:, None] * gain).astype(jnp.bfloat16)

def divide_heads(tensor):
    return jnp.transpose(tensor.reshape(tensor.shape[0], HEADS, HD), (1, 0, 2))

def merge_heads(tensor):
    return jnp.transpose(tensor, (1, 0, 2)).reshape(tensor.shape[1], HEADS * HD)

def attend_across(queries, keys_in, values_in, upstream, alive):
    score_scale = 1.0 / math.sqrt(HD)

    def per_head(head_items):
        head_query, head_key, head_value, head_grad = head_items
        scores = jnp.dot(head_query, head_key.T, preferred_element_type=jnp.float32) * score_scale
        scores = jnp.where(alive[None, :], scores, masked_score)
        largest = lax.optimization_barrier(jnp.max(scores, axis=-1, keepdims=True))
        summed = lax.optimization_barrier(jnp.sum(jnp.where(alive[None, :], jnp.exp(scores - largest), 0.0), axis=-1, keepdims=True))
        weights = jnp.where(alive[None, :], jnp.exp(scores - (largest + jnp.log(summed))), 0.0)
        weights_low = weights.astype(jnp.bfloat16)
        output = jnp.dot(weights_low, head_value, preferred_element_type=jnp.float32).astype(jnp.bfloat16)
        row_delta = lax.optimization_barrier(jnp.sum(head_grad.astype(jnp.float32) * output.astype(jnp.float32), axis=-1, keepdims=True))
        dweights = jnp.dot(head_grad, head_value.T, preferred_element_type=jnp.float32)
        dscores = (weights * (dweights - row_delta) * score_scale).astype(jnp.bfloat16)
        return (output, jnp.dot(dscores, head_key, preferred_element_type=jnp.float32), jnp.dot(dscores.T, head_query, preferred_element_type=jnp.float32), jnp.dot(weights_low.T, head_grad, preferred_element_type=jnp.float32))
    results = lax.map(per_head, (divide_heads(queries), divide_heads(keys_in), divide_heads(values_in), divide_heads(upstream)))
    return tuple((merge_heads(result) for result in results))

def norm_back(tensor, factors, gain, upstream):
    widened = tensor.astype(jnp.float32)
    column = factors[:, None]
    inner_sum = lax.optimization_barrier(jnp.sum(widened * gain * upstream, axis=-1, keepdims=True))
    gradient = column * gain * upstream - widened * (column * column * column) * inner_sum / D
    return (gradient.astype(jnp.bfloat16), lax.optimization_barrier(jnp.sum(upstream * widened * column, axis=0)))

def reference(video_query, audio_key, audio_value, audio_query, video_key, video_value_rows, video_upstream, audio_output_gradient, gains, video_lengths, audio_lengths):
    raw_inputs = (video_query, audio_key, audio_query, video_key)
    per_clip = []
    gain_total = jnp.zeros((4, HEADS * HD), jnp.float32)
    for sample_index in range(CLIPS):
        rows_in = [tensor[sample_index] for tensor in raw_inputs]
        factors = [rms_factors(tensor) for tensor in rows_in]
        rms_normalized = [normalize(rows_in[number], factors[number], gains[number]) for number in range(4)]
        audio_alive = jnp.arange(ATOK, dtype=jnp.int32) < audio_lengths[sample_index]
        video_valid_mask = jnp.arange(VTOK, dtype=jnp.int32) < video_lengths[sample_index]
        video_output, video_query_gradient, audio_key_gradient, grad_avalue = attend_across(rms_normalized[0], rms_normalized[1], audio_value[sample_index], video_upstream[sample_index], audio_alive)
        audio_cross_output, audio_query_gradient, video_key_gradient, video_value_gradient = attend_across(rms_normalized[2], rms_normalized[3], video_value_rows[sample_index], audio_output_gradient[sample_index], video_valid_mask)
        incoming_gradients = (video_query_gradient, audio_key_gradient, audio_query_gradient, video_key_gradient)
        input_grads = []
        for number in range(4):
            gradient, gain_term = norm_back(rows_in[number], factors[number], gains[number], incoming_gradients[number])
            input_grads.append(gradient)
            gain_total = gain_total.at[number].add(gain_term)
        per_clip.append((video_output, audio_cross_output, input_grads[0], input_grads[1], grad_avalue.astype(jnp.bfloat16), input_grads[2], input_grads[3], video_value_gradient.astype(jnp.bfloat16)))
    stacked = [jnp.stack([entry[number] for entry in per_clip]) for number in range(8)]
    return (stacked[0], stacked[1], stacked[2], stacked[3], stacked[4], stacked[5], stacked[6], stacked[7], gain_total)
```

```python
import functools
import math

import jax
import jax.numpy as jnp
from jax import lax
from jax.experimental import pallas as pl
from jax.experimental.pallas import tpu as pltpu
from jax.sharding import PartitionSpec as P

HD = 128
EPS = 1e-06
MASKED = -1e30
FLOOR = -1e29
F32 = jnp.float32
BF16 = jnp.bfloat16

NT = (((1,), (1,)), ((), ()))
NN = (((1,), (0,)), ((), ()))
TN = (((0,), (0,)), ((), ()))


def mm(a, b, dims):
    return lax.dot_general(a, b, dims, preferred_element_type=F32)


def aligned(start, size, unit):
    return pl.ds(pl.multiple_of(start, unit), size)


def lanes_of(products):
    part = products[:, 0:HD]
    for k in range(1, products.shape[1] // HD):
        part = part + products[:, k * HD : (k + 1) * HD]
    return jnp.sum(part.T, axis=0, keepdims=True)


def column_of(row):
    return jnp.broadcast_to(row, (HD, HD)).T


def kernel(
    sizes,
    vq_h, ak_h, av_h, aq_h, vk_h, vv_h, up_h, ao_h, gains, vlen, alen,
    vo_h, aco_h, vqg_h, akg_h, avg_h, aqg_h, vkg_h, vvg_h, gg,
    g, raw_v, raw_a, qn, kn, dvid, vout, vvg, part, rr, rl, xs, xr, fin,
    dka, dva, pb, dpb, mloc, bias_a, bias_v, rbv, rba, small, ssum, sloc, sin, sres, sall,
    gbuf, dbuf, outa,
    ld, gs, gr, ts, tr, s1s, s1r, s2s, s2r, ggs, ggr, ds_, dr_, rs_s, rs_r, ost,
):
    n_tower, n_seq, n_dp = sizes
    n_z = n_seq // 2
    nr = n_z // 2
    nl = n_z - 1 - nr
    heads = 3
    width = heads * HD
    vrows = 512
    arows = n_seq * 64
    depth = n_tower * width
    scale = 1.0 / math.sqrt(HD)
    c = scale * math.log2(math.e)

    t_at = lax.axis_index("tower")
    s_at = lax.axis_index("seq")
    d_at = lax.axis_index("dp")
    z = lax.rem(s_at, n_z)
    x = s_at // n_z

    def seq_id(xx, zz):
        return xx * n_z + zz

    right = seq_id(x, lax.rem(z + 1, n_z))
    left = seq_id(x, lax.rem(z + n_z - 1, n_z))
    over = seq_id(1 - x, z)

    def remote(src, dst, send, recv, **dev):
        return pltpu.make_async_remote_copy(
            src_ref=src, dst_ref=dst, send_sem=send, recv_sem=recv,
            device_id=dev, device_id_type=pl.DeviceIdType.MESH,
        )

    pending = []

    loads = {}
    for n, (src, dst) in enumerate([
        (ao_h, g.at[0, aligned(z * 128 + x * 64, 64, 64)]),
        (av_h, g.at[1, aligned(z * 128 + x * 64, 64, 64)]),
        (aq_h, raw_a.at[0]),
        (ak_h, raw_a.at[1]),
        (vq_h, raw_v.at[0]),
        (vk_h, raw_v.at[1]),
        (vv_h, raw_v.at[2]),
        (up_h, raw_v.at[3]),
    ]):
        loads[n] = pltpu.make_async_copy(src, dst, ld.at[n])
        loads[n].start()

    barrier = pltpu.get_barrier_semaphore()
    peers = 0
    for k in range(1, n_seq):
        pl.semaphore_signal(barrier, inc=1, device_id={"seq": lax.rem(s_at + k, n_seq)}, device_id_type=pl.DeviceIdType.MESH)
        peers += 1
    for k in range(1, n_tower):
        pl.semaphore_signal(barrier, inc=1, device_id={"tower": lax.rem(t_at + k, n_tower)}, device_id_type=pl.DeviceIdType.MESH)
        peers += 1
    if n_dp > 1:
        pl.semaphore_signal(barrier, inc=1, device_id={"dp": 1 - d_at}, device_id_type=pl.DeviceIdType.MESH)
        peers += 1
    pl.semaphore_wait(barrier, peers)

    own = aligned(z * 128 + x * 64, 64, 64)

    def pair(zz):
        return aligned(lax.rem(zz + 2 * n_z, n_z) * 128, 128, 128)

    def gather_x(a):
        copy = remote(g.at[a, own], g.at[a, own], gs.at[a, 0], gr.at[a, 0], seq=over)
        copy.start()
        pending.append(copy)
        return copy

    chains = {}

    def gather_step(a, k):
        mirrored = a % 2 == 1
        long_to, short_to = (left, right) if mirrored else (right, left)
        sign = 1 if mirrored else -1
        if k < nr:
            if k > 0:
                chains[a, "l", k - 1].wait_recv()
            block = g.at[a, pair(z + sign * k)]
            copy = remote(block, block, gs.at[a, 1 + k], gr.at[a, 1 + k], seq=long_to)
            copy.start()
            pending.append(copy)
            chains[a, "l", k] = copy
        if k < nl:
            if k > 0:
                chains[a, "s", k - 1].wait_recv()
            block = g.at[a, pair(z - sign * k)]
            copy = remote(block, block, gs.at[a, 1 + nr + k], gr.at[a, 1 + nr + k], seq=short_to)
            copy.start()
            pending.append(copy)
            chains[a, "s", k] = copy

    def gather_end(a):
        chains[a, "l", nr - 1].wait_recv()
        if nl > 0:
            chains[a, "s", nl - 1].wait_recv()

    loads[0].wait()
    loads[1].wait()
    xc = {0: gather_x(0), 1: gather_x(1)}

    def tower_start(n):
        copies = []
        for k in range(1, n_tower):
            copy = remote(
                small.at[n, t_at], small.at[n, t_at], ts.at[n, k], tr.at[n, k],
                tower=lax.rem(t_at + k, n_tower),
            )
            copy.start()
            pending.append(copy)
            copies.append(copy)
        return copies

    def tower_sum(n, copies):
        for copy in copies:
            copy.wait_recv()
        total = small[n, 0]
        for k in range(1, n_tower):
            total = total + small[n, k]
        return total

    def put_video(n, which, row):
        for k in range(4):
            small[n, t_at, which * 4 + k : which * 4 + k + 1, :] = row[:, k * HD : (k + 1) * HD]

    loads[2].wait()
    loads[3].wait()
    small[0, t_at] = jnp.zeros((16, HD), F32)
    small[1, t_at] = jnp.zeros((16, HD), F32)
    small[2, t_at] = jnp.zeros((16, HD), F32)
    both = jnp.concatenate([raw_a[0].astype(F32), raw_a[1].astype(F32)], axis=0)
    small[0, t_at, 8:9, :] = lanes_of(both * both)
    for n in range(2):
        loads[4 + n].wait()
        wide = raw_v[n].astype(F32)
        put_video(0, n, lanes_of(wide * wide))
    exch = tower_start(0)

    for a in (0, 1):
        xc[a].wait_recv()
        gather_step(a, 0)

    rho = lax.broadcasted_iota(jnp.int32, (arows, HD), 0)
    token = ((rho // 64) % 2) * (n_z * 64) + (rho // 128) * 64 + rho % 64
    bias_a[...] = jnp.where(token < alen[0], 0.0, MASKED)
    vtok = s_at * vrows + lax.broadcasted_iota(jnp.int32, (vrows, HD), 0)
    bias_v[...] = jnp.where(vtok < vlen[0], 0.0, MASKED)

    factors = lax.rsqrt(tower_sum(0, exch) / depth + EPS)
    rba[...] = column_of(factors[8:9, :])
    for n in range(2):
        for h in range(heads):
            cols = slice(h * HD, (h + 1) * HD)
            normed = raw_a[n, :, cols].astype(F32) * rba[n * 64 : n * 64 + 64, :] * gains[2 - n : 3 - n, cols]
            g[2 + n, own, cols] = normed.astype(BF16)
        xc[2 + n] = gather_x(2 + n)
    for n in range(2):
        for k in range(4):
            rows = slice(k * HD, (k + 1) * HD)
            col = column_of(factors[n * 4 + k : n * 4 + k + 1, :])
            rbv[n, rows, :] = col
            for h in range(heads):
                cols = slice(h * HD, (h + 1) * HD)
                normed = raw_v[n, rows, cols].astype(F32) * col * gains[3 * n : 3 * n + 1, cols]
                (qn, kn)[n][rows, cols] = normed.astype(BF16)
    loads[6].wait()
    loads[7].wait()

    for k in range(1, nr):
        for a in (0, 1):
            gather_step(a, k)
        if k == 1:
            for a in (2, 3):
                xc[a].wait_recv()
                gather_step(a, 0)
    if nr == 1:
        for a in (2, 3):
            xc[a].wait_recv()
            gather_step(a, 0)
    for a in (0, 1):
        gather_end(a)
    for k in range(1, nr):
        for a in (2, 3):
            gather_step(a, k)
    for a in (2, 3):
        gather_end(a)

    tile = 256
    tiles = arows // tile
    twice = lambda b: jnp.concatenate([b, b], axis=1)

    def first(i, carry):
        h = i // tiles
        t = lax.rem(i, tiles)
        cols = aligned(h * HD, HD, HD)
        rows = aligned(t * tile, tile, tile)
        s = mm(kn[:, cols], g[2, rows, cols], NT) + twice(bias_v[...])
        m = jnp.maximum(jnp.max(s, axis=0, keepdims=True), FLOOR)
        p = jnp.exp2((s - m) * c)
        dp = mm(raw_v[2, :, cols], g[0, rows, cols], NT)
        total = jnp.sum(p, axis=0, keepdims=True)
        inner = jnp.sum(p * dp, axis=0, keepdims=True)
        pb[h, :, rows] = p.astype(BF16)
        dpb[h, :, rows] = dp
        for k in range(2):
            lanes = slice(k * HD, (k + 1) * HD)
            sloc[t * 2 + k, pl.ds(h, 1), :] = m[:, lanes]
            sloc[t * 2 + k, pl.ds(3 + h, 1), :] = total[:, lanes]
            sloc[t * 2 + k, pl.ds(6 + h, 1), :] = inner[:, lanes]
        return carry

    sloc[...] = jnp.zeros_like(sloc)
    lax.fori_loop(0, heads * tiles, first, 0)

    stat1 = []
    for k in range(1, n_seq):
        to = lax.rem(s_at + k, n_seq)
        copy = remote(sloc.at[lax.rem(to, n_z)], sin.at[s_at], s1s.at[k], s1r.at[k], seq=to)
        copy.start()
        pending.append(copy)
        stat1.append(copy)
    sin[s_at] = sloc[z]

    vtile = 256

    def video_head(h):
        cols = slice(h * HD, (h + 1) * HD)

        def one(t, carry):
            rows = aligned(t * vtile, vtile, vtile)
            q_t = qn[rows, cols]
            u_t = raw_v[3, rows, cols]
            s = mm(g[3, :, cols], q_t, NT) + twice(bias_a[...])
            m = jnp.max(s, axis=0, keepdims=True)
            p = jnp.exp2((s - m) * c)
            w = p * (1.0 / jnp.sum(p, axis=0, keepdims=True))
            low = w.astype(BF16)
            out = mm(g[1, :, cols], low, TN).T.astype(BF16)
            vout[rows, cols] = out
            delta = lanes_of(out.astype(F32) * u_t.astype(F32))
            dp = mm(g[1, :, cols], u_t, NT)
            ds = (w * (dp - delta)).astype(BF16)
            dvid[0, rows, cols] = mm(g[3, :, cols], ds, TN).T * scale
            dka[...] += mm(ds, q_t, NN) * scale
            dva[...] += mm(low, u_t, NN)
            return carry

        dka[...] = jnp.zeros_like(dka)
        dva[...] = jnp.zeros_like(dva)
        lax.fori_loop(0, vrows // vtile, one, 0)
        grad = dka[...]
        gbuf[s_at, 1:2, cols] = jnp.sum(grad * g[3, :, cols].astype(F32), axis=0, keepdims=True) / gains[1:2, cols]
        part[0, :, cols] = grad.astype(BF16)
        part[0, :, width + h * HD : width + (h + 1) * HD] = dva[...].astype(BF16)

    video_head(0)

    for copy in stat1:
        copy.wait_recv()
    mx = sin[0, 0:3, :]
    for k in range(1, n_seq):
        mx = jnp.maximum(mx, sin[k, 0:3, :])
    tot = jnp.zeros((3, HD), F32)
    inn = jnp.zeros((3, HD), F32)
    for k in range(n_seq):
        f = jnp.exp2((sin[k, 0:3, :] - mx) * c)
        tot = tot + sin[k, 3:6, :] * f
        inn = inn + sin[k, 6:9, :] * f
    sres[...] = jnp.zeros_like(sres)
    sres[0:3, :] = mx * c + jnp.log2(tot)
    sres[3:6, :] = inn / tot
    stat2 = []
    for k in range(1, n_z):
        copy = remote(sres, sall.at[z], s2s.at[k], s2r.at[k], seq=seq_id(x, lax.rem(z + k, n_z)))
        copy.start()
        pending.append(copy)
        stat2.append(copy)
    sall[z] = sres[...]

    for h in range(1, heads):
        video_head(h)

    rchain = {}

    def rs_step(b, k):
        for name, n, to, sign, base, land in (("r", nr, right, 1, 0, rr), ("l", nl, left, -1, nr, rl)):
            if k < n:
                block = pair(z + sign * (n - k))
                if k > 0:
                    rchain[b, name, k - 1].wait_recv()
                    part[b, block, :] = (part[b, block, :].astype(F32) + land[b, k - 1].astype(F32)).astype(BF16)
                copy = remote(part.at[b, block], land.at[b, k], rs_s.at[b, base + k], rs_r.at[b, base + k], seq=to)
                copy.start()
                pending.append(copy)
                rchain[b, name, k] = copy

    def rs_cross(b):
        total = part[b, pair(z), :].astype(F32)
        rchain[b, "r", nr - 1].wait_recv()
        total = total + rr[b, nr - 1].astype(F32)
        if nl > 0:
            rchain[b, "l", nl - 1].wait_recv()
            total = total + rl[b, nl - 1].astype(F32)
        fin[b] = total
        xs[b] = fin[b, aligned((1 - x) * 64, 64, 64), :].astype(BF16)
        copy = remote(xs.at[b], xr.at[b], rs_s.at[b, nr + nl], rs_r.at[b, nr + nl], seq=over)
        copy.start()
        pending.append(copy)
        return copy

    def rs_end(b, copy):
        copy.wait_recv()
        return fin[b, aligned(x * 64, 64, 64), :] + xr[b].astype(F32)

    rs_step(0, 0)

    for copy in stat2:
        copy.wait_recv()

    def second_head(h):
        cols = slice(h * HD, (h + 1) * HD)

        def one(t, carry):
            rows = aligned(t * tile, tile, tile)

            def stat(ref, at):
                return jnp.concatenate([ref[t * 2, at : at + 1, :], ref[t * 2 + 1, at : at + 1, :]], axis=1)

            coef = jnp.exp2(stat(sloc, h) * c - stat(sall, h))
            delta = stat(sall, 3 + h)
            w = pb[h, :, rows].astype(F32) * coef
            low = w.astype(BF16)
            out = mm(raw_v[2, :, cols], low, TN).T
            part[1, rows, cols] = out.astype(BF16)
            ds = (w * (dpb[h, :, rows] - delta)).astype(BF16)
            dq = mm(kn[:, cols], ds, TN).T * scale
            q_t = g[2, rows, cols]
            gbuf[s_at, 2:3, cols] += jnp.sum(dq * q_t.astype(F32), axis=0, keepdims=True) / gains[2:3, cols]
            part[1, rows, width + h * HD : width + (h + 1) * HD] = dq.astype(BF16)
            dvid[1, :, cols] += mm(ds, q_t, NN) * scale
            dva[0:vrows, :] += mm(low, g[0, rows, cols], NN)
            return carry

        gbuf[s_at, 2:3, cols] = jnp.zeros((1, HD), F32)
        dvid[1, :, cols] = jnp.zeros((vrows, HD), F32)
        dva[0:vrows, :] = jnp.zeros((vrows, HD), F32)
        lax.fori_loop(0, tiles, one, 0)
        vvg[:, cols] = dva[0:vrows, :].astype(BF16)

    for h in range(heads):
        second_head(h)
        rs_step(0, 1 + h)
    rs_step(1, 0)

    for n, row in ((0, 0), (1, 3)):
        inner = dvid[n] * (qn, kn)[n][...].astype(F32)
        put_video(1, n, lanes_of(inner))
        gbuf[s_at, row : row + 1, :] = jnp.sum(inner, axis=0, keepdims=True) / gains[row : row + 1, :]
    exch = tower_start(1)
    gcopies = []
    for k in range(1, n_seq):
        copy = remote(gbuf.at[s_at], gbuf.at[s_at], ggs.at[k], ggr.at[k], seq=lax.rem(s_at + k, n_seq))
        copy.start()
        pending.append(copy)
        gcopies.append(copy)
    rs_step(1, 1)
    cross0 = rs_cross(0)
    outs = [
        pltpu.make_async_copy(vout, vo_h, ost.at[0]),
        pltpu.make_async_copy(vvg, vvg_h, ost.at[1]),
    ]
    for copy in outs:
        copy.start()

    inner = tower_sum(1, exch) * (1.0 / depth)
    for n in range(2):
        row = 3 * n
        for k in range(4):
            rows = slice(k * HD, (k + 1) * HD)
            col = column_of(inner[n * 4 + k : n * 4 + k + 1, :])
            r = rbv[n, rows, :]
            for h in range(heads):
                cols = slice(h * HD, (h + 1) * HD)
                grad = r * gains[row : row + 1, cols] * dvid[n, rows, cols] - raw_v[n, rows, cols].astype(F32) * (r * r * col)
                (qn, kn)[n][rows, cols] = grad.astype(BF16)
        copy = pltpu.make_async_copy((qn, kn)[n], (vqg_h, vkg_h)[n], ost.at[2 + n])
        copy.start()
        outs.append(copy)
    rs_step(1, 2)

    for copy in gcopies:
        copy.wait_recv()
    total = gbuf[0, 0:4, :]
    for k in range(1, n_seq):
        total = total + gbuf[k, 0:4, :]
    if n_dp > 1:
        dbuf[d_at, 0:4, :] = total
        copy = remote(dbuf.at[d_at], dbuf.at[d_at], ds_.at[0], dr_.at[0], dp=1 - d_at)
        copy.start()
        pending.append(copy)

    key_side = rs_end(0, cross0)
    rs_step(1, 3)
    outa[3] = key_side[:, width:].astype(BF16)
    if n_dp > 1:
        copy.wait_recv()
        gg[...] = dbuf[0, 0:4, :] + dbuf[1, 0:4, :]
    else:
        gg[...] = total
    cross1 = rs_cross(1)
    query_side = rs_end(1, cross1)
    outa[0] = query_side[:, 0:width].astype(BF16)
    sides = (query_side[:, width:], key_side[:, 0:width])
    inner = jnp.concatenate([sides[n] * g[2 + n, own, :].astype(F32) for n in range(2)], axis=0)
    small[2, t_at, 0:1, :] = lanes_of(inner)
    exch = tower_start(2)
    col = column_of(tower_sum(2, exch)[0:1, :] * (1.0 / depth))
    for n in range(2):
        half = slice(n * 64, n * 64 + 64)
        r = rba[half, :]
        for h in range(heads):
            cols = slice(h * HD, (h + 1) * HD)
            grad = r * gains[2 - n : 3 - n, cols] * sides[n][:, cols] - raw_a[n, :, cols].astype(F32) * (r * r * col[half, :])
            outa[1 + n, :, cols] = grad.astype(BF16)
    for n, dst in enumerate((aco_h, aqg_h, akg_h, avg_h)):
        copy = pltpu.make_async_copy(outa.at[n], dst, ost.at[4 + n])
        copy.start()
        outs.append(copy)
    for copy in outs:
        copy.wait()
    for copy in pending:
        copy.wait_send()


def solution(mesh):
    sizes = tuple(mesh.shape[name] for name in ("tower", "seq", "dp"))
    n_tower, n_seq, n_dp = sizes
    n_z = n_seq // 2
    arows = n_seq * 64
    hops = n_z - 1
    nr = n_z // 2
    nl = max(hops - nr, 1)
    width = 384
    any_spec = pl.BlockSpec(memory_space=pl.ANY)
    vmem = pl.BlockSpec(memory_space=pltpu.VMEM)
    smem = pl.BlockSpec(memory_space=pltpu.SMEM)
    dma = lambda *shape: pltpu.SemaphoreType.DMA(shape)

    def body(vq, ak, av, aq, vk, vv, up, ao, gains, vlen, alen):
        video = jax.ShapeDtypeStruct((512, width), BF16)
        audio = jax.ShapeDtypeStruct((64, width), BF16)
        results = pl.pallas_call(
            functools.partial(kernel, sizes),
            out_shape=(video, audio, video, audio, audio, audio, video, video, jax.ShapeDtypeStruct((4, width), F32)),
            in_specs=[any_spec] * 8 + [vmem, smem, smem],
            out_specs=tuple([any_spec] * 8 + [vmem]),
            scratch_shapes=[
                pltpu.VMEM((4, arows, width), BF16),
                pltpu.VMEM((4, 512, width), BF16),
                pltpu.VMEM((2, 64, width), BF16),
                pltpu.VMEM((512, width), BF16),
                pltpu.VMEM((512, width), BF16),
                pltpu.VMEM((2, 512, width), F32),
                pltpu.VMEM((512, width), BF16),
                pltpu.VMEM((512, width), BF16),
                pltpu.VMEM((2, arows, 2 * width), BF16),
                pltpu.VMEM((2, nr, 128, 2 * width), BF16),
                pltpu.VMEM((2, nl, 128, 2 * width), BF16),
                pltpu.VMEM((2, 64, 2 * width), BF16),
                pltpu.VMEM((2, 64, 2 * width), BF16),
                pltpu.VMEM((2, 128, 2 * width), F32),
                pltpu.VMEM((max(arows, 512), HD), F32),
                pltpu.VMEM((max(arows, 512), HD), F32),
                pltpu.VMEM((3, 512, arows), BF16),
                pltpu.VMEM((3, 512, arows), F32),
                pltpu.VMEM((8, HD), F32),
                pltpu.VMEM((arows, HD), F32),
                pltpu.VMEM((512, HD), F32),
                pltpu.VMEM((2, 512, HD), F32),
                pltpu.VMEM((128, HD), F32),
                pltpu.VMEM((3, n_tower, 16, HD), F32),
                pltpu.VMEM((16, HD), F32),
                pltpu.VMEM((n_z, 16, HD), F32),
                pltpu.VMEM((n_seq, 16, HD), F32),
                pltpu.VMEM((8, HD), F32),
                pltpu.VMEM((n_z, 8, HD), F32),
                pltpu.VMEM((n_seq, 8, width), F32),
                pltpu.VMEM((2, 8, width), F32),
                pltpu.VMEM((4, 64, width), BF16),
                dma(8), dma(4, hops + 1), dma(4, hops + 1), dma(3, n_tower), dma(3, n_tower),
                dma(n_seq), dma(n_seq), dma(n_z), dma(n_z), dma(n_seq), dma(n_seq), dma(1), dma(1),
                dma(2, hops + 1), dma(2, hops + 1), dma(8),
            ],
            compiler_params=pltpu.CompilerParams(
                collective_id=0, has_side_effects=True, vmem_limit_bytes=56 * 1024 * 1024
            ),
            cost_estimate=pl.CostEstimate(flops=4_800_000_000, bytes_accessed=4_000_000, transcendentals=3_200_000),
        )(vq[0], ak[0], av[0], aq[0], vk[0], vv[0], up[0], ao[0], gains, vlen, alen)
        return tuple(r[None] for r in results[:8]) + (results[8],)

    spec = P("dp", "seq", "tower")
    return jax.shard_map(
        body,
        mesh=mesh,
        in_specs=(spec,) * 8 + (P(None, "tower"), P("dp"), P("dp")),
        out_specs=(spec,) * 8 + (P(None, "tower"),),
        check_vma=False,
    )
```

```python
import functools
import math

import jax
import jax.numpy as jnp
from jax import lax
from jax.experimental import pallas as pl
from jax.experimental.pallas import tpu as pltpu
from jax.sharding import PartitionSpec as P

HD = 128
HEADS = 3
WIDTH = HEADS * HD
VROWS = 512
EPS = 1e-06
MASKED = -1e30
FLOOR = -1e29
F32 = jnp.float32
BF16 = jnp.bfloat16
MESH = pl.DeviceIdType.MESH

NT = (((1,), (1,)), ((), ()))
NN = (((1,), (0,)), ((), ()))
TN = (((0,), (0,)), ((), ()))


def mm(a, b, dims):
    return lax.dot_general(a, b, dims, preferred_element_type=F32)


def aligned(start, size, unit):
    return pl.ds(pl.multiple_of(start, unit), size)


def lanes_of(products):
    part = products[:, 0:HD]
    for k in range(1, products.shape[1] // HD):
        part = part + products[:, k * HD : (k + 1) * HD]
    return jnp.sum(part.T, axis=0, keepdims=True)


def column_of(row):
    return jnp.broadcast_to(row, (HD, HD)).T


def head_cols(h):
    return slice(h * HD, (h + 1) * HD)


def wide(block, n):
    return jnp.concatenate([block] * n, axis=1)


def kernel(
    sizes,
    vq_h, ak_h, av_h, aq_h, vk_h, vv_h, up_h, ao_h, gains, vlen, alen,
    vo_h, aco_h, vqg_h, akg_h, avg_h, aqg_h, vkg_h, vvg_h, gg_h,
    g, raw_v, raw_a, qn, kn, dvid, vout, vvg, part, rr, rl, xin, xs, xr, fin,
    pa, dpa, dsa, ast, acf, pb, dpb, dsb, acc, bias_a, bias_v, rbv, rba, small,
    sloc, sin, sres, sall, ub, uin, ucol, gbuf, dbuf, gout, outa,
    ld, gs, gr, gxs, gxr, ts, tr, s1s, s1r, s2s, s2r, us, ur, ggs, ggr, ds_, dr_,
    rs_s, rs_r, xi_s, xi_r, ost,
):
    n_tower, n_seq, n_dp = sizes
    n_z = n_seq // 2
    nr = n_z // 2
    nl = n_z - 1 - nr
    arows = n_seq * 64
    depth = n_tower * WIDTH
    scale = 1.0 / math.sqrt(HD)
    c = scale * math.log2(math.e)
    unscale = scale / c

    t_at = lax.axis_index("tower")
    s_at = lax.axis_index("seq")
    d_at = lax.axis_index("dp")
    z = lax.rem(s_at, n_z)
    x = s_at // n_z

    def ring(zz):
        return lax.rem(zz + 2 * n_z, n_z)

    def seq_id(xx, zz):
        return xx * n_z + ring(zz)

    right, left, over = seq_id(x, z + 1), seq_id(x, z - 1), seq_id(1 - x, z)

    pending = []

    def send(src, dst, send_sem, recv_sem, **dev):
        copy = pltpu.make_async_remote_copy(
            src_ref=src, dst_ref=dst, send_sem=send_sem, recv_sem=recv_sem,
            device_id=dev, device_id_type=MESH,
        )
        copy.start()
        pending.append(copy)
        return copy

    own = aligned(z * 128 + x * 64, 64, 64)
    loads = []
    for n, (src, dst) in enumerate([
        (aq_h, raw_a.at[0]),
        (ak_h, raw_a.at[1]),
        (ao_h, g.at[0, own]),
        (av_h, g.at[1, own]),
        (vq_h, raw_v.at[0]),
        (vk_h, raw_v.at[1]),
        (vv_h, raw_v.at[2]),
        (up_h, raw_v.at[3]),
    ]):
        loads.append(pltpu.make_async_copy(src, dst, ld.at[n]))
        loads[n].start()
    barrier = pltpu.get_barrier_semaphore()
    peers = 0
    for k in range(1, n_seq):
        pl.semaphore_signal(barrier, inc=1, device_id={"seq": lax.rem(s_at + k, n_seq)}, device_id_type=MESH)
        peers += 1
    for k in range(1, n_tower):
        pl.semaphore_signal(barrier, inc=1, device_id={"tower": lax.rem(t_at + k, n_tower)}, device_id_type=MESH)
        peers += 1
    if n_dp > 1:
        pl.semaphore_signal(barrier, inc=1, device_id={"dp": 1 - d_at}, device_id_type=MESH)
        peers += 1

    def put_video(n, which, row):
        for k in range(4):
            small[n, t_at, which * 4 + k : which * 4 + k + 1, :] = row[:, k * HD : (k + 1) * HD]

    for n in range(3):
        small[n, t_at] = jnp.zeros((16, HD), F32)
    sloc[...] = jnp.zeros_like(sloc)
    sres[...] = jnp.zeros_like(sres)
    ub[...] = jnp.zeros_like(ub)
    gbuf[s_at] = jnp.zeros((8, WIDTH), F32)
    loads[0].wait()
    loads[1].wait()
    both = jnp.concatenate([raw_a[0].astype(F32), raw_a[1].astype(F32)], axis=0)
    small[0, t_at, 8:9, :] = lanes_of(both * both)
    rho = lax.broadcasted_iota(jnp.int32, (arows, HD), 0)
    token = ((rho // 64) % 2) * (n_z * 64) + (rho // 128) * 64 + rho % 64
    bias_a[...] = jnp.where(token < alen[0], 0.0, MASKED)
    vtok = s_at * VROWS + lax.broadcasted_iota(jnp.int32, (VROWS, HD), 0)
    bias_v[...] = jnp.where(vtok < vlen[0], 0.0, MASKED)
    for n in range(2):
        loads[4 + n].wait()
        widened = raw_v[n].astype(F32)
        put_video(0, n, lanes_of(widened * widened))
    for n in (2, 3, 6, 7):
        loads[n].wait()
    pl.semaphore_wait(barrier, peers)

    def tower_start(n):
        return [
            send(small.at[n, t_at], small.at[n, t_at], ts.at[n, k], tr.at[n, k], tower=lax.rem(t_at + k, n_tower))
            for k in range(1, n_tower)
        ]

    def tower_sum(n, copies):
        for copy in copies:
            copy.wait_recv()
        total = small[n, 0]
        for k in range(1, n_tower):
            total = total + small[n, k]
        return total

    chains = {}

    def gather_step(a, k):
        last_over = a % 2 == 0
        sign = 1 if a >= 2 else -1
        ways = (("l", nr, left if a >= 2 else right, sign, 0), ("s", nl, right if a >= 2 else left, -sign, nr))

        def block(zz):
            if last_over:
                return g.at[a, aligned(ring(zz) * 128 + x * 64, 64, 64)]
            return g.at[a, aligned(ring(zz) * 128, 128, 128)]

        if k == 0 and last_over:
            chains[a, "x", 0] = send(block(z), block(z), gxs.at[a // 2, 0], gxr.at[a // 2, 0], seq=over)
        for name, n, to, way, base in ways:
            if k > n:
                continue
            here = block(z + way * k)
            if k > 0:
                chains[a, name, k].wait_recv()
            if k < n:
                chains[a, name, k + 1] = send(here, here, gs.at[a, 1 + base + k], gr.at[a, 1 + base + k], seq=to)
            if k > 0 and last_over:
                chains[a, "x", base + k] = send(here, here, gxs.at[a // 2, base + k], gxr.at[a // 2, base + k], seq=over)

    def gather_over(a):
        chains[a, "x", 0] = send(g.at[a, own], g.at[a, own], gs.at[a, 0], gr.at[a, 0], seq=over)

    def over_wait(a, delta):
        towards = delta if a >= 2 else -delta
        if delta == 0:
            at = 0
        elif abs(delta) == nr or towards > 0:
            at = abs(delta)
        else:
            at = nr + abs(delta)
        chains[a, "x", at].wait_recv()

    exch = tower_start(0)
    gather_over(1)
    gather_step(0, 0)

    stat1 = []

    def audio_first(delta):
        at = ring(z + delta)
        rows = aligned(at * 128, 128, 128)
        over_wait(0, delta)
        over_wait(2, delta)

        def one(h, carry):
            cols = aligned(h * HD, HD, HD)
            s = mm(kn[:, cols], g[2, rows, cols], NT) + bias_v[...]
            m = jnp.maximum(jnp.max(s, axis=0, keepdims=True), FLOOR)
            p = jnp.exp2(s - m)
            dp = mm(raw_v[2, :, cols], g[0, rows, cols], NT)
            pb[h, :, rows] = p.astype(BF16)
            dpb[h, :, rows] = dp
            sloc[at, pl.ds(h, 1), :] = m
            sloc[at, pl.ds(3 + h, 1), :] = jnp.sum(p, axis=0, keepdims=True)
            sloc[at, pl.ds(6 + h, 1), :] = jnp.sum(p * dp, axis=0, keepdims=True)
            return carry

        lax.fori_loop(0, HEADS, one, 0)
        slot = delta % n_z
        for k, xx in enumerate((x, 1 - x)):
            if delta == 0 and k == 0:
                sin[s_at] = sloc[at]
            else:
                stat1.append(
                    send(sloc.at[at], sin.at[s_at], s1s.at[2 * slot + k], s1r.at[2 * slot + k], seq=seq_id(xx, at))
                )

    def video_first(delta):
        at = ring(z + delta)
        rows = aligned(at * 128, 128, 128)

        def one(h, carry):
            cols = aligned(h * HD, HD, HD)
            s = mm(g[3, rows, cols], qn[:, cols], NT) + wide(bias_a[rows, :], 4)
            m = jnp.maximum(jnp.max(s, axis=0, keepdims=True), FLOOR)
            p = jnp.exp2(s - m)
            dp = mm(g[1, rows, cols], raw_v[3, :, cols], NT)
            pa[h, rows, :] = p.astype(BF16)
            dpa[h, rows, :] = dp
            ast[h, at, 0:1, :] = m
            ast[h, at, 1:2, :] = jnp.sum(p, axis=0, keepdims=True)
            ast[h, at, 2:3, :] = jnp.sum(p * dp, axis=0, keepdims=True)
            return carry

        lax.fori_loop(0, HEADS, one, 0)

    def factor_audio(factors):
        rba[...] = column_of(factors[8:9, :])
        for n in range(2):
            half = slice(n * 64, n * 64 + 64)
            for h in range(HEADS):
                cols = head_cols(h)
                gain = gains[2 - n : 3 - n, cols] * (c if n == 0 else 1.0)
                g[2 + n, own, cols] = (raw_a[n, :, cols].astype(F32) * rba[half, :] * gain).astype(BF16)

    def factor_video(factors):
        for n in range(2):
            for k in range(4):
                rows = slice(k * HD, (k + 1) * HD)
                col = column_of(factors[n * 4 + k : n * 4 + k + 1, :])
                rbv[n, rows, :] = col
                for h in range(HEADS):
                    cols = head_cols(h)
                    gain = gains[3 * n : 3 * n + 1, cols] * (c if n == 0 else 1.0)
                    (qn, kn)[n][rows, cols] = (raw_v[n, rows, cols].astype(F32) * col * gain).astype(BF16)

    chains[1, "x", 0].wait_recv()
    gather_step(1, 0)
    gather_step(0, 1)
    factors = lax.rsqrt(tower_sum(0, exch) / depth + EPS)
    factor_audio(factors)
    gather_step(2, 0)
    gather_over(3)
    factor_video(factors)
    far = nr

    def maybe(a, k):
        if k <= far:
            gather_step(a, k)

    maybe(0, 2)
    maybe(1, 1)
    maybe(2, 1)
    chains[3, "x", 0].wait_recv()
    gather_step(3, 0)
    maybe(0, 3)
    audio_first(0)
    maybe(1, 2)
    maybe(2, 2)
    maybe(3, 1)
    video_first(0)
    maybe(0, 4)
    maybe(1, 3)
    maybe(2, 3)
    maybe(3, 2)

    def both_ways(run, dist):
        run(-dist)
        if dist <= nl:
            run(dist)

    both_ways(audio_first, 1)
    maybe(2, 4)
    maybe(1, 4)
    maybe(3, 3)
    both_ways(video_first, 1)
    for dist in range(2, nr + 1):
        both_ways(audio_first, dist)
        if dist == 2:
            maybe(3, 4)
        both_ways(video_first, dist)

    def video_second(h):
        cols = head_cols(h)
        m = ast[h, 0, 0:1, :]
        for k in range(1, n_z):
            m = jnp.maximum(m, ast[h, k, 0:1, :])
        total = jnp.zeros((1, VROWS), F32)
        inner = jnp.zeros((1, VROWS), F32)
        for k in range(n_z):
            f = jnp.exp2(ast[h, k, 0:1, :] - m)
            acf[k, 0:1, :] = f
            total = total + f * ast[h, k, 1:2, :]
            inner = inner + f * ast[h, k, 2:3, :]
        inverse = 1.0 / total
        delta = inner * inverse

        def one(k, carry):
            rows = aligned(k * 128, 128, 128)
            w = pa[h, rows, :].astype(F32) * (acf[k, 0:1, :] * inverse)
            pa[h, rows, :] = w.astype(BF16)
            dsa[rows, :] = (w * (dpa[h, rows, :] - delta)).astype(BF16)
            return carry

        lax.fori_loop(0, n_z, one, 0)
        low = pa[h]
        ds = dsa[...]
        dk = mm(ds, qn[:, cols], NN) * unscale
        part[0, :, h * 256 : h * 256 + HD] = dk.astype(BF16)
        part[0, :, h * 256 + HD : h * 256 + 256] = mm(low, raw_v[3, :, cols], NN).astype(BF16)
        prod = dk * g[3, :, cols].astype(F32)
        gbuf[s_at, 1:2, cols] = jnp.sum(prod, axis=0, keepdims=True) / gains[1:2, cols]
        acc[0] = prod if h == 0 else acc[0] + prod
        vout[:, cols] = mm(g[1, :, cols], low, TN).T.astype(BF16)
        dvid[0, :, cols] = mm(g[3, :, cols], ds, TN).T * scale

    tile = 256
    tiles = arows // tile

    def audio_second(h):
        cols = head_cols(h)

        def one(t, carry):
            lanes = aligned(t * tile, tile, tile)

            def stat(ref, at):
                return jnp.concatenate([ref[t * 2, at : at + 1, :], ref[t * 2 + 1, at : at + 1, :]], axis=1)

            coef = jnp.exp2(stat(sloc, h) - stat(sall, h))
            delta = stat(sall, 3 + h)
            w = pb[h, :, lanes].astype(F32) * coef
            pb[h, :, lanes] = w.astype(BF16)
            dsb[:, lanes] = (w * (dpb[h, :, lanes] - delta)).astype(BF16)
            return carry

        lax.fori_loop(0, tiles, one, 0)
        low = pb[h]
        ds = dsb[...]
        part[1, :, h * 256 : h * 256 + HD] = mm(raw_v[2, :, cols], low, TN).T.astype(BF16)
        dq = mm(kn[:, cols], ds, TN).T * scale
        part[1, :, h * 256 + HD : h * 256 + 256] = dq.astype(BF16)
        prod = dq * g[2, :, cols].astype(F32) * (1.0 / c)
        gbuf[s_at, 2:3, cols] = jnp.sum(prod, axis=0, keepdims=True) / gains[2:3, cols]
        acc[1] = prod if h == 0 else acc[1] + prod
        dvid[1, :, cols] = mm(ds, g[2, :, cols], NN) * unscale
        vvg[:, cols] = mm(low, g[0, :, cols], NN).astype(BF16)

    rchain = {}

    def group(h):
        return slice(h * 256, (h + 1) * 256)

    def scatter_over(h):
        for k, delta in enumerate(order):
            at = ring(z + delta)
            rchain[h, "x", delta % n_z] = send(
                part.at[1, aligned(at * 128 + (1 - x) * 64, 64, 64), group(h)],
                xin.at[at, :, group(h)],
                xi_s.at[h, k], xi_r.at[h, k], seq=over,
            )

    order = []
    for dist in range(nr, 0, -1):
        order.append(dist)
        if dist <= nl:
            order.append(-dist)
    order.append(0)

    def scatter_step(b, h, k):
        cols = group(h)
        for name, n, to, way, base, land in (("r", nr, right, 1, 0, rr), ("l", nl, left, -1, nr, rl)):
            if k >= n:
                continue
            delta = way * (n - k)
            at = ring(z + delta)
            size = 128 if b == 0 else 64
            rows = aligned(at * 128, 128, 128) if b == 0 else aligned(at * 128 + x * 64, 64, 64)
            if b == 1 or k > 0:
                total = part[b, rows, cols].astype(F32)
                if b == 1:
                    rchain[h, "x", delta % n_z].wait_recv()
                    total = total + xin[at, :, cols].astype(F32)
                if k > 0:
                    rchain[b, h, name, k - 1].wait_recv()
                    total = total + land[b, k - 1, 0:size, cols].astype(F32)
                part[b, rows, cols] = total.astype(BF16)
            rchain[b, h, name, k] = send(
                part.at[b, rows, cols], land.at[b, k, 0:size, cols],
                rs_s.at[b, h, base + k], rs_r.at[b, h, base + k], seq=to,
            )

    def scatter_landed(b, h, total, size):
        cols = group(h)
        rchain[b, h, "r", nr - 1].wait_recv()
        total = total + rr[b, nr - 1, 0:size, cols].astype(F32)
        if nl > 0:
            rchain[b, h, "l", nl - 1].wait_recv()
            total = total + rl[b, nl - 1, 0:size, cols].astype(F32)
        return total

    def key_cross(h):
        cols = group(h)
        fin[:, cols] = scatter_landed(0, h, part[0, aligned(z * 128, 128, 128), cols].astype(F32), 128)
        xs[:, cols] = fin[aligned((1 - x) * 64, 64, 64), cols].astype(BF16)
        rchain[h, "k"] = send(xs.at[:, cols], xr.at[:, cols], rs_s.at[0, h, n_z - 1], rs_r.at[0, h, n_z - 1], seq=over)

    def key_end(h):
        cols = group(h)
        rchain[h, "k"].wait_recv()
        return fin[aligned(x * 64, 64, 64), cols] + xr[:, cols].astype(F32)

    def query_end(h):
        cols = group(h)
        rchain[h, "x", 0].wait_recv()
        return scatter_landed(1, h, part[1, own, cols].astype(F32) + xin[z, :, cols].astype(F32), 64)

    video_second(0)
    scatter_step(0, 0, 0)

    for copy in stat1:
        copy.wait_recv()
    mx = sin[0, 0:3, :]
    for k in range(1, n_seq):
        mx = jnp.maximum(mx, sin[k, 0:3, :])
    tot = jnp.zeros((3, HD), F32)
    inn = jnp.zeros((3, HD), F32)
    for k in range(n_seq):
        f = jnp.exp2(sin[k, 0:3, :] - mx)
        tot = tot + sin[k, 3:6, :] * f
        inn = inn + sin[k, 6:9, :] * f
    sres[0:3, :] = mx + jnp.log2(tot)
    sres[3:6, :] = inn / tot
    stat2 = [send(sres, sall.at[z], s2s.at[k], s2r.at[k], seq=seq_id(x, z + k)) for k in range(1, n_z)]
    sall[z] = sres[...]

    def steps(b, at):
        for h in range(HEADS):
            k = at - h
            if 0 <= k < nr:
                scatter_step(b, h, k)

    video_second(1)
    steps(0, 1)
    video_second(2)
    steps(0, 2)
    for copy in stat2:
        copy.wait_recv()
    audio_second(0)
    scatter_over(0)
    steps(0, 3)
    audio_second(1)
    scatter_over(1)
    steps(0, 4)
    audio_second(2)
    scatter_over(2)
    steps(0, 5)

    for n, row in ((0, 0), (1, 3)):
        inner = dvid[n] * (qn, kn)[n][...].astype(F32) * (1.0 / c if n == 0 else 1.0)
        put_video(1, n, lanes_of(inner))
        gbuf[s_at, row : row + 1, :] = jnp.sum(inner, axis=0, keepdims=True) / gains[row : row + 1, :]
    exch = tower_start(1)
    for n in range(2):
        row = lanes_of(acc[n])
        for k in range(n_z):
            ub[k, n : n + 1, :] = row[:, k * HD : (k + 1) * HD]
    ucopies = []
    for k in range(1, n_seq):
        to = lax.rem(s_at + k, n_seq)
        ucopies.append(send(ub.at[lax.rem(to, n_z)], uin.at[s_at], us.at[k], ur.at[k], seq=to))
    uin[s_at] = ub[z]
    gcopies = [
        send(gbuf.at[s_at], gbuf.at[s_at], ggs.at[k], ggr.at[k], seq=lax.rem(s_at + k, n_seq))
        for k in range(1, n_seq)
    ]
    outs = []

    def write(src, dst):
        copy = pltpu.make_async_copy(src, dst, ost.at[len(outs)])
        copy.start()
        outs.append(copy)

    write(vout, vo_h)
    write(vvg, vvg_h)
    steps(1, 0)
    for h in range(HEADS):
        key_cross(h)
    steps(1, 1)

    inner = tower_sum(1, exch) * (1.0 / depth)

    def video_grad(n):
        row = 3 * n
        for k in range(4):
            rows = slice(k * HD, (k + 1) * HD)
            col = column_of(inner[n * 4 + k : n * 4 + k + 1, :])
            r = rbv[n, rows, :]
            for h in range(HEADS):
                cols = head_cols(h)
                grad = r * gains[row : row + 1, cols] * dvid[n, rows, cols] - raw_v[n, rows, cols].astype(F32) * (r * r * col)
                (qn, kn)[n][rows, cols] = grad.astype(BF16)
        write((qn, kn)[n], (vqg_h, vkg_h)[n])

    video_grad(0)
    steps(1, 2)
    for copy in ucopies:
        copy.wait_recv()
    total = uin[0]
    for k in range(1, n_seq):
        total = total + uin[k]
    small[2, t_at, 0:8, :] = total
    uexch = tower_start(2)
    video_grad(1)
    steps(1, 3)
    for copy in gcopies:
        copy.wait_recv()
    total = gbuf[0]
    for k in range(1, n_seq):
        total = total + gbuf[k]
    if n_dp > 1:
        dbuf[d_at] = total
        gcopy = send(dbuf.at[d_at], dbuf.at[d_at], ds_.at[0], dr_.at[0], dp=1 - d_at)
    steps(1, 4)
    uall = tower_sum(2, uexch) * (1.0 / depth)
    for n in range(2):
        ucol[n] = column_of(uall[n : n + 1, :])

    def audio_grad(n, h, total):
        cols = head_cols(h)
        r = rba[(1 - n) * 64 : (2 - n) * 64, :]
        col = ucol[n, aligned(x * 64, 64, 64), :]
        return (r * gains[n + 1 : n + 2, cols] * total - raw_a[1 - n, :, cols].astype(F32) * (r * r * col)).astype(BF16)

    for h in range(HEADS):
        both = key_end(h)
        outa[2, :, head_cols(h)] = audio_grad(0, h, both[:, 0:HD])
        outa[3, :, head_cols(h)] = both[:, HD:].astype(BF16)
    write(outa.at[2], akg_h)
    write(outa.at[3], avg_h)
    if n_dp > 1:
        gcopy.wait_recv()
        total = dbuf[0] + dbuf[1]
    gout[...] = total[0:4, :]
    write(gout, gg_h)
    steps(1, 5)
    for h in range(HEADS):
        both = query_end(h)
        outa[0, :, head_cols(h)] = both[:, 0:HD].astype(BF16)
        outa[1, :, head_cols(h)] = audio_grad(1, h, both[:, HD:])
    write(outa.at[0], aco_h)
    write(outa.at[1], aqg_h)
    for copy in outs:
        copy.wait()
    for copy in pending:
        copy.wait_send()


def hand_over(*refs):
    count = (len(refs) - 1) // 2
    sems = refs[-1]
    copies = [pltpu.make_async_copy(refs[n], refs[count + n], sems.at[n]) for n in range(count)]
    for copy in copies:
        copy.start()
    for copy in copies:
        copy.wait()


def solution(mesh):
    sizes = tuple(mesh.shape[name] for name in ("tower", "seq", "dp"))
    n_tower, n_seq, n_dp = sizes
    n_z = n_seq // 2
    arows = n_seq * 64
    nr = n_z // 2
    nl = max(n_z - 1 - nr, 1)
    any_spec = pl.BlockSpec(memory_space=pl.ANY)
    vmem = pl.BlockSpec(memory_space=pltpu.VMEM)
    smem = pl.BlockSpec(memory_space=pltpu.SMEM)
    dma = lambda *shape: pltpu.SemaphoreType.DMA(shape)
    low = lambda *shape: pltpu.VMEM(shape, BF16)
    full = lambda *shape: pltpu.VMEM(shape, F32)

    def body(vq, ak, av, aq, vk, vv, up, ao, gains, vlen, alen):
        video = jax.ShapeDtypeStruct((VROWS, WIDTH), BF16)
        audio = jax.ShapeDtypeStruct((64, WIDTH), BF16)
        shapes = (video, audio, video, audio, audio, audio, video, video, jax.ShapeDtypeStruct((4, WIDTH), F32))
        results = pl.pallas_call(
            functools.partial(kernel, sizes),
            out_shape=shapes,
            in_specs=[any_spec] * 8 + [vmem, smem, smem],
            out_specs=tuple([any_spec] * 9),
            scratch_shapes=[
                low(4, arows, WIDTH),
                low(4, VROWS, WIDTH),
                low(2, 64, WIDTH),
                low(VROWS, WIDTH),
                low(VROWS, WIDTH),
                full(2, VROWS, WIDTH),
                low(VROWS, WIDTH),
                low(VROWS, WIDTH),
                low(2, arows, 2 * WIDTH),
                low(2, nr, 128, 2 * WIDTH),
                low(2, nl, 128, 2 * WIDTH),
                low(n_z, 64, 2 * WIDTH),
                low(64, 2 * WIDTH),
                low(64, 2 * WIDTH),
                full(128, 2 * WIDTH),
                low(HEADS, arows, VROWS),
                full(HEADS, arows, VROWS),
                low(arows, VROWS),
                full(HEADS, n_z, 8, VROWS),
                full(n_z, 8, VROWS),
                low(HEADS, VROWS, arows),
                full(HEADS, VROWS, arows),
                low(VROWS, arows),
                full(2, arows, HD),
                full(arows, HD),
                full(VROWS, HD),
                full(2, VROWS, HD),
                full(128, HD),
                full(3, n_tower, 16, HD),
                full(n_z, 16, HD),
                full(n_seq, 16, HD),
                full(8, HD),
                full(n_z, 8, HD),
                full(n_z, 8, HD),
                full(n_seq, 8, HD),
                full(2, 128, HD),
                full(n_seq, 8, WIDTH),
                full(2, 8, WIDTH),
                full(4, WIDTH),
                low(4, 64, WIDTH),
                dma(8), dma(4, n_z), dma(4, n_z), dma(2, n_z), dma(2, n_z), dma(3, n_tower), dma(3, n_tower),
                dma(n_seq), dma(n_seq), dma(n_z), dma(n_z), dma(n_seq), dma(n_seq), dma(n_seq), dma(n_seq),
                dma(1), dma(1), dma(2, HEADS, n_z), dma(2, HEADS, n_z), dma(HEADS, n_z), dma(HEADS, n_z), dma(9),
            ],
            compiler_params=pltpu.CompilerParams(
                collective_id=0, has_side_effects=True, vmem_limit_bytes=58 * 1024 * 1024
            ),
            cost_estimate=pl.CostEstimate(flops=4_800_000_000, bytes_accessed=4_000_000, transcendentals=3_200_000),
        )(vq[0], ak[0], av[0], aq[0], vk[0], vv[0], up[0], ao[0], gains, vlen, alen)
        results = pl.pallas_call(
            hand_over,
            out_shape=shapes,
            in_specs=[any_spec] * 9,
            out_specs=tuple([any_spec] * 9),
            scratch_shapes=[dma(9)],
        )(*results)
        return tuple(r[None] for r in results[:8]) + (results[8],)

    spec = P("dp", "seq", "tower")
    return jax.shard_map(
        body,
        mesh=mesh,
        in_specs=(spec,) * 8 + (P(None, "tower"), P("dp"), P("dp")),
        out_specs=(spec,) * 8 + (P(None, "tower"),),
        check_vma=False,
    )
```

```python
import functools
import math

import jax
import jax.numpy as jnp
from jax import lax
from jax.experimental import pallas as pl
from jax.experimental.pallas import tpu as pltpu
from jax.sharding import PartitionSpec as P

HD = 128
HEADS = 3
WIDTH = HEADS * HD
VROWS = 512
EPS = 1e-06
MASKED = -1e30
FLOOR = -1e29
F32 = jnp.float32
BF16 = jnp.bfloat16
MESH = pl.DeviceIdType.MESH

NT = (((1,), (1,)), ((), ()))
NN = (((1,), (0,)), ((), ()))
TN = (((0,), (0,)), ((), ()))


def mm(a, b, dims):
    return lax.dot_general(a, b, dims, preferred_element_type=F32)


def aligned(start, size, unit):
    return pl.ds(pl.multiple_of(start, unit), size)


def lanes_of(products):
    part = products[:, 0:HD]
    for k in range(1, products.shape[1] // HD):
        part = part + products[:, k * HD : (k + 1) * HD]
    return jnp.sum(part.T, axis=0, keepdims=True)


def column_of(row):
    return jnp.broadcast_to(row, (HD, HD)).T


def head_cols(h):
    return slice(h * HD, (h + 1) * HD)


def wide(block, n):
    return jnp.concatenate([block] * n, axis=1)


def kernel(
    sizes,
    vq_h, ak_h, av_h, aq_h, vk_h, vv_h, up_h, ao_h, gains, vlen, alen,
    vo_h, aco_h, vqg_h, akg_h, avg_h, aqg_h, vkg_h, vvg_h, gg_h,
    g, raw_v, gqn, gkn, qn, kn, dvid, vout, vvg, part, rr, rl, xin, xs, xr, fin,
    pa, dpa, dsa, ast, acf, pb, dpb, dsb, acc, bias_a, bias_v, rbv, rba, small, fbuf,
    sloc, sin, sres, sall, ub, uin, ucol, gbuf, dbuf, gout, outa,
    ld, gs, gr, gxs, gxr, ts, tr, fs, fr, s1s, s1r, s2s, s2r, us, ur, ggs, ggr, ds_, dr_,
    rs_s, rs_r, xi_s, xi_r, ost,
):
    n_tower, n_seq, n_dp = sizes
    n_z = n_seq // 2
    nr = n_z // 2
    nl = n_z - 1 - nr
    arows = n_seq * 64
    depth = n_tower * WIDTH
    scale = 1.0 / math.sqrt(HD)
    c = scale * math.log2(math.e)
    unscale = scale / c

    t_at = lax.axis_index("tower")
    s_at = lax.axis_index("seq")
    d_at = lax.axis_index("dp")
    z = lax.rem(s_at, n_z)
    x = s_at // n_z

    def ring(zz):
        return lax.rem(zz + 2 * n_z, n_z)

    def seq_id(xx, zz):
        return xx * n_z + ring(zz)

    right, left, over = seq_id(x, z + 1), seq_id(x, z - 1), seq_id(1 - x, z)

    pending = []

    def send(src, dst, send_sem, recv_sem, **dev):
        copy = pltpu.make_async_remote_copy(
            src_ref=src, dst_ref=dst, send_sem=send_sem, recv_sem=recv_sem,
            device_id=dev, device_id_type=MESH,
        )
        copy.start()
        pending.append(copy)
        return copy

    own = aligned(z * 128 + x * 64, 64, 64)
    loads = []
    for n, (src, dst) in enumerate([
        (aq_h, g.at[2, own]),
        (ak_h, g.at[3, own]),
        (ao_h, g.at[0, own]),
        (av_h, g.at[1, own]),
        (vq_h, raw_v.at[0]),
        (vk_h, raw_v.at[1]),
        (vv_h, raw_v.at[2]),
        (up_h, raw_v.at[3]),
    ]):
        loads.append(pltpu.make_async_copy(src, dst, ld.at[n]))
        loads[n].start()
    barrier = pltpu.get_barrier_semaphore()
    peers = 0
    for k in range(1, n_seq):
        pl.semaphore_signal(barrier, inc=1, device_id={"seq": lax.rem(s_at + k, n_seq)}, device_id_type=MESH)
        peers += 1
    for k in range(1, n_tower):
        pl.semaphore_signal(barrier, inc=1, device_id={"tower": lax.rem(t_at + k, n_tower)}, device_id_type=MESH)
        peers += 1
    if n_dp > 1:
        pl.semaphore_signal(barrier, inc=1, device_id={"dp": 1 - d_at}, device_id_type=MESH)
        peers += 1

    def put_video(n, which, row):
        for k in range(4):
            small[n, t_at, which * 4 + k : which * 4 + k + 1, :] = row[:, k * HD : (k + 1) * HD]

    for n in range(3):
        small[n, t_at] = jnp.zeros((16, HD), F32)
    sloc[...] = jnp.zeros_like(sloc)
    sres[...] = jnp.zeros_like(sres)
    ub[...] = jnp.zeros_like(ub)
    gbuf[s_at] = jnp.zeros((8, WIDTH), F32)
    loads[0].wait()
    loads[1].wait()
    both = jnp.concatenate([g[2, own, :].astype(F32), g[3, own, :].astype(F32)], axis=0)
    small[0, t_at, 8:9, :] = lanes_of(both * both)
    rho = lax.broadcasted_iota(jnp.int32, (arows, HD), 0)
    token = ((rho // 64) % 2) * (n_z * 64) + (rho // 128) * 64 + rho % 64
    bias_a[...] = jnp.where(token < alen[0], 0.0, MASKED)
    vtok = s_at * VROWS + lax.broadcasted_iota(jnp.int32, (VROWS, HD), 0)
    bias_v[...] = jnp.where(vtok < vlen[0], 0.0, MASKED)
    for n in range(2):
        loads[4 + n].wait()
        widened = raw_v[n].astype(F32)
        put_video(0, n, lanes_of(widened * widened))
    for n in (2, 3, 6, 7):
        loads[n].wait()
    pl.semaphore_wait(barrier, peers)

    def tower_start(n):
        return [
            send(small.at[n, t_at], small.at[n, t_at], ts.at[n, k], tr.at[n, k], tower=lax.rem(t_at + k, n_tower))
            for k in range(1, n_tower)
        ]

    def tower_sum(n, copies):
        for copy in copies:
            copy.wait_recv()
        total = small[n, 0]
        for k in range(1, n_tower):
            total = total + small[n, k]
        return total

    chains = {}

    def gather_step(a, k):
        last_over = a % 2 == 0
        sign = 1 if a >= 2 else -1
        ways = (("l", nr, left if a >= 2 else right, sign, 0), ("s", nl, right if a >= 2 else left, -sign, nr))

        def block(zz):
            if last_over:
                return g.at[a, aligned(ring(zz) * 128 + x * 64, 64, 64)]
            return g.at[a, aligned(ring(zz) * 128, 128, 128)]

        if k == 0 and last_over:
            chains[a, "x", 0] = send(block(z), block(z), gxs.at[a // 2, 0], gxr.at[a // 2, 0], seq=over)
        for name, n, to, way, base in ways:
            if k > n:
                continue
            here = block(z + way * k)
            if k > 0:
                chains[a, name, k].wait_recv()
            if k < n:
                chains[a, name, k + 1] = send(here, here, gs.at[a, 1 + base + k], gr.at[a, 1 + base + k], seq=to)
            if k > 0 and last_over:
                chains[a, "x", base + k] = send(here, here, gxs.at[a // 2, base + k], gxr.at[a // 2, base + k], seq=over)

    def gather_over(a):
        chains[a, "x", 0] = send(g.at[a, own], g.at[a, own], gs.at[a, 0], gr.at[a, 0], seq=over)

    def over_wait(a, delta):
        towards = delta if a >= 2 else -delta
        if delta == 0:
            at = 0
        elif abs(delta) == nr or towards > 0:
            at = abs(delta)
        else:
            at = nr + abs(delta)
        chains[a, "x", at].wait_recv()

    exch = tower_start(0)
    gather_over(1)
    gather_step(0, 0)
    gather_over(3)
    gather_step(2, 0)

    everyone = [(delta, k) for delta in range(n_z) for k in range(2) if delta or k]
    fsent = {}

    def factors_out(row):
        fbuf[s_at] = jnp.broadcast_to(row, (8, HD))
        for delta, k in everyone:
            to = seq_id(1 - x if k else x, z + delta)
            at = 2 * delta + k
            fsent[delta, k] = send(fbuf.at[s_at], fbuf.at[s_at], fs.at[at], fr.at[at], seq=to)

    def factors_in(delta):
        for k in range(2):
            if delta or k:
                fsent[-delta % n_z, k].wait_recv()

    def pair_factors(at, n):
        half = slice(n * 64, n * 64 + 64)
        return jnp.concatenate([column_of(fbuf[seq_id(xx, at), 0:1, :])[half] for xx in range(2)], axis=0)

    stat1 = []

    def audio_first(delta):
        at = ring(z + delta)
        rows = aligned(at * 128, 128, 128)
        over_wait(0, delta)
        over_wait(2, delta)
        factors_in(delta)
        col = pair_factors(at, 0)
        for h in range(HEADS):
            cols = head_cols(h)
            gqn[rows, cols] = (g[2, rows, cols].astype(F32) * col * (gains[2:3, cols] * c)).astype(BF16)

        def one(h, carry):
            cols = aligned(h * HD, HD, HD)
            s = mm(kn[:, cols], gqn[rows, cols], NT) + bias_v[...]
            m = jnp.maximum(jnp.max(s, axis=0, keepdims=True), FLOOR)
            p = jnp.exp2(s - m)
            dp = mm(raw_v[2, :, cols], g[0, rows, cols], NT)
            pb[h, :, rows] = p.astype(BF16)
            dpb[h, :, rows] = dp
            sloc[at, pl.ds(h, 1), :] = m
            sloc[at, pl.ds(3 + h, 1), :] = jnp.sum(p, axis=0, keepdims=True)
            sloc[at, pl.ds(6 + h, 1), :] = jnp.sum(p * dp, axis=0, keepdims=True)
            return carry

        lax.fori_loop(0, HEADS, one, 0)
        slot = delta % n_z
        for k, xx in enumerate((x, 1 - x)):
            if delta == 0 and k == 0:
                sin[s_at] = sloc[at]
            else:
                stat1.append(
                    send(sloc.at[at], sin.at[s_at], s1s.at[2 * slot + k], s1r.at[2 * slot + k], seq=seq_id(xx, at))
                )

    def video_first(delta):
        at = ring(z + delta)
        rows = aligned(at * 128, 128, 128)
        col = pair_factors(at, 1)
        for h in range(HEADS):
            cols = head_cols(h)
            gkn[rows, cols] = (g[3, rows, cols].astype(F32) * col * gains[1:2, cols]).astype(BF16)

        def one(h, carry):
            cols = aligned(h * HD, HD, HD)
            s = mm(gkn[rows, cols], qn[:, cols], NT) + wide(bias_a[rows, :], 4)
            m = jnp.maximum(jnp.max(s, axis=0, keepdims=True), FLOOR)
            p = jnp.exp2(s - m)
            dp = mm(g[1, rows, cols], raw_v[3, :, cols], NT)
            pa[h, rows, :] = p.astype(BF16)
            dpa[h, rows, :] = dp
            ast[h, at, 0:1, :] = m
            ast[h, at, 1:2, :] = jnp.sum(p, axis=0, keepdims=True)
            ast[h, at, 2:3, :] = jnp.sum(p * dp, axis=0, keepdims=True)
            return carry

        lax.fori_loop(0, HEADS, one, 0)

    def factor_video(factors):
        for n in range(2):
            for k in range(4):
                rows = slice(k * HD, (k + 1) * HD)
                col = column_of(factors[n * 4 + k : n * 4 + k + 1, :])
                rbv[n, rows, :] = col
                for h in range(HEADS):
                    cols = head_cols(h)
                    gain = gains[3 * n : 3 * n + 1, cols] * (c if n == 0 else 1.0)
                    (qn, kn)[n][rows, cols] = (raw_v[n, rows, cols].astype(F32) * col * gain).astype(BF16)

    def maybe(*what):
        for a, k in what:
            if k <= nr:
                gather_step(a, k)

    def both_ways(run, dist):
        if dist > nr:
            return
        if dist == 0:
            run(0)
            return
        run(-dist)
        if dist <= nl:
            run(dist)

    maybe((0, 1))
    chains[1, "x", 0].wait_recv()
    gather_step(1, 0)
    maybe((2, 1))
    chains[3, "x", 0].wait_recv()
    gather_step(3, 0)
    factors = lax.rsqrt(tower_sum(0, exch) / depth + EPS)
    factors_out(factors[8:9, :])
    rba[...] = column_of(factors[8:9, :])
    factor_video(factors)
    maybe((0, 2), (2, 2), (1, 1), (3, 1))
    audio_first(0)
    maybe((0, 3), (2, 3))
    video_first(0)
    maybe((1, 2))
    both_ways(audio_first, 1)
    maybe((0, 4), (2, 4), (3, 2))
    both_ways(video_first, 1)
    both_ways(audio_first, 2)
    maybe((1, 3), (3, 3))
    both_ways(video_first, 2)
    both_ways(audio_first, 3)
    both_ways(audio_first, 4)
    maybe((1, 4), (3, 4))
    both_ways(video_first, 3)

    for copy in stat1:
        copy.wait_recv()
    mx = sin[0, 0:3, :]
    for k in range(1, n_seq):
        mx = jnp.maximum(mx, sin[k, 0:3, :])
    tot = jnp.zeros((3, HD), F32)
    inn = jnp.zeros((3, HD), F32)
    for k in range(n_seq):
        f = jnp.exp2(sin[k, 0:3, :] - mx)
        tot = tot + sin[k, 3:6, :] * f
        inn = inn + sin[k, 6:9, :] * f
    sres[0:3, :] = mx + jnp.log2(tot)
    sres[3:6, :] = inn / tot
    stat2 = [send(sres, sall.at[z], s2s.at[k], s2r.at[k], seq=seq_id(x, z + k)) for k in range(1, n_z)]
    sall[z] = sres[...]
    both_ways(video_first, 4)

    def video_second(h):
        cols = head_cols(h)
        m = ast[h, 0, 0:1, :]
        for k in range(1, n_z):
            m = jnp.maximum(m, ast[h, k, 0:1, :])
        total = jnp.zeros((1, VROWS), F32)
        inner = jnp.zeros((1, VROWS), F32)
        for k in range(n_z):
            f = jnp.exp2(ast[h, k, 0:1, :] - m)
            acf[k, 0:1, :] = f
            total = total + f * ast[h, k, 1:2, :]
            inner = inner + f * ast[h, k, 2:3, :]
        inverse = 1.0 / total
        delta = inner * inverse

        def one(k, carry):
            rows = aligned(k * 128, 128, 128)
            w = pa[h, rows, :].astype(F32) * (acf[k, 0:1, :] * inverse)
            pa[h, rows, :] = w.astype(BF16)
            dsa[rows, :] = (w * (dpa[h, rows, :] - delta)).astype(BF16)
            return carry

        lax.fori_loop(0, n_z, one, 0)
        low = pa[h]
        ds = dsa[...]
        dk = mm(ds, qn[:, cols], NN) * unscale
        part[h, :, 0:HD] = dk.astype(BF16)
        part[h, :, HD:] = mm(low, raw_v[3, :, cols], NN).astype(BF16)
        prod = dk * gkn[:, cols].astype(F32)
        gbuf[s_at, 1:2, cols] = jnp.sum(prod, axis=0, keepdims=True) / gains[1:2, cols]
        acc[0] = prod if h == 0 else acc[0] + prod
        vout[:, cols] = mm(g[1, :, cols], low, TN).T.astype(BF16)
        dvid[0, :, cols] = mm(gkn[:, cols], ds, TN).T * scale

    tile = 256
    tiles = arows // tile

    def audio_second(h):
        cols = head_cols(h)

        def one(t, carry):
            lanes = aligned(t * tile, tile, tile)

            def stat(ref, at):
                return jnp.concatenate([ref[t * 2, at : at + 1, :], ref[t * 2 + 1, at : at + 1, :]], axis=1)

            coef = jnp.exp2(stat(sloc, h) - stat(sall, h))
            delta = stat(sall, 3 + h)
            w = pb[h, :, lanes].astype(F32) * coef
            pb[h, :, lanes] = w.astype(BF16)
            dsb[:, lanes] = (w * (dpb[h, :, lanes] - delta)).astype(BF16)
            return carry

        lax.fori_loop(0, tiles, one, 0)
        low = pb[h]
        ds = dsb[...]
        part[HEADS + h, :, 0:HD] = mm(raw_v[2, :, cols], low, TN).T.astype(BF16)
        dq = mm(kn[:, cols], ds, TN).T * scale
        part[HEADS + h, :, HD:] = dq.astype(BF16)
        prod = dq * gqn[:, cols].astype(F32) * (1.0 / c)
        gbuf[s_at, 2:3, cols] = jnp.sum(prod, axis=0, keepdims=True) / gains[2:3, cols]
        acc[1] = prod if h == 0 else acc[1] + prod
        dvid[1, :, cols] = mm(ds, gqn[:, cols], NN) * unscale
        vvg[:, cols] = mm(low, g[0, :, cols], NN).astype(BF16)

    over_first = (0, HEADS + 1, HEADS + 2)
    mirrored = (0, 2, HEADS + 2)
    rchain = {}
    order = []
    for dist in range(nr, 0, -1):
        order.append(dist)
        if dist <= nl:
            order.append(-dist)
    order.append(0)

    def scatter_over(*units):
        for k in range(n_z):
            for u in units:
                delta = -order[k] if u in mirrored else order[k]
                at = ring(z + delta)
                rchain[u, "x", delta % n_z] = send(
                    part.at[u, aligned(at * 128 + (1 - x) * 64, 64, 64)], xin.at[u, at],
                    xi_s.at[u, k], xi_r.at[u, k], seq=over,
                )

    def scatter_step(*what):
        for u, k in what:
            early = u in over_first
            way = -1 if u in mirrored else 1
            size = 64 if early else 128
            ends = (right, left)[::way]
            for name, n, to, sign, base, land in (
                ("l", nr, ends[0], way, 0, rr), ("s", nl, ends[1], -way, nr, rl),
            ):
                if k >= n:
                    continue
                delta = sign * (n - k)
                at = ring(z + delta)
                rows = aligned(at * 128 + x * 64, 64, 64) if early else aligned(at * 128, 128, 128)
                if early or k > 0:
                    total = part[u, rows, :].astype(F32)
                    if early:
                        rchain[u, "x", delta % n_z].wait_recv()
                        total = total + xin[u, at].astype(F32)
                    if k > 0:
                        rchain[u, name, k - 1].wait_recv()
                        total = total + land[u, k - 1, 0:size, :].astype(F32)
                    part[u, rows, :] = total.astype(BF16)
                rchain[u, name, k] = send(
                    part.at[u, rows], land.at[u, k, 0:size], rs_s.at[u, base + k], rs_r.at[u, base + k], seq=to
                )

    def landed(u, total, size):
        rchain[u, "l", nr - 1].wait_recv()
        total = total + rr[u, nr - 1, 0:size, :].astype(F32)
        if nl > 0:
            rchain[u, "s", nl - 1].wait_recv()
            total = total + rl[u, nl - 1, 0:size, :].astype(F32)
        return total

    def scatter_cross(*units):
        for u in units:
            fin[u] = landed(u, part[u, aligned(z * 128, 128, 128), :].astype(F32), 128)
            xs[u] = fin[u, aligned((1 - x) * 64, 64, 64), :].astype(BF16)
            rchain[u, "k"] = send(xs.at[u], xr.at[u], rs_s.at[u, n_z - 1], rs_r.at[u, n_z - 1], seq=over)

    def scatter_end(u):
        if u in over_first:
            rchain[u, "x", 0].wait_recv()
            return landed(u, part[u, own, :].astype(F32) + xin[u, z].astype(F32), 64)
        rchain[u, "k"].wait_recv()
        return fin[u, aligned(x * 64, 64, 64), :] + xr[u].astype(F32)

    def steps(*what):
        scatter_step(*[(u, k) for u, k in what if k < nr])

    video_second(0)
    scatter_over(0)
    video_second(1)
    steps((1, 0))
    video_second(2)
    steps((2, 0))
    steps((0, 0))
    for copy in stat2:
        copy.wait_recv()
    audio_second(0)
    steps((3, 0), (1, 1), (2, 1), (0, 1))
    audio_second(1)
    scatter_over(4)
    audio_second(2)
    scatter_over(5)
    steps((3, 1), (1, 2), (2, 2), (0, 2))

    for n, row in ((0, 0), (1, 3)):
        inner = dvid[n] * (qn, kn)[n][...].astype(F32) * (1.0 / c if n == 0 else 1.0)
        put_video(1, n, lanes_of(inner))
        gbuf[s_at, row : row + 1, :] = jnp.sum(inner, axis=0, keepdims=True) / gains[row : row + 1, :]
    exch = tower_start(1)
    for n in range(2):
        row = lanes_of(acc[n])
        for k in range(n_z):
            ub[k, n : n + 1, :] = row[:, k * HD : (k + 1) * HD]
    ucopies = []
    for k in range(1, n_seq):
        to = lax.rem(s_at + k, n_seq)
        ucopies.append(send(ub.at[lax.rem(to, n_z)], uin.at[s_at], us.at[k], ur.at[k], seq=to))
    uin[s_at] = ub[z]
    gcopies = [
        send(gbuf.at[s_at], gbuf.at[s_at], ggs.at[k], ggr.at[k], seq=lax.rem(s_at + k, n_seq))
        for k in range(1, n_seq)
    ]
    outs = []

    def write(src, dst):
        copy = pltpu.make_async_copy(src, dst, ost.at[len(outs)])
        copy.start()
        outs.append(copy)

    write(vout, vo_h)
    write(vvg, vvg_h)
    steps((4, 0), (5, 0), (1, 3), (2, 3), (3, 2), (0, 3), (4, 1), (5, 1))

    inner = tower_sum(1, exch) * (1.0 / depth)

    def video_grad(n):
        row = 3 * n
        for k in range(4):
            rows = slice(k * HD, (k + 1) * HD)
            col = column_of(inner[n * 4 + k : n * 4 + k + 1, :])
            r = rbv[n, rows, :]
            for h in range(HEADS):
                cols = head_cols(h)
                grad = r * gains[row : row + 1, cols] * dvid[n, rows, cols] - raw_v[n, rows, cols].astype(F32) * (r * r * col)
                (qn, kn)[n][rows, cols] = grad.astype(BF16)
        write((qn, kn)[n], (vqg_h, vkg_h)[n])

    video_grad(0)
    steps((3, 3), (4, 2), (5, 2))
    for copy in ucopies:
        copy.wait_recv()
    total = uin[0]
    for k in range(1, n_seq):
        total = total + uin[k]
    small[2, t_at, 0:8, :] = total
    uexch = tower_start(2)
    video_grad(1)
    scatter_cross(1, 2)
    steps((4, 3), (5, 3))
    scatter_cross(3)
    for copy in gcopies:
        copy.wait_recv()
    total = gbuf[0]
    for k in range(1, n_seq):
        total = total + gbuf[k]
    if n_dp > 1:
        dbuf[d_at] = total
        gcopy = send(dbuf.at[d_at], dbuf.at[d_at], ds_.at[0], dr_.at[0], dp=1 - d_at)
    uall = tower_sum(2, uexch) * (1.0 / depth)
    for n in range(2):
        ucol[n] = column_of(uall[n : n + 1, :])

    def audio_grad(n, h, total):
        cols = head_cols(h)
        r = rba[(1 - n) * 64 : (2 - n) * 64, :]
        col = ucol[n, aligned(x * 64, 64, 64), :]
        return (r * gains[n + 1 : n + 2, cols] * total - g[3 - n, own, cols].astype(F32) * (r * r * col)).astype(BF16)

    if n_dp > 1:
        gcopy.wait_recv()
        total = dbuf[0] + dbuf[1]
    gout[...] = total[0:4, :]
    write(gout, gg_h)
    for h in range(HEADS):
        both = scatter_end(h)
        outa[2, :, head_cols(h)] = audio_grad(0, h, both[:, 0:HD])
        outa[3, :, head_cols(h)] = both[:, HD:].astype(BF16)
    write(outa.at[2], akg_h)
    write(outa.at[3], avg_h)
    for h in range(HEADS):
        both = scatter_end(HEADS + h)
        outa[0, :, head_cols(h)] = both[:, 0:HD].astype(BF16)
        outa[1, :, head_cols(h)] = audio_grad(1, h, both[:, HD:])
    write(outa.at[0], aco_h)
    write(outa.at[1], aqg_h)
    for copy in outs:
        copy.wait()
    for copy in pending:
        copy.wait_send()


def hand_over(*refs):
    count = (len(refs) - 1) // 2
    sems = refs[-1]
    copies = [pltpu.make_async_copy(refs[n], refs[count + n], sems.at[n]) for n in range(count)]
    for copy in copies:
        copy.start()
    for copy in copies:
        copy.wait()


def solution(mesh):
    sizes = tuple(mesh.shape[name] for name in ("tower", "seq", "dp"))
    n_tower, n_seq, n_dp = sizes
    n_z = n_seq // 2
    arows = n_seq * 64
    nr = n_z // 2
    nl = max(n_z - 1 - nr, 1)
    any_spec = pl.BlockSpec(memory_space=pl.ANY)
    vmem = pl.BlockSpec(memory_space=pltpu.VMEM)
    smem = pl.BlockSpec(memory_space=pltpu.SMEM)
    dma = lambda *shape: pltpu.SemaphoreType.DMA(shape)
    low = lambda *shape: pltpu.VMEM(shape, BF16)
    full = lambda *shape: pltpu.VMEM(shape, F32)

    def body(vq, ak, av, aq, vk, vv, up, ao, gains, vlen, alen):
        video = jax.ShapeDtypeStruct((VROWS, WIDTH), BF16)
        audio = jax.ShapeDtypeStruct((64, WIDTH), BF16)
        shapes = (video, audio, video, audio, audio, audio, video, video, jax.ShapeDtypeStruct((4, WIDTH), F32))
        results = pl.pallas_call(
            functools.partial(kernel, sizes),
            out_shape=shapes,
            in_specs=[any_spec] * 8 + [vmem, smem, smem],
            out_specs=tuple([any_spec] * 9),
            scratch_shapes=[
                low(4, arows, WIDTH),
                low(4, VROWS, WIDTH),
                low(arows, WIDTH),
                low(arows, WIDTH),
                low(VROWS, WIDTH),
                low(VROWS, WIDTH),
                full(2, VROWS, WIDTH),
                low(VROWS, WIDTH),
                low(VROWS, WIDTH),
                low(6, arows, 256),
                low(6, nr, 128, 256),
                low(6, nl, 128, 256),
                low(6, n_z, 64, 256),
                low(6, 64, 256),
                low(6, 64, 256),
                full(6, 128, 256),
                low(HEADS, arows, VROWS),
                full(HEADS, arows, VROWS),
                low(arows, VROWS),
                full(HEADS, n_z, 8, VROWS),
                full(n_z, 8, VROWS),
                low(HEADS, VROWS, arows),
                full(HEADS, VROWS, arows),
                low(VROWS, arows),
                full(2, arows, HD),
                full(arows, HD),
                full(VROWS, HD),
                full(2, VROWS, HD),
                full(128, HD),
                full(3, n_tower, 16, HD),
                full(n_seq, 8, HD),
                full(n_z, 16, HD),
                full(n_seq, 16, HD),
                full(8, HD),
                full(n_z, 8, HD),
                full(n_z, 8, HD),
                full(n_seq, 8, HD),
                full(2, 128, HD),
                full(n_seq, 8, WIDTH),
                full(2, 8, WIDTH),
                full(4, WIDTH),
                low(4, 64, WIDTH),
                dma(8), dma(4, n_z), dma(4, n_z), dma(2, n_z), dma(2, n_z), dma(3, n_tower), dma(3, n_tower),
                dma(n_seq), dma(n_seq), dma(n_seq), dma(n_seq), dma(n_z), dma(n_z), dma(n_seq), dma(n_seq),
                dma(n_seq), dma(n_seq), dma(1), dma(1), dma(6, n_z), dma(6, n_z), dma(6, n_z), dma(6, n_z), dma(9),
            ],
            compiler_params=pltpu.CompilerParams(
                collective_id=0, has_side_effects=True, vmem_limit_bytes=58 * 1024 * 1024
            ),
            cost_estimate=pl.CostEstimate(flops=4_800_000_000, bytes_accessed=4_000_000, transcendentals=3_200_000),
        )(vq[0], ak[0], av[0], aq[0], vk[0], vv[0], up[0], ao[0], gains, vlen, alen)
        results = pl.pallas_call(
            hand_over,
            out_shape=shapes,
            in_specs=[vmem] * 9,
            out_specs=tuple([any_spec] * 9),
            scratch_shapes=[dma(9)],
        )(*results)
        return tuple(r[None] for r in results[:8]) + (results[8],)

    spec = P("dp", "seq", "tower")
    return jax.shard_map(
        body,
        mesh=mesh,
        in_specs=(spec,) * 8 + (P(None, "tower"), P("dp"), P("dp")),
        out_specs=(spec,) * 8 + (P(None, "tower"),),
        check_vma=False,
    )
```

```python
import functools
import math

import jax
import jax.numpy as jnp
from jax import lax
from jax.experimental import pallas as pl
from jax.experimental.pallas import tpu as pltpu
from jax.sharding import PartitionSpec as P

HD = 128
HEADS = 3
WIDTH = HEADS * HD
VROWS = 512
EPS = 1e-06
MASKED = -1e30
FLOOR = -1e29
F32 = jnp.float32
BF16 = jnp.bfloat16
MESH = pl.DeviceIdType.MESH

NT = (((1,), (1,)), ((), ()))
NN = (((1,), (0,)), ((), ()))
TN = (((0,), (0,)), ((), ()))


def mm(a, b, dims):
    return lax.dot_general(a, b, dims, preferred_element_type=F32)


def aligned(start, size, unit):
    return pl.ds(pl.multiple_of(start, unit), size)


def lanes_of(products):
    part = products[:, 0:HD]
    for k in range(1, products.shape[1] // HD):
        part = part + products[:, k * HD : (k + 1) * HD]
    return jnp.sum(part.T, axis=0, keepdims=True)


def column_of(row):
    return jnp.broadcast_to(row, (HD, HD)).T


def head_cols(h):
    return slice(h * HD, (h + 1) * HD)


def wide(block, n):
    return jnp.concatenate([block] * n, axis=1)


def kernel(
    sizes,
    vq_h, ak_h, av_h, aq_h, vk_h, vv_h, up_h, ao_h, gains, vlen, alen,
    vo_h, aco_h, vqg_h, akg_h, avg_h, aqg_h, vkg_h, vvg_h, gg_h,
    g, raw_v, gqn, gkn, qn, kn, dvid, vout, vvg, part, rr, rl, xin, xs, xr, fin,
    pa, dpa, dsa, ast, acf, pb, dpb, dsb, acc, bias_a, bias_v, rbv, rba, small, fbuf,
    sloc, sin, sres, sall, ub, uin, ucol, gbuf, dbuf, gout, outa,
    ld, gs, gr, gxs, gxr, ts, tr, fs, fr, s1s, s1r, s2s, s2r, us, ur, ggs, ggr, ds_, dr_,
    rs_s, rs_r, xi_s, xi_r, ost,
):
    n_tower, n_seq, n_dp = sizes
    n_z = n_seq // 2
    nr = n_z // 2
    nl = n_z - 1 - nr
    arows = n_seq * 64
    depth = n_tower * WIDTH
    scale = 1.0 / math.sqrt(HD)
    c = scale * math.log2(math.e)
    unscale = scale / c

    t_at = lax.axis_index("tower")
    s_at = lax.axis_index("seq")
    d_at = lax.axis_index("dp")
    z = lax.rem(s_at, n_z)
    x = s_at // n_z

    def ring(zz):
        return lax.rem(zz + 2 * n_z, n_z)

    def seq_id(xx, zz):
        return xx * n_z + ring(zz)

    right, left, over = seq_id(x, z + 1), seq_id(x, z - 1), seq_id(1 - x, z)

    pending = []

    def send(src, dst, send_sem, recv_sem, **dev):
        copy = pltpu.make_async_remote_copy(
            src_ref=src, dst_ref=dst, send_sem=send_sem, recv_sem=recv_sem,
            device_id=dev, device_id_type=MESH,
        )
        copy.start()
        pending.append(copy)
        return copy

    own = aligned(z * 128 + x * 64, 64, 64)
    loads = []
    for n, (src, dst) in enumerate([
        (aq_h, g.at[2, own]),
        (ak_h, g.at[3, own]),
        (ao_h, g.at[0, own]),
        (av_h, g.at[1, own]),
        (vq_h, raw_v.at[0]),
        (vk_h, raw_v.at[1]),
        (vv_h, raw_v.at[2]),
        (up_h, raw_v.at[3]),
    ]):
        loads.append(pltpu.make_async_copy(src, dst, ld.at[n]))
        loads[n].start()
    barrier = pltpu.get_barrier_semaphore()
    peers = 0
    for k in range(1, n_seq):
        pl.semaphore_signal(barrier, inc=1, device_id={"seq": lax.rem(s_at + k, n_seq)}, device_id_type=MESH)
        peers += 1
    for k in range(1, n_tower):
        pl.semaphore_signal(barrier, inc=1, device_id={"tower": lax.rem(t_at + k, n_tower)}, device_id_type=MESH)
        peers += 1
    if n_dp > 1:
        pl.semaphore_signal(barrier, inc=1, device_id={"dp": 1 - d_at}, device_id_type=MESH)
        peers += 1

    def put_video(n, which, row):
        for k in range(4):
            small[n, t_at, which * 4 + k : which * 4 + k + 1, :] = row[:, k * HD : (k + 1) * HD]

    for n in range(4):
        loads[n].wait()
    pl.semaphore_wait(barrier, peers)

    def tower_start(n):
        return [
            send(small.at[n, t_at], small.at[n, t_at], ts.at[n, k], tr.at[n, k], tower=lax.rem(t_at + k, n_tower))
            for k in range(1, n_tower)
        ]

    def tower_sum(n, copies):
        for copy in copies:
            copy.wait_recv()
        total = small[n, 0]
        for k in range(1, n_tower):
            total = total + small[n, k]
        return total

    arrays = (0, 2, 1, 3, 1, 3)
    chains = {}

    def gather_step(n, k):
        a = arrays[n]
        sign = 1 if n % 2 else -1
        ways = (("l", nr, left if n % 2 else right, sign, 0), ("s", nl, right if n % 2 else left, -sign, nr))
        half = 1 - x if n >= 4 else x

        def block(zz):
            return g.at[a, aligned(ring(zz) * 128 + half * 64, 64, 64)]

        if k == 0 and n >= 4:
            chains[n - 2, "x", 0].wait_recv()
        for name, count, to, way, base in ways:
            if k > count:
                continue
            here = block(z + way * k)
            if k > 0:
                chains[n, name, k].wait_recv()
            if k < count:
                chains[n, name, k + 1] = send(here, here, gs.at[n, base + k], gr.at[n, base + k], seq=to)
            if k > 0 and n < 2:
                chains[n, "x", base + k] = send(here, here, gxs.at[n, base + k], gxr.at[n, base + k], seq=over)

    def gather_over(n):
        here = g.at[arrays[n], own]
        chains[n, "x", 0] = send(here, here, gxs.at[n, 0], gxr.at[n, 0], seq=over)

    def over_wait(n, delta):
        towards = delta if n % 2 else -delta
        if delta == 0:
            at = 0
        elif abs(delta) == nr or towards > 0:
            at = abs(delta)
        else:
            at = nr + abs(delta)
        chains[n, "x", at].wait_recv()

    def gather(*what):
        for n, k in what:
            if k <= nr:
                gather_step(n, k)

    gather_over(2)
    gather_over(3)
    gather((0, 0), (1, 0), (2, 0), (3, 0))
    gather_over(0)
    gather_over(1)

    def put_video(n, which, row):
        for k in range(4):
            small[n, t_at, which * 4 + k : which * 4 + k + 1, :] = row[:, k * HD : (k + 1) * HD]

    for n in range(3):
        small[n, t_at] = jnp.zeros((16, HD), F32)
    both = jnp.concatenate([g[2, own, :].astype(F32), g[3, own, :].astype(F32)], axis=0)
    small[0, t_at, 8:9, :] = lanes_of(both * both)
    for n in range(2):
        loads[4 + n].wait()
        widened = raw_v[n].astype(F32)
        put_video(0, n, lanes_of(widened * widened))
    exch = tower_start(0)
    gather((4, 0), (5, 0), (0, 1), (1, 1))
    sloc[...] = jnp.zeros_like(sloc)
    sres[...] = jnp.zeros_like(sres)
    ub[...] = jnp.zeros_like(ub)
    gbuf[s_at] = jnp.zeros((8, WIDTH), F32)
    rho = lax.broadcasted_iota(jnp.int32, (arows, HD), 0)
    token = ((rho // 64) % 2) * (n_z * 64) + (rho // 128) * 64 + rho % 64
    bias_a[...] = jnp.where(token < alen[0], 0.0, MASKED)
    vtok = s_at * VROWS + lax.broadcasted_iota(jnp.int32, (VROWS, HD), 0)
    bias_v[...] = jnp.where(vtok < vlen[0], 0.0, MASKED)
    for n in (6, 7):
        loads[n].wait()

    everyone = [(delta, k) for delta in range(n_z) for k in range(2) if delta or k]
    fsent = {}

    def factors_out(row):
        fbuf[s_at] = jnp.broadcast_to(row, (8, HD))
        for delta, k in everyone:
            to = seq_id(1 - x if k else x, z + delta)
            at = 2 * delta + k
            fsent[delta, k] = send(fbuf.at[s_at], fbuf.at[s_at], fs.at[at], fr.at[at], seq=to)

    def factors_in(delta):
        for k in range(2):
            if delta or k:
                fsent[-delta % n_z, k].wait_recv()

    def pair_factors(at, n):
        half = slice(n * 64, n * 64 + 64)
        return jnp.concatenate([column_of(fbuf[seq_id(xx, at), 0:1, :])[half] for xx in range(2)], axis=0)

    stat1 = []

    def audio_first(*deltas):
        for delta in deltas:
            over_wait(0, delta)
            over_wait(1, delta)
            factors_in(delta)
        for delta in deltas:
            at = ring(z + delta)
            rows = aligned(at * 128, 128, 128)
            col = pair_factors(at, 0)
            for h in range(HEADS):
                cols = head_cols(h)
                query = (g[2, rows, cols].astype(F32) * col * (gains[2:3, cols] * c)).astype(BF16)
                gqn[rows, cols] = query
                s = mm(kn[:, cols], query, NT) + bias_v[...]
                m = jnp.maximum(jnp.max(s, axis=0, keepdims=True), FLOOR)
                p = jnp.exp2(s - m)
                dp = mm(raw_v[2, :, cols], g[0, rows, cols], NT)
                pb[h, :, rows] = p.astype(BF16)
                dpb[h, :, rows] = dp
                sloc[at, h : h + 1, :] = m
                sloc[at, 3 + h : 4 + h, :] = jnp.sum(p, axis=0, keepdims=True)
                sloc[at, 6 + h : 7 + h, :] = jnp.sum(p * dp, axis=0, keepdims=True)
        for delta in deltas:
            at = ring(z + delta)
            slot = delta % n_z
            for k, xx in enumerate((x, 1 - x)):
                if delta == 0 and k == 0:
                    sin[s_at] = sloc[at]
                else:
                    n = 2 * slot + k
                    stat1.append(send(sloc.at[at], sin.at[s_at], s1s.at[n], s1r.at[n], seq=seq_id(xx, at)))

    def video_first(*deltas):
        for delta in deltas:
            at = ring(z + delta)
            rows = aligned(at * 128, 128, 128)
            col = pair_factors(at, 1)
            bias = wide(bias_a[rows, :], 4)
            for h in range(HEADS):
                cols = head_cols(h)
                key = (g[3, rows, cols].astype(F32) * col * gains[1:2, cols]).astype(BF16)
                gkn[rows, cols] = key
                s = mm(key, qn[:, cols], NT) + bias
                m = jnp.maximum(jnp.max(s, axis=0, keepdims=True), FLOOR)
                p = jnp.exp2(s - m)
                dp = mm(g[1, rows, cols], raw_v[3, :, cols], NT)
                pa[h, rows, :] = p.astype(BF16)
                dpa[h, rows, :] = dp
                ast[h, at, 0:1, :] = m
                ast[h, at, 1:2, :] = jnp.sum(p, axis=0, keepdims=True)
                ast[h, at, 2:3, :] = jnp.sum(p * dp, axis=0, keepdims=True)

    def factor_video(factors):
        for n in range(2):
            for k in range(4):
                rows = slice(k * HD, (k + 1) * HD)
                col = column_of(factors[n * 4 + k : n * 4 + k + 1, :])
                rbv[n, rows, :] = col
                for h in range(HEADS):
                    cols = head_cols(h)
                    gain = gains[3 * n : 3 * n + 1, cols] * (c if n == 0 else 1.0)
                    (qn, kn)[n][rows, cols] = (raw_v[n, rows, cols].astype(F32) * col * gain).astype(BF16)

    def both_ways(run, dist):
        if dist < nr or dist <= nl:
            run(-dist, dist)
        elif dist == nr:
            run(-dist)

    factors = lax.rsqrt(tower_sum(0, exch) / depth + EPS)
    factors_out(factors[8:9, :])
    gather((2, 1), (3, 1))
    rba[...] = column_of(factors[8:9, :])
    factor_video(factors)
    gather((4, 1), (5, 1), (0, 2), (1, 2))
    audio_first(0)
    gather((2, 2), (3, 2), (4, 2), (5, 2), (0, 3), (1, 3))
    both_ways(audio_first, 1)
    video_first(0)
    gather((2, 3), (3, 3), (0, 4), (1, 4), (4, 3), (5, 3))
    both_ways(video_first, 1)
    both_ways(audio_first, 2)
    both_ways(video_first, 2)
    both_ways(audio_first, 3)
    both_ways(audio_first, 4)
    gather((2, 4), (3, 4))
    both_ways(video_first, 3)

    for copy in stat1:
        copy.wait_recv()
    mx = sin[0, 0:3, :]
    for k in range(1, n_seq):
        mx = jnp.maximum(mx, sin[k, 0:3, :])
    tot = jnp.zeros((3, HD), F32)
    inn = jnp.zeros((3, HD), F32)
    for k in range(n_seq):
        f = jnp.exp2(sin[k, 0:3, :] - mx)
        tot = tot + sin[k, 3:6, :] * f
        inn = inn + sin[k, 6:9, :] * f
    sres[0:3, :] = mx + jnp.log2(tot)
    sres[3:6, :] = inn / tot
    stat2 = [send(sres, sall.at[z], s2s.at[k], s2r.at[k], seq=seq_id(x, z + k)) for k in range(1, n_z)]
    sall[z] = sres[...]
    gather((4, 4), (5, 4))
    both_ways(video_first, 4)

    def video_second(h):
        cols = head_cols(h)
        m = ast[h, 0, 0:1, :]
        for k in range(1, n_z):
            m = jnp.maximum(m, ast[h, k, 0:1, :])
        total = jnp.zeros((1, VROWS), F32)
        inner = jnp.zeros((1, VROWS), F32)
        for k in range(n_z):
            f = jnp.exp2(ast[h, k, 0:1, :] - m)
            acf[k, 0:1, :] = f
            total = total + f * ast[h, k, 1:2, :]
            inner = inner + f * ast[h, k, 2:3, :]
        inverse = 1.0 / total
        delta = inner * inverse

        for k in range(n_z):
            rows = slice(k * 128, (k + 1) * 128)
            w = pa[h, rows, :].astype(F32) * (acf[k, 0:1, :] * inverse)
            pa[h, rows, :] = w.astype(BF16)
            dsa[rows, :] = (w * (dpa[h, rows, :] - delta)).astype(BF16)
        low = pa[h]
        ds = dsa[...]
        dk = mm(ds, qn[:, cols], NN) * unscale
        part[h, :, 0:HD] = dk.astype(BF16)
        part[h, :, HD:] = mm(low, raw_v[3, :, cols], NN).astype(BF16)
        prod = dk * gkn[:, cols].astype(F32)
        gbuf[s_at, 1:2, cols] = jnp.sum(prod, axis=0, keepdims=True) / gains[1:2, cols]
        acc[0] = prod if h == 0 else acc[0] + prod
        vout[:, cols] = mm(g[1, :, cols], low, TN).T.astype(BF16)
        dvid[0, :, cols] = mm(gkn[:, cols], ds, TN).T * scale

    def audio_second(h):
        cols = head_cols(h)

        for k in range(n_z):
            lanes = slice(k * HD, (k + 1) * HD)
            coef = jnp.exp2(sloc[k, h : h + 1, :] - sall[k, h : h + 1, :])
            w = pb[h, :, lanes].astype(F32) * coef
            pb[h, :, lanes] = w.astype(BF16)
            dsb[:, lanes] = (w * (dpb[h, :, lanes] - sall[k, 3 + h : 4 + h, :])).astype(BF16)
        low = pb[h]
        ds = dsb[...]
        part[HEADS + h, :, 0:HD] = mm(raw_v[2, :, cols], low, TN).T.astype(BF16)
        dq = mm(kn[:, cols], ds, TN).T * scale
        part[HEADS + h, :, HD:] = dq.astype(BF16)
        prod = dq * gqn[:, cols].astype(F32) * (1.0 / c)
        gbuf[s_at, 2:3, cols] = jnp.sum(prod, axis=0, keepdims=True) / gains[2:3, cols]
        acc[1] = prod if h == 0 else acc[1] + prod
        dvid[1, :, cols] = mm(ds, gqn[:, cols], NN) * unscale
        vvg[:, cols] = mm(low, g[0, :, cols], NN).astype(BF16)

    over_first = (3, 4, 5)
    mirrored = (1, 3, 5)
    rchain = {}
    order = []
    for dist in range(nr, 0, -1):
        order.append(dist)
        if dist <= nl:
            order.append(-dist)
    order.append(0)

    def scatter_over(*units):
        for k in range(n_z):
            for u in units:
                delta = -order[k] if u in mirrored else order[k]
                at = ring(z + delta)
                rchain[u, "x", delta % n_z] = send(
                    part.at[u, aligned(at * 128 + (1 - x) * 64, 64, 64)], xin.at[u, at],
                    xi_s.at[u, k], xi_r.at[u, k], seq=over,
                )

    def scatter_step(*what):
        for u, k in what:
            early = u in over_first
            way = -1 if u in mirrored else 1
            size = 64 if early else 128
            ends = (right, left)[::way]
            for name, n, to, sign, base, land in (
                ("l", nr, ends[0], way, 0, rr), ("s", nl, ends[1], -way, nr, rl),
            ):
                if k >= n:
                    continue
                delta = sign * (n - k)
                at = ring(z + delta)
                rows = aligned(at * 128 + x * 64, 64, 64) if early else aligned(at * 128, 128, 128)
                if early or k > 0:
                    total = part[u, rows, :].astype(F32)
                    if early:
                        rchain[u, "x", delta % n_z].wait_recv()
                        total = total + xin[u, at].astype(F32)
                    if k > 0:
                        rchain[u, name, k - 1].wait_recv()
                        total = total + land[u, k - 1, 0:size, :].astype(F32)
                    part[u, rows, :] = total.astype(BF16)
                rchain[u, name, k] = send(
                    part.at[u, rows], land.at[u, k, 0:size], rs_s.at[u, base + k], rs_r.at[u, base + k], seq=to
                )

    def landed(u, total, size):
        rchain[u, "l", nr - 1].wait_recv()
        total = total + rr[u, nr - 1, 0:size, :].astype(F32)
        if nl > 0:
            rchain[u, "s", nl - 1].wait_recv()
            total = total + rl[u, nl - 1, 0:size, :].astype(F32)
        return total

    def scatter_cross(*units):
        for u in units:
            fin[u] = landed(u, part[u, aligned(z * 128, 128, 128), :].astype(F32), 128)
            xs[u] = fin[u, aligned((1 - x) * 64, 64, 64), :].astype(BF16)
            rchain[u, "k"] = send(xs.at[u], xr.at[u], rs_s.at[u, n_z - 1], rs_r.at[u, n_z - 1], seq=over)

    def scatter_end(u):
        if u in over_first:
            rchain[u, "x", 0].wait_recv()
            return landed(u, part[u, own, :].astype(F32) + xin[u, z].astype(F32), 64)
        rchain[u, "k"].wait_recv()
        return fin[u, aligned(x * 64, 64, 64), :] + xr[u].astype(F32)

    def steps(*what):
        scatter_step(*[(u, k) for u, k in what if k < nr])

    for h in range(HEADS):
        video_second(h)
        steps((h, 0))
    for copy in stat2:
        copy.wait_recv()
    audio_second(0)
    scatter_over(3)
    audio_second(1)
    audio_second(2)
    scatter_over(4, 5)
    steps((0, 1), (1, 1), (2, 1), (3, 0))

    for n, row in ((0, 0), (1, 3)):
        inner = dvid[n] * (qn, kn)[n][...].astype(F32) * (1.0 / c if n == 0 else 1.0)
        put_video(1, n, lanes_of(inner))
        gbuf[s_at, row : row + 1, :] = jnp.sum(inner, axis=0, keepdims=True) / gains[row : row + 1, :]
    exch = tower_start(1)
    for n in range(2):
        row = lanes_of(acc[n])
        for k in range(n_z):
            ub[k, n : n + 1, :] = row[:, k * HD : (k + 1) * HD]
    ucopies = []
    for k in range(1, n_seq):
        to = lax.rem(s_at + k, n_seq)
        ucopies.append(send(ub.at[lax.rem(to, n_z)], uin.at[s_at], us.at[k], ur.at[k], seq=to))
    uin[s_at] = ub[z]
    gcopies = [
        send(gbuf.at[s_at], gbuf.at[s_at], ggs.at[k], ggr.at[k], seq=lax.rem(s_at + k, n_seq))
        for k in range(1, n_seq)
    ]
    outs = []

    def write(src, dst):
        copy = pltpu.make_async_copy(src, dst, ost.at[len(outs)])
        copy.start()
        outs.append(copy)

    write(vout, vo_h)
    write(vvg, vvg_h)
    steps((0, 2), (1, 2), (2, 2), (3, 1), (4, 0), (5, 0))

    inner = tower_sum(1, exch) * (1.0 / depth)

    def video_grad(n):
        row = 3 * n
        for k in range(4):
            rows = slice(k * HD, (k + 1) * HD)
            col = column_of(inner[n * 4 + k : n * 4 + k + 1, :])
            r = rbv[n, rows, :]
            for h in range(HEADS):
                cols = head_cols(h)
                grad = r * gains[row : row + 1, cols] * dvid[n, rows, cols] - raw_v[n, rows, cols].astype(F32) * (r * r * col)
                (qn, kn)[n][rows, cols] = grad.astype(BF16)
        write((qn, kn)[n], (vqg_h, vkg_h)[n])

    video_grad(0)
    steps((0, 3), (1, 3), (2, 3), (3, 2), (4, 1), (5, 1))
    for copy in ucopies:
        copy.wait_recv()
    total = uin[0]
    for k in range(1, n_seq):
        total = total + uin[k]
    small[2, t_at, 0:8, :] = total
    uexch = tower_start(2)
    video_grad(1)
    steps((3, 3))
    scatter_cross(0, 1, 2)
    steps((4, 2), (5, 2))
    for copy in gcopies:
        copy.wait_recv()
    total = gbuf[0]
    for k in range(1, n_seq):
        total = total + gbuf[k]
    if n_dp > 1:
        dbuf[d_at] = total
        gcopy = send(dbuf.at[d_at], dbuf.at[d_at], ds_.at[0], dr_.at[0], dp=1 - d_at)
    steps((4, 3), (5, 3))
    uall = tower_sum(2, uexch) * (1.0 / depth)
    for n in range(2):
        ucol[n] = column_of(uall[n : n + 1, :])

    def audio_grad(n, h, total):
        cols = head_cols(h)
        r = rba[(1 - n) * 64 : (2 - n) * 64, :]
        col = ucol[n, aligned(x * 64, 64, 64), :]
        return (r * gains[n + 1 : n + 2, cols] * total - g[3 - n, own, cols].astype(F32) * (r * r * col)).astype(BF16)

    if n_dp > 1:
        gcopy.wait_recv()
        total = dbuf[0] + dbuf[1]
    gout[...] = total[0:4, :]
    write(gout, gg_h)
    for h in range(HEADS):
        both = scatter_end(h)
        outa[2, :, head_cols(h)] = audio_grad(0, h, both[:, 0:HD])
        outa[3, :, head_cols(h)] = both[:, HD:].astype(BF16)
    write(outa.at[2], akg_h)
    write(outa.at[3], avg_h)
    for h in range(HEADS):
        both = scatter_end(HEADS + h)
        outa[0, :, head_cols(h)] = both[:, 0:HD].astype(BF16)
        outa[1, :, head_cols(h)] = audio_grad(1, h, both[:, HD:])
    write(outa.at[0], aco_h)
    write(outa.at[1], aqg_h)
    for copy in outs:
        copy.wait()
    for copy in pending:
        copy.wait_send()


def hand_over(*refs):
    count = (len(refs) - 1) // 2
    sems = refs[-1]
    copies = [pltpu.make_async_copy(refs[n], refs[count + n], sems.at[n]) for n in range(count)]
    for copy in copies:
        copy.start()
    for copy in copies:
        copy.wait()


def solution(mesh):
    sizes = tuple(mesh.shape[name] for name in ("tower", "seq", "dp"))
    n_tower, n_seq, n_dp = sizes
    n_z = n_seq // 2
    arows = n_seq * 64
    nr = n_z // 2
    nl = max(n_z - 1 - nr, 1)
    any_spec = pl.BlockSpec(memory_space=pl.ANY)
    vmem = pl.BlockSpec(memory_space=pltpu.VMEM)
    smem = pl.BlockSpec(memory_space=pltpu.SMEM)
    dma = lambda *shape: pltpu.SemaphoreType.DMA(shape)
    low = lambda *shape: pltpu.VMEM(shape, BF16)
    full = lambda *shape: pltpu.VMEM(shape, F32)

    def body(vq, ak, av, aq, vk, vv, up, ao, gains, vlen, alen):
        video = jax.ShapeDtypeStruct((VROWS, WIDTH), BF16)
        audio = jax.ShapeDtypeStruct((64, WIDTH), BF16)
        shapes = (video, audio, video, audio, audio, audio, video, video, jax.ShapeDtypeStruct((4, WIDTH), F32))
        results = pl.pallas_call(
            functools.partial(kernel, sizes),
            out_shape=shapes,
            in_specs=[any_spec] * 8 + [vmem, smem, smem],
            out_specs=tuple([any_spec] * 9),
            scratch_shapes=[
                low(4, arows, WIDTH),
                low(4, VROWS, WIDTH),
                low(arows, WIDTH),
                low(arows, WIDTH),
                low(VROWS, WIDTH),
                low(VROWS, WIDTH),
                full(2, VROWS, WIDTH),
                low(VROWS, WIDTH),
                low(VROWS, WIDTH),
                low(6, arows, 256),
                low(6, nr, 128, 256),
                low(6, nl, 128, 256),
                low(6, n_z, 64, 256),
                low(6, 64, 256),
                low(6, 64, 256),
                full(6, 128, 256),
                low(HEADS, arows, VROWS),
                full(HEADS, arows, VROWS),
                low(arows, VROWS),
                full(HEADS, n_z, 8, VROWS),
                full(n_z, 8, VROWS),
                low(HEADS, VROWS, arows),
                full(HEADS, VROWS, arows),
                low(VROWS, arows),
                full(2, arows, HD),
                full(arows, HD),
                full(VROWS, HD),
                full(2, VROWS, HD),
                full(128, HD),
                full(3, n_tower, 16, HD),
                full(n_seq, 8, HD),
                full(n_z, 16, HD),
                full(n_seq, 16, HD),
                full(8, HD),
                full(n_z, 8, HD),
                full(n_z, 8, HD),
                full(n_seq, 8, HD),
                full(2, 128, HD),
                full(n_seq, 8, WIDTH),
                full(2, 8, WIDTH),
                full(4, WIDTH),
                low(4, 64, WIDTH),
                dma(8), dma(6, n_z), dma(6, n_z), dma(4, n_z), dma(4, n_z), dma(3, n_tower), dma(3, n_tower),
                dma(n_seq), dma(n_seq), dma(n_seq), dma(n_seq), dma(n_z), dma(n_z), dma(n_seq), dma(n_seq),
                dma(n_seq), dma(n_seq), dma(1), dma(1), dma(6, n_z), dma(6, n_z), dma(6, n_z), dma(6, n_z), dma(9),
            ],
            compiler_params=pltpu.CompilerParams(
                collective_id=0, has_side_effects=True, vmem_limit_bytes=58 * 1024 * 1024
            ),
            cost_estimate=pl.CostEstimate(flops=4_800_000_000, bytes_accessed=4_000_000, transcendentals=3_200_000),
        )(vq[0], ak[0], av[0], aq[0], vk[0], vv[0], up[0], ao[0], gains, vlen, alen)
        results = pl.pallas_call(
            hand_over,
            out_shape=shapes,
            in_specs=[vmem] * 9,
            out_specs=tuple([any_spec] * 9),
            scratch_shapes=[dma(9)],
        )(*results)
        return tuple(r[None] for r in results[:8]) + (results[8],)

    spec = P("dp", "seq", "tower")
    return jax.shard_map(
        body,
        mesh=mesh,
        in_specs=(spec,) * 8 + (P(None, "tower"), P("dp"), P("dp")),
        out_specs=(spec,) * 8 + (P(None, "tower"),),
        check_vma=False,
    )
```

```python
import functools
import math

import jax
import jax.numpy as jnp
from jax import lax
from jax.experimental import pallas as pl
from jax.experimental.pallas import tpu as pltpu
from jax.sharding import PartitionSpec as P

HD = 128
HEADS = 3
WIDTH = HEADS * HD
VROWS = 512
EPS = 1e-06
MASKED = -1e30
FLOOR = -1e29
F32 = jnp.float32
BF16 = jnp.bfloat16
MESH = pl.DeviceIdType.MESH

NT = (((1,), (1,)), ((), ()))
NN = (((1,), (0,)), ((), ()))
TN = (((0,), (0,)), ((), ()))


def mm(a, b, dims):
    return lax.dot_general(a, b, dims, preferred_element_type=F32)


def aligned(start, size, unit):
    return pl.ds(pl.multiple_of(start, unit), size)


def lanes_of(products):
    part = products[:, 0:HD]
    for k in range(1, products.shape[1] // HD):
        part = part + products[:, k * HD : (k + 1) * HD]
    return jnp.sum(part.T, axis=0, keepdims=True)


def column_of(row):
    return jnp.broadcast_to(row, (HD, HD)).T


def head_cols(h):
    return slice(h * HD, (h + 1) * HD)


def wide(block, n):
    return jnp.concatenate([block] * n, axis=1)


def kernel(
    sizes,
    vq_h, ak_h, av_h, aq_h, vk_h, vv_h, up_h, ao_h, gains, vlen, alen,
    vo_h, aco_h, vqg_h, akg_h, avg_h, aqg_h, vkg_h, vvg_h, gg_h,
    g, raw_v, gqn, gkn, qn, kn, dvid, vout, vvg, part, rr, rl, xin, xs, xr, fin,
    pa, dpa, dsa, ast, acf, pb, dpb, dsb, acc, bias_a, bias_v, rbv, rba, small, fbuf,
    sloc, sin, sres, sall, ub, uin, ucol, gbuf, dbuf, gout, outa,
    ld, gs, gr, gxs, gxr, ts, tr, fs, fr, s1s, s1r, s2s, s2r, us, ur, ggs, ggr, ds_, dr_,
    rs_s, rs_r, xi_s, xi_r, ost,
):
    n_tower, n_seq, n_dp = sizes
    n_z = n_seq // 2
    nr = n_z // 2
    nl = n_z - 1 - nr
    arows = n_seq * 64
    depth = n_tower * WIDTH
    scale = 1.0 / math.sqrt(HD)
    c = scale * math.log2(math.e)
    unscale = scale / c

    t_at = lax.axis_index("tower")
    s_at = lax.axis_index("seq")
    d_at = lax.axis_index("dp")
    z = lax.rem(s_at, n_z)
    x = s_at // n_z

    def ring(zz):
        return lax.rem(zz + 2 * n_z, n_z)

    def seq_id(xx, zz):
        return xx * n_z + ring(zz)

    right, left, over = seq_id(x, z + 1), seq_id(x, z - 1), seq_id(1 - x, z)

    pending = []

    def send(src, dst, send_sem, recv_sem, **dev):
        copy = pltpu.make_async_remote_copy(
            src_ref=src, dst_ref=dst, send_sem=send_sem, recv_sem=recv_sem,
            device_id=dev, device_id_type=MESH,
        )
        copy.start()
        pending.append(copy)
        return copy

    own = aligned(z * 128 + x * 64, 64, 64)
    loads = []
    for n, (src, dst) in enumerate([
        (aq_h, g.at[2, own]),
        (ak_h, g.at[3, own]),
        (ao_h, g.at[0, own]),
        (av_h, g.at[1, own]),
        (vq_h, raw_v.at[0]),
        (vk_h, raw_v.at[1]),
        (vv_h, raw_v.at[2]),
        (up_h, raw_v.at[3]),
    ]):
        loads.append(pltpu.make_async_copy(src, dst, ld.at[n]))
        loads[n].start()
    barrier = pltpu.get_barrier_semaphore()
    peers = 0
    for k in range(1, n_seq):
        pl.semaphore_signal(barrier, inc=1, device_id={"seq": lax.rem(s_at + k, n_seq)}, device_id_type=MESH)
        peers += 1
    for k in range(1, n_tower):
        pl.semaphore_signal(barrier, inc=1, device_id={"tower": lax.rem(t_at + k, n_tower)}, device_id_type=MESH)
        peers += 1
    if n_dp > 1:
        pl.semaphore_signal(barrier, inc=1, device_id={"dp": 1 - d_at}, device_id_type=MESH)
        peers += 1

    for n in range(4):
        loads[n].wait()

    def put_video(n, which, row):
        for k in range(4):
            small[n, t_at, which * 4 + k : which * 4 + k + 1, :] = row[:, k * HD : (k + 1) * HD]

    for n in range(3):
        small[n, t_at] = jnp.zeros((16, HD), F32)
    both = jnp.concatenate([g[2, own, :].astype(F32), g[3, own, :].astype(F32)], axis=0)
    small[0, t_at, 8:9, :] = lanes_of(both * both)
    for n in range(2):
        loads[4 + n].wait()
        widened = raw_v[n].astype(F32)
        put_video(0, n, lanes_of(widened * widened))
    pl.semaphore_wait(barrier, peers)

    def tower_start(n):
        return [
            send(small.at[n, t_at], small.at[n, t_at], ts.at[n, k], tr.at[n, k], tower=lax.rem(t_at + k, n_tower))
            for k in range(1, n_tower)
        ]

    def tower_sum(n, copies):
        for copy in copies:
            copy.wait_recv()
        total = small[n, 0]
        for k in range(1, n_tower):
            total = total + small[n, k]
        return total

    arrays = (0, 2, 1, 3, 1, 3)
    chains = {}

    def gather_step(n, k):
        a = arrays[n]
        sign = 1 if n % 2 else -1
        ways = (("l", nr, left if n % 2 else right, sign, 0), ("s", nl, right if n % 2 else left, -sign, nr))
        half = 1 - x if n >= 4 else x

        def block(zz):
            return g.at[a, aligned(ring(zz) * 128 + half * 64, 64, 64)]

        if k == 0 and n >= 4:
            chains[n - 2, "x", 0].wait_recv()
        for name, count, to, way, base in ways:
            if k > count:
                continue
            here = block(z + way * k)
            if k > 0:
                chains[n, name, k].wait_recv()
            if k < count:
                chains[n, name, k + 1] = send(here, here, gs.at[n, base + k], gr.at[n, base + k], seq=to)
            if k > 0 and n < 2:
                chains[n, "x", base + k] = send(here, here, gxs.at[n, base + k], gxr.at[n, base + k], seq=over)

    def gather_over(n):
        here = g.at[arrays[n], own]
        chains[n, "x", 0] = send(here, here, gxs.at[n, 0], gxr.at[n, 0], seq=over)

    def over_wait(n, delta):
        towards = delta if n % 2 else -delta
        if delta == 0:
            at = 0
        elif abs(delta) == nr or towards > 0:
            at = abs(delta)
        else:
            at = nr + abs(delta)
        chains[n, "x", at].wait_recv()

    def gather(*what):
        for n, k in what:
            if k <= nr:
                gather_step(n, k)

    exch = tower_start(0)
    gather_over(2)
    gather_over(3)
    gather((0, 0), (1, 0), (2, 0), (3, 0))
    gather_over(0)
    gather_over(1)

    gather((4, 0), (5, 0), (0, 1), (1, 1))
    sloc[...] = jnp.zeros_like(sloc)
    sres[...] = jnp.zeros_like(sres)
    ub[...] = jnp.zeros_like(ub)
    gbuf[s_at] = jnp.zeros((8, WIDTH), F32)
    rho = lax.broadcasted_iota(jnp.int32, (arows, HD), 0)
    token = ((rho // 64) % 2) * (n_z * 64) + (rho // 128) * 64 + rho % 64
    bias_a[...] = jnp.where(token < alen[0], 0.0, MASKED)
    vtok = s_at * VROWS + lax.broadcasted_iota(jnp.int32, (VROWS, HD), 0)
    bias_v[...] = jnp.where(vtok < vlen[0], 0.0, MASKED)
    for n in (6, 7):
        loads[n].wait()

    everyone = [(delta, k) for delta in range(n_z) for k in range(2) if delta or k]
    fsent = {}

    def factors_out(row):
        fbuf[s_at] = jnp.broadcast_to(row, (8, HD))
        for delta, k in everyone:
            to = seq_id(1 - x if k else x, z + delta)
            at = 2 * delta + k
            fsent[delta, k] = send(fbuf.at[s_at], fbuf.at[s_at], fs.at[at], fr.at[at], seq=to)

    def factors_in(delta):
        for k in range(2):
            if delta or k:
                fsent[-delta % n_z, k].wait_recv()

    def pair_factors(at, n):
        half = slice(n * 64, n * 64 + 64)
        return jnp.concatenate([column_of(fbuf[seq_id(xx, at), 0:1, :])[half] for xx in range(2)], axis=0)

    stat1 = []

    def audio_first(*deltas):
        for delta in deltas:
            over_wait(0, delta)
            over_wait(1, delta)
            factors_in(delta)
        for delta in deltas:
            at = ring(z + delta)
            rows = aligned(at * 128, 128, 128)
            col = pair_factors(at, 0)
            for h in range(HEADS):
                cols = head_cols(h)
                query = (g[2, rows, cols].astype(F32) * col * (gains[2:3, cols] * c)).astype(BF16)
                gqn[rows, cols] = query
                s = mm(kn[:, cols], query, NT) + bias_v[...]
                m = jnp.maximum(jnp.max(s, axis=0, keepdims=True), FLOOR)
                p = jnp.exp2(s - m)
                dp = mm(raw_v[2, :, cols], g[0, rows, cols], NT)
                pb[h, :, rows] = p.astype(BF16)
                dpb[h, :, rows] = dp
                sloc[at, h : h + 1, :] = m
                sloc[at, 3 + h : 4 + h, :] = jnp.sum(p, axis=0, keepdims=True)
                sloc[at, 6 + h : 7 + h, :] = jnp.sum(p * dp, axis=0, keepdims=True)
        for delta in deltas:
            at = ring(z + delta)
            slot = delta % n_z
            for k, xx in enumerate((x, 1 - x)):
                if delta == 0 and k == 0:
                    sin[s_at] = sloc[at]
                else:
                    n = 2 * slot + k
                    stat1.append(send(sloc.at[at], sin.at[s_at], s1s.at[n], s1r.at[n], seq=seq_id(xx, at)))

    def video_first(*deltas):
        for delta in deltas:
            at = ring(z + delta)
            rows = aligned(at * 128, 128, 128)
            col = pair_factors(at, 1)
            bias = wide(bias_a[rows, :], 4)
            for h in range(HEADS):
                cols = head_cols(h)
                key = (g[3, rows, cols].astype(F32) * col * gains[1:2, cols]).astype(BF16)
                gkn[rows, cols] = key
                s = mm(key, qn[:, cols], NT) + bias
                m = jnp.maximum(jnp.max(s, axis=0, keepdims=True), FLOOR)
                p = jnp.exp2(s - m)
                dp = mm(g[1, rows, cols], raw_v[3, :, cols], NT)
                pa[h, rows, :] = p.astype(BF16)
                dpa[h, rows, :] = dp
                ast[h, at, 0:1, :] = m
                ast[h, at, 1:2, :] = jnp.sum(p, axis=0, keepdims=True)
                ast[h, at, 2:3, :] = jnp.sum(p * dp, axis=0, keepdims=True)

    def factor_video(factors):
        for n in range(2):
            for k in range(4):
                rows = slice(k * HD, (k + 1) * HD)
                col = column_of(factors[n * 4 + k : n * 4 + k + 1, :])
                rbv[n, rows, :] = col
                for h in range(HEADS):
                    cols = head_cols(h)
                    gain = gains[3 * n : 3 * n + 1, cols] * (c if n == 0 else 1.0)
                    (qn, kn)[n][rows, cols] = (raw_v[n, rows, cols].astype(F32) * col * gain).astype(BF16)

    def both_ways(run, dist):
        if dist < nr or dist <= nl:
            run(-dist, dist)
        elif dist == nr:
            run(-dist)

    factors = lax.rsqrt(tower_sum(0, exch) / depth + EPS)
    factors_out(factors[8:9, :])
    gather((2, 1), (3, 1))
    rba[...] = column_of(factors[8:9, :])
    factor_video(factors)
    gather((4, 1), (5, 1), (0, 2), (1, 2), (2, 2), (3, 2))
    audio_first(0)
    gather((4, 2), (5, 2), (0, 3), (1, 3))
    both_ways(audio_first, 1)
    video_first(0)
    gather((2, 3), (3, 3), (0, 4), (1, 4), (4, 3), (5, 3))
    both_ways(video_first, 1)
    both_ways(audio_first, 2)
    both_ways(video_first, 2)
    both_ways(audio_first, 3)
    both_ways(audio_first, 4)
    gather((2, 4), (3, 4))
    both_ways(video_first, 3)

    gather((4, 4), (5, 4))
    both_ways(video_first, 4)

    def video_second(h):
        cols = head_cols(h)
        m = ast[h, 0, 0:1, :]
        for k in range(1, n_z):
            m = jnp.maximum(m, ast[h, k, 0:1, :])
        total = jnp.zeros((1, VROWS), F32)
        inner = jnp.zeros((1, VROWS), F32)
        for k in range(n_z):
            f = jnp.exp2(ast[h, k, 0:1, :] - m)
            acf[k, 0:1, :] = f
            total = total + f * ast[h, k, 1:2, :]
            inner = inner + f * ast[h, k, 2:3, :]
        inverse = 1.0 / total
        delta = inner * inverse

        for k in range(n_z):
            rows = slice(k * 128, (k + 1) * 128)
            w = pa[h, rows, :].astype(F32) * (acf[k, 0:1, :] * inverse)
            pa[h, rows, :] = w.astype(BF16)
            dsa[rows, :] = (w * (dpa[h, rows, :] - delta)).astype(BF16)
        low = pa[h]
        ds = dsa[...]
        dk = mm(ds, qn[:, cols], NN) * unscale
        part[h, :, 0:HD] = dk.astype(BF16)
        part[h, :, HD:] = mm(low, raw_v[3, :, cols], NN).astype(BF16)
        prod = dk * gkn[:, cols].astype(F32)
        gbuf[s_at, 1:2, cols] = jnp.sum(prod, axis=0, keepdims=True) / gains[1:2, cols]
        acc[0] = prod if h == 0 else acc[0] + prod
        vout[:, cols] = mm(g[1, :, cols], low, TN).T.astype(BF16)
        dvid[0, :, cols] = mm(gkn[:, cols], ds, TN).T * scale

    def audio_second(h):
        cols = head_cols(h)

        for k in range(n_z):
            lanes = slice(k * HD, (k + 1) * HD)
            coef = jnp.exp2(sloc[k, h : h + 1, :] - sall[k, h : h + 1, :])
            w = pb[h, :, lanes].astype(F32) * coef
            pb[h, :, lanes] = w.astype(BF16)
            dsb[:, lanes] = (w * (dpb[h, :, lanes] - sall[k, 3 + h : 4 + h, :])).astype(BF16)
        low = pb[h]
        ds = dsb[...]
        part[HEADS + h, :, 0:HD] = mm(raw_v[2, :, cols], low, TN).T.astype(BF16)
        dq = mm(kn[:, cols], ds, TN).T * scale
        part[HEADS + h, :, HD:] = dq.astype(BF16)
        prod = dq * gqn[:, cols].astype(F32) * (1.0 / c)
        gbuf[s_at, 2:3, cols] = jnp.sum(prod, axis=0, keepdims=True) / gains[2:3, cols]
        acc[1] = prod if h == 0 else acc[1] + prod
        dvid[1, :, cols] = mm(ds, gqn[:, cols], NN) * unscale
        vvg[:, cols] = mm(low, g[0, :, cols], NN).astype(BF16)

    over_first = (0, 1, 5)
    mirrored = (0, 3, 5)
    rchain = {}
    order = []
    for dist in range(nr, 0, -1):
        order.append(dist)
        if dist <= nl:
            order.append(-dist)
    order.append(0)

    def scatter_over(*units):
        for k in range(n_z):
            for u in units:
                delta = -order[k] if u in mirrored else order[k]
                at = ring(z + delta)
                rchain[u, "x", delta % n_z] = send(
                    part.at[u, aligned(at * 128 + (1 - x) * 64, 64, 64)], xin.at[u, at],
                    xi_s.at[u, k], xi_r.at[u, k], seq=over,
                )

    def scatter_step(*what):
        for u, k in what:
            early = u in over_first
            way = -1 if u in mirrored else 1
            size = 64 if early else 128
            ends = (right, left)[::way]
            for name, n, to, sign, base, land in (
                ("l", nr, ends[0], way, 0, rr), ("s", nl, ends[1], -way, nr, rl),
            ):
                if k >= n:
                    continue
                delta = sign * (n - k)
                at = ring(z + delta)
                rows = aligned(at * 128 + x * 64, 64, 64) if early else aligned(at * 128, 128, 128)
                if early or k > 0:
                    total = part[u, rows, :].astype(F32)
                    if early:
                        rchain[u, "x", delta % n_z].wait_recv()
                        total = total + xin[u, at].astype(F32)
                    if k > 0:
                        rchain[u, name, k - 1].wait_recv()
                        total = total + land[u, k - 1, 0:size, :].astype(F32)
                    part[u, rows, :] = total.astype(BF16)
                rchain[u, name, k] = send(
                    part.at[u, rows], land.at[u, k, 0:size], rs_s.at[u, base + k], rs_r.at[u, base + k], seq=to
                )

    def landed(u, total, size):
        rchain[u, "l", nr - 1].wait_recv()
        total = total + rr[u, nr - 1, 0:size, :].astype(F32)
        if nl > 0:
            rchain[u, "s", nl - 1].wait_recv()
            total = total + rl[u, nl - 1, 0:size, :].astype(F32)
        return total

    def scatter_cross(*units):
        for u in units:
            fin[u] = landed(u, part[u, aligned(z * 128, 128, 128), :].astype(F32), 128)
            xs[u] = fin[u, aligned((1 - x) * 64, 64, 64), :].astype(BF16)
            rchain[u, "k"] = send(xs.at[u], xr.at[u], rs_s.at[u, n_z - 1], rs_r.at[u, n_z - 1], seq=over)

    def scatter_end(u):
        if u in over_first:
            rchain[u, "x", 0].wait_recv()
            return landed(u, part[u, own, :].astype(F32) + xin[u, z].astype(F32), 64)
        rchain[u, "k"].wait_recv()
        return fin[u, aligned(x * 64, 64, 64), :] + xr[u].astype(F32)

    def steps(*what):
        scatter_step(*[(u, k) for u, k in what if k < nr])

    video_second(0)
    scatter_over(0)
    video_second(1)
    scatter_over(1)
    video_second(2)
    steps((2, 0))

    for copy in stat1:
        copy.wait_recv()
    mx = sin[0, 0:3, :]
    for k in range(1, n_seq):
        mx = jnp.maximum(mx, sin[k, 0:3, :])
    tot = jnp.zeros((3, HD), F32)
    inn = jnp.zeros((3, HD), F32)
    for k in range(n_seq):
        f = jnp.exp2(sin[k, 0:3, :] - mx)
        tot = tot + sin[k, 3:6, :] * f
        inn = inn + sin[k, 6:9, :] * f
    sres[0:3, :] = mx + jnp.log2(tot)
    sres[3:6, :] = inn / tot
    stat2 = [send(sres, sall.at[z], s2s.at[k], s2r.at[k], seq=seq_id(x, z + k)) for k in range(1, n_z)]
    sall[z] = sres[...]
    steps((0, 0), (1, 0))
    for copy in stat2:
        copy.wait_recv()
    audio_second(0)
    steps((3, 0))
    audio_second(1)
    steps((4, 0))
    audio_second(2)
    scatter_over(5)
    steps((2, 1), (0, 1), (1, 1))

    for n, row in ((0, 0), (1, 3)):
        inner = dvid[n] * (qn, kn)[n][...].astype(F32) * (1.0 / c if n == 0 else 1.0)
        put_video(1, n, lanes_of(inner))
        gbuf[s_at, row : row + 1, :] = jnp.sum(inner, axis=0, keepdims=True) / gains[row : row + 1, :]
    exch = tower_start(1)
    for n in range(2):
        row = lanes_of(acc[n])
        for k in range(n_z):
            ub[k, n : n + 1, :] = row[:, k * HD : (k + 1) * HD]
    ucopies = []
    for k in range(1, n_seq):
        to = lax.rem(s_at + k, n_seq)
        ucopies.append(send(ub.at[lax.rem(to, n_z)], uin.at[s_at], us.at[k], ur.at[k], seq=to))
    uin[s_at] = ub[z]
    gcopies = [
        send(gbuf.at[s_at], gbuf.at[s_at], ggs.at[k], ggr.at[k], seq=lax.rem(s_at + k, n_seq))
        for k in range(1, n_seq)
    ]
    outs = []

    def write(src, dst):
        copy = pltpu.make_async_copy(src, dst, ost.at[len(outs)])
        copy.start()
        outs.append(copy)

    write(vout, vo_h)
    write(vvg, vvg_h)
    steps((3, 1), (4, 1), (2, 2), (0, 2), (1, 2), (5, 0))
    steps((2, 3), (3, 2), (4, 2), (0, 3), (1, 3), (5, 1))
    scatter_cross(2)
    for copy in ucopies:
        copy.wait_recv()
    total = uin[0]
    for k in range(1, n_seq):
        total = total + uin[k]
    small[2, t_at, 0:8, :] = total
    uexch = tower_start(2)
    inner = tower_sum(1, exch) * (1.0 / depth)

    def video_grad(n):
        row = 3 * n
        for k in range(4):
            rows = slice(k * HD, (k + 1) * HD)
            col = column_of(inner[n * 4 + k : n * 4 + k + 1, :])
            r = rbv[n, rows, :]
            for h in range(HEADS):
                cols = head_cols(h)
                grad = r * gains[row : row + 1, cols] * dvid[n, rows, cols] - raw_v[n, rows, cols].astype(F32) * (r * r * col)
                (qn, kn)[n][rows, cols] = grad.astype(BF16)
        write((qn, kn)[n], (vqg_h, vkg_h)[n])

    video_grad(0)
    steps((3, 3), (4, 3), (5, 2))
    for copy in gcopies:
        copy.wait_recv()
    total = gbuf[0]
    for k in range(1, n_seq):
        total = total + gbuf[k]
    if n_dp > 1:
        dbuf[d_at] = total
        gcopy = send(dbuf.at[d_at], dbuf.at[d_at], ds_.at[0], dr_.at[0], dp=1 - d_at)
    video_grad(1)
    steps((5, 3))
    scatter_cross(3, 4)
    uall = tower_sum(2, uexch) * (1.0 / depth)
    for n in range(2):
        ucol[n] = column_of(uall[n : n + 1, :])

    def audio_grad(n, h, total):
        cols = head_cols(h)
        r = rba[(1 - n) * 64 : (2 - n) * 64, :]
        col = ucol[n, aligned(x * 64, 64, 64), :]
        return (r * gains[n + 1 : n + 2, cols] * total - g[3 - n, own, cols].astype(F32) * (r * r * col)).astype(BF16)

    if n_dp > 1:
        gcopy.wait_recv()
        total = dbuf[0] + dbuf[1]
    gout[...] = total[0:4, :]
    write(gout, gg_h)
    for h in range(HEADS):
        both = scatter_end(h)
        outa[2, :, head_cols(h)] = audio_grad(0, h, both[:, 0:HD])
        outa[3, :, head_cols(h)] = both[:, HD:].astype(BF16)
    write(outa.at[2], akg_h)
    write(outa.at[3], avg_h)
    for h in range(HEADS):
        both = scatter_end(HEADS + h)
        outa[0, :, head_cols(h)] = both[:, 0:HD].astype(BF16)
        outa[1, :, head_cols(h)] = audio_grad(1, h, both[:, HD:])
    write(outa.at[0], aco_h)
    write(outa.at[1], aqg_h)
    for copy in outs:
        copy.wait()
    for copy in pending:
        copy.wait_send()


def hand_over(*refs):
    count = len(refs) // 3
    sems = refs[-1]
    ins = [pltpu.make_async_copy(refs[n], refs[2 * count + n], sems.at[0, n]) for n in range(count)]
    outs = [pltpu.make_async_copy(refs[2 * count + n], refs[count + n], sems.at[1, n]) for n in range(count)]
    for copy in ins:
        copy.start()
    for n in range(count):
        ins[n].wait()
        outs[n].start()
    for copy in outs:
        copy.wait()


def solution(mesh):
    sizes = tuple(mesh.shape[name] for name in ("tower", "seq", "dp"))
    n_tower, n_seq, n_dp = sizes
    n_z = n_seq // 2
    arows = n_seq * 64
    nr = n_z // 2
    nl = max(n_z - 1 - nr, 1)
    any_spec = pl.BlockSpec(memory_space=pl.ANY)
    vmem = pl.BlockSpec(memory_space=pltpu.VMEM)
    smem = pl.BlockSpec(memory_space=pltpu.SMEM)
    dma = lambda *shape: pltpu.SemaphoreType.DMA(shape)
    low = lambda *shape: pltpu.VMEM(shape, BF16)
    full = lambda *shape: pltpu.VMEM(shape, F32)

    def body(vq, ak, av, aq, vk, vv, up, ao, gains, vlen, alen):
        video = jax.ShapeDtypeStruct((VROWS, WIDTH), BF16)
        audio = jax.ShapeDtypeStruct((64, WIDTH), BF16)
        shapes = (video, audio, video, audio, audio, audio, video, video, jax.ShapeDtypeStruct((4, WIDTH), F32))
        results = pl.pallas_call(
            functools.partial(kernel, sizes),
            out_shape=shapes,
            in_specs=[any_spec] * 8 + [vmem, smem, smem],
            out_specs=tuple([any_spec] * 9),
            scratch_shapes=[
                low(4, arows, WIDTH),
                low(4, VROWS, WIDTH),
                low(arows, WIDTH),
                low(arows, WIDTH),
                low(VROWS, WIDTH),
                low(VROWS, WIDTH),
                full(2, VROWS, WIDTH),
                low(VROWS, WIDTH),
                low(VROWS, WIDTH),
                low(6, arows, 256),
                low(6, nr, 128, 256),
                low(6, nl, 128, 256),
                low(6, n_z, 64, 256),
                low(6, 64, 256),
                low(6, 64, 256),
                full(6, 128, 256),
                low(HEADS, arows, VROWS),
                full(HEADS, arows, VROWS),
                low(arows, VROWS),
                full(HEADS, n_z, 8, VROWS),
                full(n_z, 8, VROWS),
                low(HEADS, VROWS, arows),
                full(HEADS, VROWS, arows),
                low(VROWS, arows),
                full(2, arows, HD),
                full(arows, HD),
                full(VROWS, HD),
                full(2, VROWS, HD),
                full(128, HD),
                full(3, n_tower, 16, HD),
                full(n_seq, 8, HD),
                full(n_z, 16, HD),
                full(n_seq, 16, HD),
                full(8, HD),
                full(n_z, 8, HD),
                full(n_z, 8, HD),
                full(n_seq, 8, HD),
                full(2, 128, HD),
                full(n_seq, 8, WIDTH),
                full(2, 8, WIDTH),
                full(4, WIDTH),
                low(4, 64, WIDTH),
                dma(8), dma(6, n_z), dma(6, n_z), dma(4, n_z), dma(4, n_z), dma(3, n_tower), dma(3, n_tower),
                dma(n_seq), dma(n_seq), dma(n_seq), dma(n_seq), dma(n_z), dma(n_z), dma(n_seq), dma(n_seq),
                dma(n_seq), dma(n_seq), dma(1), dma(1), dma(6, n_z), dma(6, n_z), dma(6, n_z), dma(6, n_z), dma(9),
            ],
            compiler_params=pltpu.CompilerParams(
                collective_id=0, has_side_effects=True, vmem_limit_bytes=58 * 1024 * 1024
            ),
            cost_estimate=pl.CostEstimate(flops=4_800_000_000, bytes_accessed=4_000_000, transcendentals=3_200_000),
        )(vq[0], ak[0], av[0], aq[0], vk[0], vv[0], up[0], ao[0], gains, vlen, alen)
        results = pl.pallas_call(
            hand_over,
            out_shape=shapes,
            in_specs=[any_spec] * 9,
            out_specs=tuple([any_spec] * 9),
            scratch_shapes=[pltpu.VMEM(s.shape, s.dtype) for s in shapes] + [dma(2, 9)],
        )(*results)
        return tuple(r[None] for r in results[:8]) + (results[8],)

    spec = P("dp", "seq", "tower")
    return jax.shard_map(
        body,
        mesh=mesh,
        in_specs=(spec,) * 8 + (P(None, "tower"), P("dp"), P("dp")),
        out_specs=(spec,) * 8 + (P(None, "tower"),),
        check_vma=False,
    )
```

```python
import functools
import math

import jax
import jax.numpy as jnp
from jax import lax
from jax.experimental import pallas as pl
from jax.experimental.pallas import tpu as pltpu
from jax.sharding import PartitionSpec as P

HD = 128
HEADS = 3
WIDTH = HEADS * HD
VROWS = 512
EPS = 1e-06
MASKED = -1e30
FLOOR = -1e29
F32 = jnp.float32
BF16 = jnp.bfloat16
MESH = pl.DeviceIdType.MESH

NT = (((1,), (1,)), ((), ()))
NN = (((1,), (0,)), ((), ()))
TN = (((0,), (0,)), ((), ()))


def mm(a, b, dims):
    return lax.dot_general(a, b, dims, preferred_element_type=F32)


def aligned(start, size, unit):
    return pl.ds(pl.multiple_of(start, unit), size)


def lanes_of(products):
    part = products[:, 0:HD]
    for k in range(1, products.shape[1] // HD):
        part = part + products[:, k * HD : (k + 1) * HD]
    return jnp.sum(part.T, axis=0, keepdims=True)


def column_of(row):
    return jnp.broadcast_to(row, (HD, HD)).T


def head_cols(h):
    return slice(h * HD, (h + 1) * HD)


def wide(block, n):
    return jnp.concatenate([block] * n, axis=1)


EVENTS = (
    ("masks",), ("g", 0, 1, "l"), ("g", 0, 1, "s"), ("g", 1, 1, "s"), ("g", 1, 1, "l"), ("tower",),
    ("g", 2, 1, "l"), ("g", 2, 1, "s"), ("vid",), ("g", 3, 1, "l"), ("g", 0, 2, "l"), ("g", 3, 1, "s"),
    ("g", 0, 2, "s"), ("g", 1, 2, "s"), ("g", 1, 2, "l"), ("g0", 4), ("g0", 5), ("B1", 0), ("g", 2, 2, "l"),
    ("g", 2, 2, "s"), ("B1", -1), ("g", 3, 2, "l"), ("g", 0, 3, "l"), ("B1", 1), ("A1", 0), ("g", 3, 2, "s"),
    ("g", 0, 3, "s"), ("g", 1, 3, "l"), ("g", 1, 3, "s"), ("g", 4, 1, "s"), ("g", 4, 1, "l"), ("B1", -2),
    ("g", 5, 1, "l"), ("g", 5, 1, "s"), ("B1", 2), ("A1", -1), ("g", 2, 3, "l"), ("g", 2, 3, "s"), ("A1", 1),
    ("g", 3, 3, "l"), ("g", 0, 4, "l"), ("g", 1, 4, "l"), ("g", 3, 3, "s"), ("B1", 3), ("g", 4, 2, "s"),
    ("g", 4, 2, "l"), ("B1", -3), ("g", 5, 2, "l"), ("g", 5, 2, "s"), ("A1", -2), ("A1", 2), ("g", 2, 4, "l"),
    ("g", 3, 4, "l"), ("B1", -4), ("g", 4, 3, "s"), ("g", 4, 3, "l"), ("g", 5, 3, "l"), ("g", 5, 3, "s"),
    ("A1", -3), ("A1", 3), ("g", 4, 4, "l"), ("stat1",), ("g", 5, 4, "l"), ("A1", -4), ("A2", 0), ("A2", 1),
    ("A2", 2), ("stat2",), ("B2", 0), ("u", 0, 1, "l"), ("u", 0, 1, "s"), ("u", 1, 0, "l"), ("B2", 1), ("B2", 2),
    ("u", 1, 0, "s"), ("u", 2, 1, "l"), ("u", 2, 1, "s"), ("inner",), ("u", 1, 1, "l"), ("u", 0, 2, "l"),
    ("u", 4, 1, "l"), ("u", 0, 2, "s"), ("u", 1, 1, "s"), ("u", 3, 0, "l"), ("u", 4, 1, "s"), ("u", 2, 2, "l"),
    ("u", 3, 0, "s"), ("u", 2, 2, "s"), ("u", 1, 2, "l"), ("u", 0, 3, "l"), ("usum",), ("gsum",), ("vg", 0),
    ("u", 3, 1, "l"), ("u", 4, 2, "l"), ("u", 1, 2, "s"), ("vg", 1), ("u", 5, 0, "l"), ("u", 2, 3, "l"),
    ("u", 4, 2, "s"), ("u", 5, 0, "s"), ("u", 3, 1, "s"), ("fin",), ("u", 1, 3, "l"), ("cross", 0),
    ("u", 3, 2, "l"), ("u", 5, 1, "l"), ("u", 4, 3, "l"), ("end", 1), ("end", 0), ("cross", 2), ("u", 3, 3, "l"),
    ("u", 5, 1, "s"), ("u", 5, 2, "l"), ("u", 3, 2, "s"), ("cross", 4), ("end", 2), ("u", 5, 2, "s"),
    ("u", 5, 3, "l"), ("end", 3), ("end", 4), ("end", 5),
)


def kernel(
    sizes,
    vq_h, ak_h, av_h, aq_h, vk_h, vv_h, up_h, ao_h, gains, vlen, alen,
    vo_h, aco_h, vqg_h, akg_h, avg_h, aqg_h, vkg_h, vvg_h, gg_h,
    g, raw_v, gqn, gkn, qn, kn, dvid, vout, vvg, part, rr, rl, xin, xs, xr, fin,
    pa, dpa, dsa, ast, acf, pb, dpb, dsb, acc, bias_a, bias_v, rbv, rba, small, fbuf,
    sloc, sin, sres, sall, ub, uin, ucol, gbuf, dbuf, gout, outa,
    ld, gs, gr, gxs, gxr, ts, tr, fs, fr, s1s, s1r, s2s, s2r, us, ur, ggs, ggr, ds_, dr_,
    rs_s, rs_r, xi_s, xi_r, ost,
):
    n_tower, n_seq, n_dp = sizes
    n_z = n_seq // 2
    nr = n_z // 2
    nl = n_z - 1 - nr
    arows = n_seq * 64
    depth = n_tower * WIDTH
    scale = 1.0 / math.sqrt(HD)
    c = scale * math.log2(math.e)
    unscale = scale / c

    t_at = lax.axis_index("tower")
    s_at = lax.axis_index("seq")
    d_at = lax.axis_index("dp")
    z = lax.rem(s_at, n_z)
    x = s_at // n_z

    def ring(zz):
        return lax.rem(zz + 2 * n_z, n_z)

    def seq_id(xx, zz):
        return xx * n_z + ring(zz)

    right, left, over = seq_id(x, z + 1), seq_id(x, z - 1), seq_id(1 - x, z)

    pending = []

    def send(src, dst, send_sem, recv_sem, **dev):
        copy = pltpu.make_async_remote_copy(
            src_ref=src, dst_ref=dst, send_sem=send_sem, recv_sem=recv_sem,
            device_id=dev, device_id_type=MESH,
        )
        copy.start()
        pending.append(copy)
        return copy

    own = aligned(z * 128 + x * 64, 64, 64)
    loads = []
    for n, (src, dst) in enumerate([
        (aq_h, g.at[2, own]),
        (ak_h, g.at[3, own]),
        (ao_h, g.at[0, own]),
        (av_h, g.at[1, own]),
        (vq_h, raw_v.at[0]),
        (vk_h, raw_v.at[1]),
        (vv_h, raw_v.at[2]),
        (up_h, raw_v.at[3]),
    ]):
        loads.append(pltpu.make_async_copy(src, dst, ld.at[n]))
        loads[n].start()
    barrier = pltpu.get_barrier_semaphore()
    peers = 0
    for k in range(1, n_seq):
        pl.semaphore_signal(barrier, inc=1, device_id={"seq": lax.rem(s_at + k, n_seq)}, device_id_type=MESH)
        peers += 1
    for k in range(1, n_tower):
        pl.semaphore_signal(barrier, inc=1, device_id={"tower": lax.rem(t_at + k, n_tower)}, device_id_type=MESH)
        peers += 1
    if n_dp > 1:
        pl.semaphore_signal(barrier, inc=1, device_id={"dp": 1 - d_at}, device_id_type=MESH)
        peers += 1

    for n in range(4):
        loads[n].wait()

    def put_video(n, which, row):
        for k in range(4):
            small[n, t_at, which * 4 + k : which * 4 + k + 1, :] = row[:, k * HD : (k + 1) * HD]

    for n in range(3):
        small[n, t_at] = jnp.zeros((16, HD), F32)
    both = jnp.concatenate([g[2, own, :].astype(F32), g[3, own, :].astype(F32)], axis=0)
    small[0, t_at, 8:9, :] = lanes_of(both * both)
    for n in range(2):
        loads[4 + n].wait()
        widened = raw_v[n].astype(F32)
        put_video(0, n, lanes_of(widened * widened))
    pl.semaphore_wait(barrier, peers)

    def tower_start(n):
        return [
            send(small.at[n, t_at], small.at[n, t_at], ts.at[n, k], tr.at[n, k], tower=lax.rem(t_at + k, n_tower))
            for k in range(1, n_tower)
        ]

    def tower_sum(n, copies):
        for copy in copies:
            copy.wait_recv()
        total = small[n, 0]
        for k in range(1, n_tower):
            total = total + small[n, k]
        return total

    arrays = (0, 2, 1, 3, 1, 3)
    chains = {}

    def gather_step(n, k, only=None):
        a = arrays[n]
        sign = 1 if n % 2 else -1
        ways = (("l", nr, left if n % 2 else right, sign, 0), ("s", nl, right if n % 2 else left, -sign, nr))
        half = 1 - x if n >= 4 else x

        def block(zz):
            return g.at[a, aligned(ring(zz) * 128 + half * 64, 64, 64)]

        if k == 0 and n >= 4:
            chains[n - 2, "x", 0].wait_recv()
        for name, count, to, way, base in ways:
            if k > count or only not in (None, name):
                continue
            here = block(z + way * k)
            if k > 0:
                chains[n, name, k].wait_recv()
            if k < count:
                chains[n, name, k + 1] = send(here, here, gs.at[n, base + k], gr.at[n, base + k], seq=to)
            if k > 0 and n < 2:
                chains[n, "x", base + k] = send(here, here, gxs.at[n, base + k], gxr.at[n, base + k], seq=over)

    def gather_over(n):
        here = g.at[arrays[n], own]
        chains[n, "x", 0] = send(here, here, gxs.at[n, 0], gxr.at[n, 0], seq=over)

    def over_wait(n, delta):
        towards = delta if n % 2 else -delta
        if delta == 0:
            at = 0
        elif abs(delta) == nr or towards > 0:
            at = abs(delta)
        else:
            at = nr + abs(delta)
        chains[n, "x", at].wait_recv()

    exch = tower_start(0)
    for n in range(4):
        if n > 1:
            gather_over(n)
        gather_step(n, 0)
        if n < 2:
            gather_over(n)
    sloc[...] = jnp.zeros_like(sloc)
    sres[...] = jnp.zeros_like(sres)
    ub[...] = jnp.zeros_like(ub)
    gbuf[s_at] = jnp.zeros((8, WIDTH), F32)
    for n in (6, 7):
        loads[n].wait()

    def masks():
        rho = lax.broadcasted_iota(jnp.int32, (arows, HD), 0)
        token = ((rho // 64) % 2) * (n_z * 64) + (rho // 128) * 64 + rho % 64
        bias_a[...] = jnp.where(token < alen[0], 0.0, MASKED)
        vtok = s_at * VROWS + lax.broadcasted_iota(jnp.int32, (VROWS, HD), 0)
        bias_v[...] = jnp.where(vtok < vlen[0], 0.0, MASKED)

    everyone = [(delta, k) for delta in range(n_z) for k in range(2) if delta or k]
    fsent = {}

    def factors_out(row):
        fbuf[s_at] = jnp.broadcast_to(row, (8, HD))
        for delta, k in everyone:
            to = seq_id(1 - x if k else x, z + delta)
            at = 2 * delta + k
            fsent[delta, k] = send(fbuf.at[s_at], fbuf.at[s_at], fs.at[at], fr.at[at], seq=to)

    def factors_in(delta):
        for k in range(2):
            if delta or k:
                fsent[-delta % n_z, k].wait_recv()

    def pair_factors(at, n):
        half = slice(n * 64, n * 64 + 64)
        return jnp.concatenate([column_of(fbuf[seq_id(xx, at), 0:1, :])[half] for xx in range(2)], axis=0)

    stat1 = []

    def audio_first(*deltas):
        for delta in deltas:
            over_wait(0, delta)
            over_wait(1, delta)
            factors_in(delta)
        for delta in deltas:
            at = ring(z + delta)
            rows = aligned(at * 128, 128, 128)
            col = pair_factors(at, 0)
            for h in range(HEADS):
                cols = head_cols(h)
                query = (g[2, rows, cols].astype(F32) * col * (gains[2:3, cols] * c)).astype(BF16)
                gqn[rows, cols] = query
                s = mm(kn[:, cols], query, NT) + bias_v[...]
                m = jnp.maximum(jnp.max(s, axis=0, keepdims=True), FLOOR)
                p = jnp.exp2(s - m)
                dp = mm(raw_v[2, :, cols], g[0, rows, cols], NT)
                pb[h, :, rows] = p.astype(BF16)
                dpb[h, :, rows] = dp
                sloc[at, h : h + 1, :] = m
                sloc[at, 3 + h : 4 + h, :] = jnp.sum(p, axis=0, keepdims=True)
                sloc[at, 6 + h : 7 + h, :] = jnp.sum(p * dp, axis=0, keepdims=True)
        for delta in deltas:
            at = ring(z + delta)
            slot = delta % n_z
            for k, xx in enumerate((x, 1 - x)):
                if delta == 0 and k == 0:
                    sin[s_at] = sloc[at]
                else:
                    n = 2 * slot + k
                    stat1.append(send(sloc.at[at], sin.at[s_at], s1s.at[n], s1r.at[n], seq=seq_id(xx, at)))

    def video_first(*deltas):
        for delta in deltas:
            at = ring(z + delta)
            rows = aligned(at * 128, 128, 128)
            col = pair_factors(at, 1)
            bias = wide(bias_a[rows, :], 4)
            for h in range(HEADS):
                cols = head_cols(h)
                key = (g[3, rows, cols].astype(F32) * col * gains[1:2, cols]).astype(BF16)
                gkn[rows, cols] = key
                s = mm(key, qn[:, cols], NT) + bias
                m = jnp.maximum(jnp.max(s, axis=0, keepdims=True), FLOOR)
                p = jnp.exp2(s - m)
                dp = mm(g[1, rows, cols], raw_v[3, :, cols], NT)
                pa[h, rows, :] = p.astype(BF16)
                dpa[h, rows, :] = dp
                ast[h, at, 0:1, :] = m
                ast[h, at, 1:2, :] = jnp.sum(p, axis=0, keepdims=True)
                ast[h, at, 2:3, :] = jnp.sum(p * dp, axis=0, keepdims=True)

    def factor_video(factors):
        for n in range(2):
            for k in range(4):
                rows = slice(k * HD, (k + 1) * HD)
                col = column_of(factors[n * 4 + k : n * 4 + k + 1, :])
                rbv[n, rows, :] = col
                for h in range(HEADS):
                    cols = head_cols(h)
                    gain = gains[3 * n : 3 * n + 1, cols] * (c if n == 0 else 1.0)
                    (qn, kn)[n][rows, cols] = (raw_v[n, rows, cols].astype(F32) * col * gain).astype(BF16)

    def video_second(h):
        cols = head_cols(h)
        m = ast[h, 0, 0:1, :]
        for k in range(1, n_z):
            m = jnp.maximum(m, ast[h, k, 0:1, :])
        total = jnp.zeros((1, VROWS), F32)
        inner = jnp.zeros((1, VROWS), F32)
        for k in range(n_z):
            f = jnp.exp2(ast[h, k, 0:1, :] - m)
            acf[k, 0:1, :] = f
            total = total + f * ast[h, k, 1:2, :]
            inner = inner + f * ast[h, k, 2:3, :]
        inverse = 1.0 / total
        delta = inner * inverse

        for k in range(n_z):
            rows = slice(k * 128, (k + 1) * 128)
            w = pa[h, rows, :].astype(F32) * (acf[k, 0:1, :] * inverse)
            pa[h, rows, :] = w.astype(BF16)
            dsa[rows, :] = (w * (dpa[h, rows, :] - delta)).astype(BF16)
        low = pa[h]
        ds = dsa[...]
        dk = mm(ds, qn[:, cols], NN) * unscale
        part[h, :, 0:HD] = dk.astype(BF16)
        part[h, :, HD:] = mm(low, raw_v[3, :, cols], NN).astype(BF16)
        prod = dk * gkn[:, cols].astype(F32)
        gbuf[s_at, 1:2, cols] = jnp.sum(prod, axis=0, keepdims=True) / gains[1:2, cols]
        acc[0] = prod if h == 0 else acc[0] + prod
        vout[:, cols] = mm(g[1, :, cols], low, TN).T.astype(BF16)
        dvid[0, :, cols] = mm(gkn[:, cols], ds, TN).T * scale

    def audio_second(h):
        cols = head_cols(h)

        for k in range(n_z):
            lanes = slice(k * HD, (k + 1) * HD)
            coef = jnp.exp2(sloc[k, h : h + 1, :] - sall[k, h : h + 1, :])
            w = pb[h, :, lanes].astype(F32) * coef
            pb[h, :, lanes] = w.astype(BF16)
            dsb[:, lanes] = (w * (dpb[h, :, lanes] - sall[k, 3 + h : 4 + h, :])).astype(BF16)
        low = pb[h]
        ds = dsb[...]
        part[HEADS + h, :, 0:HD] = mm(raw_v[2, :, cols], low, TN).T.astype(BF16)
        dq = mm(kn[:, cols], ds, TN).T * scale
        part[HEADS + h, :, HD:] = dq.astype(BF16)
        prod = dq * gqn[:, cols].astype(F32) * (1.0 / c)
        gbuf[s_at, 2:3, cols] = jnp.sum(prod, axis=0, keepdims=True) / gains[2:3, cols]
        acc[1] = prod if h == 0 else acc[1] + prod
        dvid[1, :, cols] = mm(ds, gqn[:, cols], NN) * unscale
        vvg[:, cols] = mm(low, g[0, :, cols], NN).astype(BF16)

    over_first = (1, 3, 5)
    mirrored = (0, 2, 4)
    rchain = {}
    order = []
    for dist in range(nr, 0, -1):
        order.append(dist)
        if dist <= nl:
            order.append(-dist)
    order.append(0)

    def scatter_over(*units):
        for k in range(n_z):
            for u in units:
                delta = -order[k] if u in mirrored else order[k]
                at = ring(z + delta)
                rchain[u, "x", delta % n_z] = send(
                    part.at[u, aligned(at * 128 + (1 - x) * 64, 64, 64)], xin.at[u, at],
                    xi_s.at[u, k], xi_r.at[u, k], seq=over,
                )

    def scatter_step(u, k, only):
        if True:
            early = u in over_first
            way = -1 if u in mirrored else 1
            size = 64 if early else 128
            ends = (right, left)[::way]
            for name, n, to, sign, base, land in (
                ("l", nr, ends[0], way, 0, rr), ("s", nl, ends[1], -way, nr, rl),
            ):
                if k >= n or name != only:
                    continue
                delta = sign * (n - k)
                at = ring(z + delta)
                rows = aligned(at * 128 + x * 64, 64, 64) if early else aligned(at * 128, 128, 128)
                if early or k > 0:
                    total = part[u, rows, :].astype(F32)
                    if early:
                        rchain[u, "x", delta % n_z].wait_recv()
                        total = total + xin[u, at].astype(F32)
                    if k > 0:
                        rchain[u, name, k - 1].wait_recv()
                        total = total + land[u, k - 1, 0:size, :].astype(F32)
                    part[u, rows, :] = total.astype(BF16)
                rchain[u, name, k] = send(
                    part.at[u, rows], land.at[u, k, 0:size], rs_s.at[u, base + k], rs_r.at[u, base + k], seq=to
                )

    def landed(u, total, size):
        rchain[u, "l", nr - 1].wait_recv()
        total = total + rr[u, nr - 1, 0:size, :].astype(F32)
        if nl > 0:
            rchain[u, "s", nl - 1].wait_recv()
            total = total + rl[u, nl - 1, 0:size, :].astype(F32)
        return total

    def scatter_cross(*units):
        for u in units:
            fin[u] = landed(u, part[u, aligned(z * 128, 128, 128), :].astype(F32), 128)
            xs[u] = fin[u, aligned((1 - x) * 64, 64, 64), :].astype(BF16)
            rchain[u, "k"] = send(xs.at[u], xr.at[u], rs_s.at[u, n_z - 1], rs_r.at[u, n_z - 1], seq=over)

    def scatter_end(u):
        if u in over_first:
            rchain[u, "x", 0].wait_recv()
            return landed(u, part[u, own, :].astype(F32) + xin[u, z].astype(F32), 64)
        rchain[u, "k"].wait_recv()
        return fin[u, aligned(x * 64, 64, 64), :] + xr[u].astype(F32)

    def scatter_start(u):
        if u in over_first:
            scatter_over(u)
        else:
            scatter_step(u, 0, "l")
            scatter_step(u, 0, "s")

    state = {}

    def combine():
        for copy in stat1:
            copy.wait_recv()
        mx = sin[0, 0:3, :]
        for k in range(1, n_seq):
            mx = jnp.maximum(mx, sin[k, 0:3, :])
        tot = jnp.zeros((3, HD), F32)
        inn = jnp.zeros((3, HD), F32)
        for k in range(n_seq):
            f = jnp.exp2(sin[k, 0:3, :] - mx)
            tot = tot + sin[k, 3:6, :] * f
            inn = inn + sin[k, 6:9, :] * f
        sres[0:3, :] = mx + jnp.log2(tot)
        sres[3:6, :] = inn / tot
        state["stat2"] = [send(sres, sall.at[z], s2s.at[k], s2r.at[k], seq=seq_id(x, z + k)) for k in range(1, n_z)]
        sall[z] = sres[...]

    def inner_products():
        for n, row in ((0, 0), (1, 3)):
            inner = dvid[n] * (qn, kn)[n][...].astype(F32) * (1.0 / c if n == 0 else 1.0)
            put_video(1, n, lanes_of(inner))
            gbuf[s_at, row : row + 1, :] = jnp.sum(inner, axis=0, keepdims=True) / gains[row : row + 1, :]
        state["video"] = tower_start(1)
        for n in range(2):
            row = lanes_of(acc[n])
            for k in range(n_z):
                ub[k, n : n + 1, :] = row[:, k * HD : (k + 1) * HD]
        state["u"] = []
        state["g"] = []
        for k in range(1, n_seq):
            to = lax.rem(s_at + k, n_seq)
            state["u"].append(send(ub.at[lax.rem(to, n_z)], uin.at[s_at], us.at[k], ur.at[k], seq=to))
        uin[s_at] = ub[z]
        for k in range(1, n_seq):
            to = lax.rem(s_at + k, n_seq)
            state["g"].append(send(gbuf.at[s_at], gbuf.at[s_at], ggs.at[k], ggr.at[k], seq=to))
        write(vout, vo_h)
        write(vvg, vvg_h)

    def total_of(copies, ref):
        for copy in copies:
            copy.wait_recv()
        total = ref[0]
        for k in range(1, n_seq):
            total = total + ref[k]
        return total

    def audio_inner():
        small[2, t_at, 0:8, :] = total_of(state["u"], uin)
        state["audio"] = tower_start(2)

    def gain_sums():
        dbuf[d_at] = total_of(state["g"], gbuf)
        if n_dp > 1:
            state["dp"] = send(dbuf.at[d_at], dbuf.at[d_at], ds_.at[0], dr_.at[0], dp=1 - d_at)

    def gain_out():
        if n_dp > 1:
            state["dp"].wait_recv()
            gout[...] = dbuf[0, 0:4, :] + dbuf[1, 0:4, :]
        else:
            gout[...] = dbuf[d_at, 0:4, :]
        write(gout, gg_h)

    outs = []

    def write(src, dst):
        copy = pltpu.make_async_copy(src, dst, ost.at[len(outs)])
        copy.start()
        outs.append(copy)

    def video_grad(n):
        if n == 0:
            state["inner"] = tower_sum(1, state["video"]) * (1.0 / depth)
        row = 3 * n
        for k in range(4):
            rows = slice(k * HD, (k + 1) * HD)
            col = column_of(state["inner"][n * 4 + k : n * 4 + k + 1, :])
            r = rbv[n, rows, :]
            for h in range(HEADS):
                cols = head_cols(h)
                grad = r * gains[row : row + 1, cols] * dvid[n, rows, cols] - raw_v[n, rows, cols].astype(F32) * (r * r * col)
                (qn, kn)[n][rows, cols] = grad.astype(BF16)
        write((qn, kn)[n], (vqg_h, vkg_h)[n])

    def audio_grad(n, h, total):
        cols = head_cols(h)
        r = rba[(1 - n) * 64 : (2 - n) * 64, :]
        col = ucol[n, aligned(x * 64, 64, 64), :]
        return (r * gains[n + 1 : n + 2, cols] * total - g[3 - n, own, cols].astype(F32) * (r * r * col)).astype(BF16)

    ended = []

    def unit_end(u):
        if not ended:
            uall = tower_sum(2, state["audio"]) * (1.0 / depth)
            for n in range(2):
                ucol[n] = column_of(uall[n : n + 1, :])
        both = scatter_end(u)
        h = u % HEADS
        if u < HEADS:
            outa[2, :, head_cols(h)] = audio_grad(0, h, both[:, 0:HD])
            outa[3, :, head_cols(h)] = both[:, HD:].astype(BF16)
        else:
            outa[0, :, head_cols(h)] = both[:, 0:HD].astype(BF16)
            outa[1, :, head_cols(h)] = audio_grad(1, h, both[:, HD:])
        ended.append(u)
        for first, parts in ((0, ((2, akg_h), (3, avg_h))), (HEADS, ((0, aco_h), (1, aqg_h)))):
            if first <= u < first + HEADS and all(first + k in ended for k in range(HEADS)):
                for n, dst in parts:
                    write(outa.at[n], dst)

    def tower_factors():
        state["factors"] = lax.rsqrt(tower_sum(0, exch) / depth + EPS)
        factors_out(state["factors"][8:9, :])
        rba[...] = column_of(state["factors"][8:9, :])

    reach = {"l": nr, "s": nl}
    for what, *at in EVENTS:
        if what == "g0":
            gather_step(at[0], 0)
        elif what == "g":
            if at[1] <= reach[at[2]]:
                gather_step(*at)
        elif what == "masks":
            masks()
        elif what == "tower":
            tower_factors()
        elif what == "vid":
            factor_video(state["factors"])
        elif what in ("A1", "B1"):
            if -nr <= at[0] <= nl:
                (video_first if what == "A1" else audio_first)(at[0])
        elif what == "A2":
            video_second(at[0])
            scatter_start(at[0])
        elif what == "B2":
            audio_second(at[0])
            scatter_start(HEADS + at[0])
        elif what == "stat1":
            combine()
        elif what == "stat2":
            for copy in state["stat2"]:
                copy.wait_recv()
        elif what == "u":
            if at[1] < reach[at[2]]:
                scatter_step(*at)
        elif what == "cross":
            scatter_cross(at[0])
        elif what == "inner":
            inner_products()
        elif what == "usum":
            audio_inner()
        elif what == "gsum":
            gain_sums()
        elif what == "vg":
            video_grad(at[0])
        elif what == "fin":
            gain_out()
        else:
            unit_end(at[0])
    for copy in outs:
        copy.wait()
    for copy in pending:
        copy.wait_send()


def hand_over(*refs):
    count = len(refs) // 3
    sems = refs[-1]
    ins = [pltpu.make_async_copy(refs[n], refs[2 * count + n], sems.at[0, n]) for n in range(count)]
    outs = [pltpu.make_async_copy(refs[2 * count + n], refs[count + n], sems.at[1, n]) for n in range(count)]
    for copy in ins:
        copy.start()
    for n in range(count):
        ins[n].wait()
        outs[n].start()
    for copy in outs:
        copy.wait()


def solution(mesh):
    sizes = tuple(mesh.shape[name] for name in ("tower", "seq", "dp"))
    n_tower, n_seq, n_dp = sizes
    n_z = n_seq // 2
    arows = n_seq * 64
    nr = n_z // 2
    nl = max(n_z - 1 - nr, 1)
    any_spec = pl.BlockSpec(memory_space=pl.ANY)
    vmem = pl.BlockSpec(memory_space=pltpu.VMEM)
    smem = pl.BlockSpec(memory_space=pltpu.SMEM)
    dma = lambda *shape: pltpu.SemaphoreType.DMA(shape)
    low = lambda *shape: pltpu.VMEM(shape, BF16)
    full = lambda *shape: pltpu.VMEM(shape, F32)

    def body(vq, ak, av, aq, vk, vv, up, ao, gains, vlen, alen):
        video = jax.ShapeDtypeStruct((VROWS, WIDTH), BF16)
        audio = jax.ShapeDtypeStruct((64, WIDTH), BF16)
        shapes = (video, audio, video, audio, audio, audio, video, video, jax.ShapeDtypeStruct((4, WIDTH), F32))
        results = pl.pallas_call(
            functools.partial(kernel, sizes),
            out_shape=shapes,
            in_specs=[any_spec] * 8 + [vmem, smem, smem],
            out_specs=tuple([any_spec] * 9),
            scratch_shapes=[
                low(4, arows, WIDTH),
                low(4, VROWS, WIDTH),
                low(arows, WIDTH),
                low(arows, WIDTH),
                low(VROWS, WIDTH),
                low(VROWS, WIDTH),
                full(2, VROWS, WIDTH),
                low(VROWS, WIDTH),
                low(VROWS, WIDTH),
                low(6, arows, 256),
                low(6, nr, 128, 256),
                low(6, nl, 128, 256),
                low(6, n_z, 64, 256),
                low(6, 64, 256),
                low(6, 64, 256),
                full(6, 128, 256),
                low(HEADS, arows, VROWS),
                full(HEADS, arows, VROWS),
                low(arows, VROWS),
                full(HEADS, n_z, 8, VROWS),
                full(n_z, 8, VROWS),
                low(HEADS, VROWS, arows),
                full(HEADS, VROWS, arows),
                low(VROWS, arows),
                full(2, arows, HD),
                full(arows, HD),
                full(VROWS, HD),
                full(2, VROWS, HD),
                full(128, HD),
                full(3, n_tower, 16, HD),
                full(n_seq, 8, HD),
                full(n_z, 16, HD),
                full(n_seq, 16, HD),
                full(8, HD),
                full(n_z, 8, HD),
                full(n_z, 8, HD),
                full(n_seq, 8, HD),
                full(2, 128, HD),
                full(n_seq, 8, WIDTH),
                full(2, 8, WIDTH),
                full(4, WIDTH),
                low(4, 64, WIDTH),
                dma(8), dma(6, n_z), dma(6, n_z), dma(4, n_z), dma(4, n_z), dma(3, n_tower), dma(3, n_tower),
                dma(n_seq), dma(n_seq), dma(n_seq), dma(n_seq), dma(n_z), dma(n_z), dma(n_seq), dma(n_seq),
                dma(n_seq), dma(n_seq), dma(1), dma(1), dma(6, n_z), dma(6, n_z), dma(6, n_z), dma(6, n_z), dma(9),
            ],
            compiler_params=pltpu.CompilerParams(
                collective_id=0, has_side_effects=True, vmem_limit_bytes=58 * 1024 * 1024
            ),
            cost_estimate=pl.CostEstimate(flops=4_800_000_000, bytes_accessed=4_000_000, transcendentals=3_200_000),
        )(vq[0], ak[0], av[0], aq[0], vk[0], vv[0], up[0], ao[0], gains, vlen, alen)
        results = pl.pallas_call(
            hand_over,
            out_shape=shapes,
            in_specs=[any_spec] * 9,
            out_specs=tuple([any_spec] * 9),
            scratch_shapes=[pltpu.VMEM(s.shape, s.dtype) for s in shapes] + [dma(2, 9)],
        )(*results)
        return tuple(r[None] for r in results[:8]) + (results[8],)

    spec = P("dp", "seq", "tower")
    return jax.shard_map(
        body,
        mesh=mesh,
        in_specs=(spec,) * 8 + (P(None, "tower"), P("dp"), P("dp")),
        out_specs=(spec,) * 8 + (P(None, "tower"),),
        check_vma=False,
    )
```

```python
import functools
import math

import jax
import jax.numpy as jnp
from jax import lax
from jax.experimental import pallas as pl
from jax.experimental.pallas import tpu as pltpu
from jax.sharding import PartitionSpec as P

HD = 128
HEADS = 3
WIDTH = HEADS * HD
VROWS = 512
EPS = 1e-06
MASKED = -1e30
FLOOR = -1e29
F32 = jnp.float32
BF16 = jnp.bfloat16
MESH = pl.DeviceIdType.MESH

NT = (((1,), (1,)), ((), ()))
NN = (((1,), (0,)), ((), ()))
TN = (((0,), (0,)), ((), ()))


def mm(a, b, dims):
    return lax.dot_general(a, b, dims, preferred_element_type=F32)


def aligned(start, size, unit):
    return pl.ds(pl.multiple_of(start, unit), size)


def lanes_of(products):
    part = products[:, 0:HD]
    for k in range(1, products.shape[1] // HD):
        part = part + products[:, k * HD : (k + 1) * HD]
    return jnp.sum(part.T, axis=0, keepdims=True)


def column_of(row):
    return jnp.broadcast_to(row, (HD, HD)).T


def head_cols(h):
    return slice(h * HD, (h + 1) * HD)


def wide(block, n):
    return jnp.concatenate([block] * n, axis=1)


EVENTS = (
    ("masks",), ("g", 0, 1, "l"), ("g", 0, 1, "s"), ("g", 1, 1, "s"), ("g", 1, 1, "l"), ("tower",), ("vid",),
    ("g0", 4), ("g0", 5), ("g", 2, 1, "l"), ("g", 3, 1, "l"), ("g", 2, 1, "s"), ("g", 3, 1, "s"), ("g", 0, 2, "l"),
    ("g", 0, 2, "s"), ("g", 1, 2, "s"), ("g", 1, 2, "l"), ("B1", 0), ("g", 4, 1, "l"), ("g", 4, 1, "s"), ("B1", -1),
    ("B1", 1), ("g", 5, 1, "l"), ("g", 5, 1, "s"), ("A1", 0), ("g", 2, 2, "l"), ("g", 3, 2, "l"), ("A1", -1),
    ("A1", 1), ("g", 2, 2, "s"), ("g", 3, 2, "s"), ("B1", -2), ("g", 0, 3, "l"), ("g", 0, 3, "s"), ("B1", 2),
    ("g", 1, 3, "s"), ("g", 1, 3, "l"), ("g", 4, 2, "l"), ("g", 4, 2, "s"), ("g", 5, 2, "s"), ("g", 5, 2, "l"),
    ("A1", -2), ("A1", 2), ("g", 2, 3, "l"), ("g", 3, 3, "l"), ("g", 3, 3, "s"), ("g", 2, 3, "s"), ("B1", -3),
    ("g", 0, 4, "l"), ("g", 1, 4, "l"), ("B1", 3), ("g", 4, 3, "l"), ("g", 4, 3, "s"), ("g", 5, 3, "s"),
    ("g", 5, 3, "l"), ("A1", -3), ("A1", 3), ("g", 2, 4, "l"), ("g", 3, 4, "l"), ("g", 4, 4, "l"), ("B1", -4),
    ("g", 5, 4, "l"), ("A1", -4), ("A2", 0), ("A2", 1), ("A2", 2), ("stat1",), ("u", 0, 1, "l"), ("u", 0, 1, "s"),
    ("u", 1, 1, "s"), ("u", 1, 1, "l"), ("u", 2, 1, "l"), ("u", 2, 1, "s"), ("u", 0, 2, "l"), ("u", 0, 2, "s"),
    ("stat2",), ("B2", 0), ("u", 1, 2, "s"), ("u", 1, 2, "l"), ("B2", 1), ("u", 2, 2, "l"), ("u", 2, 2, "s"),
    ("B2", 2), ("u", 0, 3, "l"), ("u", 3, 0, "l"), ("inner",), ("u", 3, 0, "s"), ("u", 1, 3, "l"), ("u", 4, 1, "s"),
    ("u", 4, 1, "l"), ("u", 2, 3, "l"), ("u", 3, 1, "l"), ("cross", 0), ("u", 5, 0, "l"), ("u", 3, 1, "s"),
    ("cross", 1), ("u", 5, 0, "s"), ("usum",), ("u", 4, 2, "l"), ("u", 4, 2, "s"), ("gsum",), ("u", 3, 2, "l"),
    ("vg", 0), ("cross", 2), ("u", 5, 1, "l"), ("vg", 1), ("u", 5, 1, "s"), ("u", 3, 2, "s"), ("u", 4, 3, "l"),
    ("fin",), ("u", 3, 3, "l"), ("u", 5, 2, "l"), ("end", 0), ("end", 1), ("end", 2), ("u", 5, 2, "s"),
    ("cross", 4), ("u", 5, 3, "l"), ("end", 3), ("end", 4), ("end", 5),
)


def kernel(
    sizes,
    vq_h, ak_h, av_h, aq_h, vk_h, vv_h, up_h, ao_h, gains, vlen, alen,
    vo_h, aco_h, vqg_h, akg_h, avg_h, aqg_h, vkg_h, vvg_h, gg_h,
    g, raw_v, gqn, gkn, qn, kn, dvid, vout, vvg, part, rr, rl, xin, xs, xr, fin,
    pa, dpa, dsa, ast, acf, pb, dpb, dsb, acc, bias_a, bias_v, rbv, rba, small, fbuf,
    sloc, sin, sres, sall, ub, uin, ucol, gbuf, dbuf, gout, outa,
    ld, gs, gr, gxs, gxr, ts, tr, fs, fr, s1s, s1r, s2s, s2r, us, ur, ggs, ggr, ds_, dr_,
    rs_s, rs_r, xi_s, xi_r, ost,
):
    n_tower, n_seq, n_dp = sizes
    n_z = n_seq // 2
    nr = n_z // 2
    nl = n_z - 1 - nr
    arows = n_seq * 64
    depth = n_tower * WIDTH
    scale = 1.0 / math.sqrt(HD)
    c = scale * math.log2(math.e)
    unscale = scale / c

    t_at = lax.axis_index("tower")
    s_at = lax.axis_index("seq")
    d_at = lax.axis_index("dp")
    z = lax.rem(s_at, n_z)
    x = s_at // n_z

    def ring(zz):
        return lax.rem(zz + 2 * n_z, n_z)

    def seq_id(xx, zz):
        return xx * n_z + ring(zz)

    right, left, over = seq_id(x, z + 1), seq_id(x, z - 1), seq_id(1 - x, z)

    pending = []

    def send(src, dst, send_sem, recv_sem, **dev):
        copy = pltpu.make_async_remote_copy(
            src_ref=src, dst_ref=dst, send_sem=send_sem, recv_sem=recv_sem,
            device_id=dev, device_id_type=MESH,
        )
        copy.start()
        pending.append(copy)
        return copy

    own = aligned(z * 128 + x * 64, 64, 64)
    loads = []
    for n, (src, dst) in enumerate([
        (aq_h, g.at[2, own]),
        (ak_h, g.at[3, own]),
        (ao_h, g.at[0, own]),
        (av_h, g.at[1, own]),
        (vq_h, raw_v.at[0]),
        (vk_h, raw_v.at[1]),
        (vv_h, raw_v.at[2]),
        (up_h, raw_v.at[3]),
    ]):
        loads.append(pltpu.make_async_copy(src, dst, ld.at[n]))
        loads[n].start()
    barrier = pltpu.get_barrier_semaphore()
    peers = 0
    for k in range(1, n_seq):
        pl.semaphore_signal(barrier, inc=1, device_id={"seq": lax.rem(s_at + k, n_seq)}, device_id_type=MESH)
        peers += 1
    for k in range(1, n_tower):
        pl.semaphore_signal(barrier, inc=1, device_id={"tower": lax.rem(t_at + k, n_tower)}, device_id_type=MESH)
        peers += 1
    if n_dp > 1:
        pl.semaphore_signal(barrier, inc=1, device_id={"dp": 1 - d_at}, device_id_type=MESH)
        peers += 1

    for n in range(4):
        loads[n].wait()

    def put_video(n, which, row):
        for k in range(4):
            small[n, t_at, which * 4 + k : which * 4 + k + 1, :] = row[:, k * HD : (k + 1) * HD]

    for n in range(3):
        small[n, t_at] = jnp.zeros((16, HD), F32)
    both = jnp.concatenate([g[2, own, :].astype(F32), g[3, own, :].astype(F32)], axis=0)
    small[0, t_at, 8:9, :] = lanes_of(both * both)
    for n in range(2):
        loads[4 + n].wait()
        widened = raw_v[n].astype(F32)
        put_video(0, n, lanes_of(widened * widened))
    pl.semaphore_wait(barrier, peers)

    def tower_start(n):
        return [
            send(small.at[n, t_at], small.at[n, t_at], ts.at[n, k], tr.at[n, k], tower=lax.rem(t_at + k, n_tower))
            for k in range(1, n_tower)
        ]

    def tower_sum(n, copies):
        for copy in copies:
            copy.wait_recv()
        total = small[n, 0]
        for k in range(1, n_tower):
            total = total + small[n, k]
        return total

    arrays = (0, 2, 1, 3, 1, 3)
    chains = {}

    def gather_step(n, k, only=None):
        a = arrays[n]
        sign = 1 if n % 2 else -1
        ways = (("l", nr, left if n % 2 else right, sign, 0), ("s", nl, right if n % 2 else left, -sign, nr))
        half = 1 - x if n >= 4 else x

        def block(zz):
            return g.at[a, aligned(ring(zz) * 128 + half * 64, 64, 64)]

        if k == 0 and n >= 4:
            chains[n - 2, "x", 0].wait_recv()
        for name, count, to, way, base in ways:
            if k > count or only not in (None, name):
                continue
            here = block(z + way * k)
            if k > 0:
                chains[n, name, k].wait_recv()
            if k < count:
                chains[n, name, k + 1] = send(here, here, gs.at[n, base + k], gr.at[n, base + k], seq=to)
            if k > 0 and n < 2:
                chains[n, "x", base + k] = send(here, here, gxs.at[n, base + k], gxr.at[n, base + k], seq=over)

    def gather_over(n):
        here = g.at[arrays[n], own]
        chains[n, "x", 0] = send(here, here, gxs.at[n, 0], gxr.at[n, 0], seq=over)

    def over_wait(n, delta):
        towards = delta if n % 2 else -delta
        if delta == 0:
            at = 0
        elif abs(delta) == nr or towards > 0:
            at = abs(delta)
        else:
            at = nr + abs(delta)
        chains[n, "x", at].wait_recv()

    exch = tower_start(0)
    for n in range(4):
        if n > 1:
            gather_over(n)
        gather_step(n, 0)
        if n < 2:
            gather_over(n)
    sloc[...] = jnp.zeros_like(sloc)
    sres[...] = jnp.zeros_like(sres)
    ub[...] = jnp.zeros_like(ub)
    gbuf[s_at] = jnp.zeros((8, WIDTH), F32)
    for n in (6, 7):
        loads[n].wait()

    def masks():
        rho = lax.broadcasted_iota(jnp.int32, (arows, HD), 0)
        token = ((rho // 64) % 2) * (n_z * 64) + (rho // 128) * 64 + rho % 64
        bias_a[...] = jnp.where(token < alen[0], 0.0, MASKED)
        vtok = s_at * VROWS + lax.broadcasted_iota(jnp.int32, (VROWS, HD), 0)
        bias_v[...] = jnp.where(vtok < vlen[0], 0.0, MASKED)

    everyone = [(delta, k) for delta in range(n_z) for k in range(2) if delta or k]
    fsent = {}

    def factors_out(row):
        fbuf[s_at] = jnp.broadcast_to(row, (8, HD))
        for delta, k in everyone:
            to = seq_id(1 - x if k else x, z + delta)
            at = 2 * delta + k
            fsent[delta, k] = send(fbuf.at[s_at], fbuf.at[s_at], fs.at[at], fr.at[at], seq=to)

    def factors_in(delta):
        for k in range(2):
            if delta or k:
                fsent[-delta % n_z, k].wait_recv()

    def pair_factors(at, n):
        half = slice(n * 64, n * 64 + 64)
        return jnp.concatenate([column_of(fbuf[seq_id(xx, at), 0:1, :])[half] for xx in range(2)], axis=0)

    stat1 = []

    def audio_first(*deltas):
        for delta in deltas:
            over_wait(0, delta)
            over_wait(1, delta)
            factors_in(delta)
        for delta in deltas:
            at = ring(z + delta)
            rows = aligned(at * 128, 128, 128)
            col = pair_factors(at, 0)
            for h in range(HEADS):
                cols = head_cols(h)
                query = (g[2, rows, cols].astype(F32) * col * (gains[2:3, cols] * c)).astype(BF16)
                gqn[rows, cols] = query
                s = mm(kn[:, cols], query, NT) + bias_v[...]
                m = jnp.maximum(jnp.max(s, axis=0, keepdims=True), FLOOR)
                p = jnp.exp2(s - m)
                dp = mm(raw_v[2, :, cols], g[0, rows, cols], NT)
                pb[h, :, rows] = p.astype(BF16)
                dpb[h, :, rows] = dp
                sloc[at, h : h + 1, :] = m
                sloc[at, 3 + h : 4 + h, :] = jnp.sum(p, axis=0, keepdims=True)
                sloc[at, 6 + h : 7 + h, :] = jnp.sum(p * dp, axis=0, keepdims=True)
        for delta in deltas:
            at = ring(z + delta)
            slot = delta % n_z
            for k, xx in enumerate((x, 1 - x)):
                if delta == 0 and k == 0:
                    sin[s_at] = sloc[at]
                else:
                    n = 2 * slot + k
                    stat1.append(send(sloc.at[at], sin.at[s_at], s1s.at[n], s1r.at[n], seq=seq_id(xx, at)))

    def video_first(*deltas):
        for delta in deltas:
            at = ring(z + delta)
            rows = aligned(at * 128, 128, 128)
            col = pair_factors(at, 1)
            bias = wide(bias_a[rows, :], 4)
            for h in range(HEADS):
                cols = head_cols(h)
                key = (g[3, rows, cols].astype(F32) * col * gains[1:2, cols]).astype(BF16)
                gkn[rows, cols] = key
                s = mm(key, qn[:, cols], NT) + bias
                m = jnp.maximum(jnp.max(s, axis=0, keepdims=True), FLOOR)
                p = jnp.exp2(s - m)
                dp = mm(g[1, rows, cols], raw_v[3, :, cols], NT)
                pa[h, rows, :] = p.astype(BF16)
                dpa[h, rows, :] = dp
                ast[h, at, 0:1, :] = m
                ast[h, at, 1:2, :] = jnp.sum(p, axis=0, keepdims=True)
                ast[h, at, 2:3, :] = jnp.sum(p * dp, axis=0, keepdims=True)

    def factor_video(factors):
        for n in range(2):
            for k in range(4):
                rows = slice(k * HD, (k + 1) * HD)
                col = column_of(factors[n * 4 + k : n * 4 + k + 1, :])
                rbv[n, rows, :] = col
                for h in range(HEADS):
                    cols = head_cols(h)
                    gain = gains[3 * n : 3 * n + 1, cols] * (c if n == 0 else 1.0)
                    (qn, kn)[n][rows, cols] = (raw_v[n, rows, cols].astype(F32) * col * gain).astype(BF16)

    def video_second(h):
        cols = head_cols(h)
        m = ast[h, 0, 0:1, :]
        for k in range(1, n_z):
            m = jnp.maximum(m, ast[h, k, 0:1, :])
        total = jnp.zeros((1, VROWS), F32)
        inner = jnp.zeros((1, VROWS), F32)
        for k in range(n_z):
            f = jnp.exp2(ast[h, k, 0:1, :] - m)
            acf[k, 0:1, :] = f
            total = total + f * ast[h, k, 1:2, :]
            inner = inner + f * ast[h, k, 2:3, :]
        inverse = 1.0 / total
        delta = inner * inverse

        for k in range(n_z):
            rows = slice(k * 128, (k + 1) * 128)
            w = pa[h, rows, :].astype(F32) * (acf[k, 0:1, :] * inverse)
            pa[h, rows, :] = w.astype(BF16)
            dsa[rows, :] = (w * (dpa[h, rows, :] - delta)).astype(BF16)
        low = pa[h]
        ds = dsa[...]
        dk = mm(ds, qn[:, cols], NN) * unscale
        part[h, :, 0:HD] = dk.astype(BF16)
        part[h, :, HD:] = mm(low, raw_v[3, :, cols], NN).astype(BF16)
        prod = dk * gkn[:, cols].astype(F32)
        gbuf[s_at, 1:2, cols] = jnp.sum(prod, axis=0, keepdims=True) / gains[1:2, cols]
        acc[0] = prod if h == 0 else acc[0] + prod
        vout[:, cols] = mm(g[1, :, cols], low, TN).T.astype(BF16)
        dvid[0, :, cols] = mm(gkn[:, cols], ds, TN).T * scale

    def audio_second(h):
        cols = head_cols(h)

        for k in range(n_z):
            lanes = slice(k * HD, (k + 1) * HD)
            coef = jnp.exp2(sloc[k, h : h + 1, :] - sall[k, h : h + 1, :])
            w = pb[h, :, lanes].astype(F32) * coef
            pb[h, :, lanes] = w.astype(BF16)
            dsb[:, lanes] = (w * (dpb[h, :, lanes] - sall[k, 3 + h : 4 + h, :])).astype(BF16)
        low = pb[h]
        ds = dsb[...]
        part[HEADS + h, :, 0:HD] = mm(raw_v[2, :, cols], low, TN).T.astype(BF16)
        dq = mm(kn[:, cols], ds, TN).T * scale
        part[HEADS + h, :, HD:] = dq.astype(BF16)
        prod = dq * gqn[:, cols].astype(F32) * (1.0 / c)
        gbuf[s_at, 2:3, cols] = jnp.sum(prod, axis=0, keepdims=True) / gains[2:3, cols]
        acc[1] = prod if h == 0 else acc[1] + prod
        dvid[1, :, cols] = mm(ds, gqn[:, cols], NN) * unscale
        vvg[:, cols] = mm(low, g[0, :, cols], NN).astype(BF16)

    over_first = (3, 5)
    mirrored = (0, 2, 5)
    rchain = {}
    order = []
    for dist in range(nr, 0, -1):
        order.append(dist)
        if dist <= nl:
            order.append(-dist)
    order.append(0)

    def scatter_over(*units):
        for k in range(n_z):
            for u in units:
                delta = -order[k] if u in mirrored else order[k]
                at = ring(z + delta)
                rchain[u, "x", delta % n_z] = send(
                    part.at[u, aligned(at * 128 + (1 - x) * 64, 64, 64)], xin.at[u, at],
                    xi_s.at[u, k], xi_r.at[u, k], seq=over,
                )

    def scatter_step(u, k, only):
        if True:
            early = u in over_first
            way = -1 if u in mirrored else 1
            size = 64 if early else 128
            ends = (right, left)[::way]
            for name, n, to, sign, base, land in (
                ("l", nr, ends[0], way, 0, rr), ("s", nl, ends[1], -way, nr, rl),
            ):
                if k >= n or name != only:
                    continue
                delta = sign * (n - k)
                at = ring(z + delta)
                rows = aligned(at * 128 + x * 64, 64, 64) if early else aligned(at * 128, 128, 128)
                if early or k > 0:
                    total = part[u, rows, :].astype(F32)
                    if early:
                        rchain[u, "x", delta % n_z].wait_recv()
                        total = total + xin[u, at].astype(F32)
                    if k > 0:
                        rchain[u, name, k - 1].wait_recv()
                        total = total + land[u, k - 1, 0:size, :].astype(F32)
                    part[u, rows, :] = total.astype(BF16)
                rchain[u, name, k] = send(
                    part.at[u, rows], land.at[u, k, 0:size], rs_s.at[u, base + k], rs_r.at[u, base + k], seq=to
                )

    def landed(u, total, size):
        rchain[u, "l", nr - 1].wait_recv()
        total = total + rr[u, nr - 1, 0:size, :].astype(F32)
        if nl > 0:
            rchain[u, "s", nl - 1].wait_recv()
            total = total + rl[u, nl - 1, 0:size, :].astype(F32)
        return total

    def scatter_cross(*units):
        for u in units:
            fin[u] = landed(u, part[u, aligned(z * 128, 128, 128), :].astype(F32), 128)
            xs[u] = fin[u, aligned((1 - x) * 64, 64, 64), :].astype(BF16)
            rchain[u, "k"] = send(xs.at[u], xr.at[u], rs_s.at[u, n_z - 1], rs_r.at[u, n_z - 1], seq=over)

    def scatter_end(u):
        if u in over_first:
            rchain[u, "x", 0].wait_recv()
            return landed(u, part[u, own, :].astype(F32) + xin[u, z].astype(F32), 64)
        rchain[u, "k"].wait_recv()
        return fin[u, aligned(x * 64, 64, 64), :] + xr[u].astype(F32)

    def scatter_start(u):
        if u in over_first:
            scatter_over(u)
        else:
            scatter_step(u, 0, "l")
            scatter_step(u, 0, "s")

    state = {}

    def combine():
        for copy in stat1:
            copy.wait_recv()
        mx = sin[0, 0:3, :]
        for k in range(1, n_seq):
            mx = jnp.maximum(mx, sin[k, 0:3, :])
        tot = jnp.zeros((3, HD), F32)
        inn = jnp.zeros((3, HD), F32)
        for k in range(n_seq):
            f = jnp.exp2(sin[k, 0:3, :] - mx)
            tot = tot + sin[k, 3:6, :] * f
            inn = inn + sin[k, 6:9, :] * f
        sres[0:3, :] = mx + jnp.log2(tot)
        sres[3:6, :] = inn / tot
        state["stat2"] = [send(sres, sall.at[z], s2s.at[k], s2r.at[k], seq=seq_id(x, z + k)) for k in range(1, n_z)]
        sall[z] = sres[...]

    def inner_products():
        for n, row in ((0, 0), (1, 3)):
            inner = dvid[n] * (qn, kn)[n][...].astype(F32) * (1.0 / c if n == 0 else 1.0)
            put_video(1, n, lanes_of(inner))
            gbuf[s_at, row : row + 1, :] = jnp.sum(inner, axis=0, keepdims=True) / gains[row : row + 1, :]
        state["video"] = tower_start(1)
        for n in range(2):
            row = lanes_of(acc[n])
            for k in range(n_z):
                ub[k, n : n + 1, :] = row[:, k * HD : (k + 1) * HD]
        state["u"] = []
        state["g"] = []
        for k in range(1, n_seq):
            to = lax.rem(s_at + k, n_seq)
            state["u"].append(send(ub.at[lax.rem(to, n_z)], uin.at[s_at], us.at[k], ur.at[k], seq=to))
        uin[s_at] = ub[z]
        for k in range(1, n_seq):
            to = lax.rem(s_at + k, n_seq)
            state["g"].append(send(gbuf.at[s_at], gbuf.at[s_at], ggs.at[k], ggr.at[k], seq=to))
        write(vout, vo_h)
        write(vvg, vvg_h)

    def total_of(copies, ref):
        for copy in copies:
            copy.wait_recv()
        total = ref[0]
        for k in range(1, n_seq):
            total = total + ref[k]
        return total

    def audio_inner():
        small[2, t_at, 0:8, :] = total_of(state["u"], uin)
        state["audio"] = tower_start(2)

    def gain_sums():
        dbuf[d_at] = total_of(state["g"], gbuf)
        if n_dp > 1:
            state["dp"] = send(dbuf.at[d_at], dbuf.at[d_at], ds_.at[0], dr_.at[0], dp=1 - d_at)

    def gain_out():
        if n_dp > 1:
            state["dp"].wait_recv()
            gout[...] = dbuf[0, 0:4, :] + dbuf[1, 0:4, :]
        else:
            gout[...] = dbuf[d_at, 0:4, :]
        write(gout, gg_h)

    outs = []

    def write(src, dst):
        copy = pltpu.make_async_copy(src, dst, ost.at[len(outs)])
        copy.start()
        outs.append(copy)

    def video_grad(n):
        if n == 0:
            state["inner"] = tower_sum(1, state["video"]) * (1.0 / depth)
        row = 3 * n
        for k in range(4):
            rows = slice(k * HD, (k + 1) * HD)
            col = column_of(state["inner"][n * 4 + k : n * 4 + k + 1, :])
            r = rbv[n, rows, :]
            for h in range(HEADS):
                cols = head_cols(h)
                grad = r * gains[row : row + 1, cols] * dvid[n, rows, cols] - raw_v[n, rows, cols].astype(F32) * (r * r * col)
                (qn, kn)[n][rows, cols] = grad.astype(BF16)
        write((qn, kn)[n], (vqg_h, vkg_h)[n])

    def audio_grad(n, h, total):
        cols = head_cols(h)
        r = rba[(1 - n) * 64 : (2 - n) * 64, :]
        col = ucol[n, aligned(x * 64, 64, 64), :]
        return (r * gains[n + 1 : n + 2, cols] * total - g[3 - n, own, cols].astype(F32) * (r * r * col)).astype(BF16)

    ended = []

    def unit_end(u):
        if not ended:
            uall = tower_sum(2, state["audio"]) * (1.0 / depth)
            for n in range(2):
                ucol[n] = column_of(uall[n : n + 1, :])
        both = scatter_end(u)
        h = u % HEADS
        if u < HEADS:
            outa[2, :, head_cols(h)] = audio_grad(0, h, both[:, 0:HD])
            outa[3, :, head_cols(h)] = both[:, HD:].astype(BF16)
        else:
            outa[0, :, head_cols(h)] = both[:, 0:HD].astype(BF16)
            outa[1, :, head_cols(h)] = audio_grad(1, h, both[:, HD:])
        ended.append(u)
        for first, parts in ((0, ((2, akg_h), (3, avg_h))), (HEADS, ((0, aco_h), (1, aqg_h)))):
            if first <= u < first + HEADS and all(first + k in ended for k in range(HEADS)):
                for n, dst in parts:
                    write(outa.at[n], dst)

    def tower_factors():
        state["factors"] = lax.rsqrt(tower_sum(0, exch) / depth + EPS)
        factors_out(state["factors"][8:9, :])
        rba[...] = column_of(state["factors"][8:9, :])

    reach = {"l": nr, "s": nl}
    for what, *at in EVENTS:
        if what == "g0":
            gather_step(at[0], 0)
        elif what == "g":
            if at[1] <= reach[at[2]]:
                gather_step(*at)
        elif what == "masks":
            masks()
        elif what == "tower":
            tower_factors()
        elif what == "vid":
            factor_video(state["factors"])
        elif what in ("A1", "B1"):
            if -nr <= at[0] <= nl:
                (video_first if what == "A1" else audio_first)(at[0])
        elif what == "A2":
            video_second(at[0])
            scatter_start(at[0])
        elif what == "B2":
            audio_second(at[0])
            scatter_start(HEADS + at[0])
        elif what == "stat1":
            combine()
        elif what == "stat2":
            for copy in state["stat2"]:
                copy.wait_recv()
        elif what == "u":
            if at[1] < reach[at[2]]:
                scatter_step(*at)
        elif what == "cross":
            scatter_cross(at[0])
        elif what == "inner":
            inner_products()
        elif what == "usum":
            audio_inner()
        elif what == "gsum":
            gain_sums()
        elif what == "vg":
            video_grad(at[0])
        elif what == "fin":
            gain_out()
        else:
            unit_end(at[0])
    for copy in outs:
        copy.wait()
    for copy in pending:
        copy.wait_send()


def hand_over(*refs):
    count = len(refs) // 3
    sems = refs[-1]
    ins = [pltpu.make_async_copy(refs[n], refs[2 * count + n], sems.at[0, n]) for n in range(count)]
    outs = [pltpu.make_async_copy(refs[2 * count + n], refs[count + n], sems.at[1, n]) for n in range(count)]
    for copy in ins:
        copy.start()
    for n in range(count):
        ins[n].wait()
        outs[n].start()
    for copy in outs:
        copy.wait()


def solution(mesh):
    sizes = tuple(mesh.shape[name] for name in ("tower", "seq", "dp"))
    n_tower, n_seq, n_dp = sizes
    n_z = n_seq // 2
    arows = n_seq * 64
    nr = n_z // 2
    nl = max(n_z - 1 - nr, 1)
    any_spec = pl.BlockSpec(memory_space=pl.ANY)
    vmem = pl.BlockSpec(memory_space=pltpu.VMEM)
    smem = pl.BlockSpec(memory_space=pltpu.SMEM)
    dma = lambda *shape: pltpu.SemaphoreType.DMA(shape)
    low = lambda *shape: pltpu.VMEM(shape, BF16)
    full = lambda *shape: pltpu.VMEM(shape, F32)

    def body(vq, ak, av, aq, vk, vv, up, ao, gains, vlen, alen):
        video = jax.ShapeDtypeStruct((VROWS, WIDTH), BF16)
        audio = jax.ShapeDtypeStruct((64, WIDTH), BF16)
        shapes = (video, audio, video, audio, audio, audio, video, video, jax.ShapeDtypeStruct((4, WIDTH), F32))
        results = pl.pallas_call(
            functools.partial(kernel, sizes),
            out_shape=shapes,
            in_specs=[any_spec] * 8 + [vmem, smem, smem],
            out_specs=tuple([any_spec] * 9),
            scratch_shapes=[
                low(4, arows, WIDTH),
                low(4, VROWS, WIDTH),
                low(arows, WIDTH),
                low(arows, WIDTH),
                low(VROWS, WIDTH),
                low(VROWS, WIDTH),
                full(2, VROWS, WIDTH),
                low(VROWS, WIDTH),
                low(VROWS, WIDTH),
                low(6, arows, 256),
                low(6, nr, 128, 256),
                low(6, nl, 128, 256),
                low(6, n_z, 64, 256),
                low(6, 64, 256),
                low(6, 64, 256),
                full(6, 128, 256),
                low(HEADS, arows, VROWS),
                full(HEADS, arows, VROWS),
                low(arows, VROWS),
                full(HEADS, n_z, 8, VROWS),
                full(n_z, 8, VROWS),
                low(HEADS, VROWS, arows),
                full(HEADS, VROWS, arows),
                low(VROWS, arows),
                full(2, arows, HD),
                full(arows, HD),
                full(VROWS, HD),
                full(2, VROWS, HD),
                full(128, HD),
                full(3, n_tower, 16, HD),
                full(n_seq, 8, HD),
                full(n_z, 16, HD),
                full(n_seq, 16, HD),
                full(8, HD),
                full(n_z, 8, HD),
                full(n_z, 8, HD),
                full(n_seq, 8, HD),
                full(2, 128, HD),
                full(n_seq, 8, WIDTH),
                full(2, 8, WIDTH),
                full(4, WIDTH),
                low(4, 64, WIDTH),
                dma(8), dma(6, n_z), dma(6, n_z), dma(4, n_z), dma(4, n_z), dma(3, n_tower), dma(3, n_tower),
                dma(n_seq), dma(n_seq), dma(n_seq), dma(n_seq), dma(n_z), dma(n_z), dma(n_seq), dma(n_seq),
                dma(n_seq), dma(n_seq), dma(1), dma(1), dma(6, n_z), dma(6, n_z), dma(6, n_z), dma(6, n_z), dma(9),
            ],
            compiler_params=pltpu.CompilerParams(
                collective_id=0, has_side_effects=True, vmem_limit_bytes=58 * 1024 * 1024
            ),
            cost_estimate=pl.CostEstimate(flops=4_800_000_000, bytes_accessed=4_000_000, transcendentals=3_200_000),
        )(vq[0], ak[0], av[0], aq[0], vk[0], vv[0], up[0], ao[0], gains, vlen, alen)
        results = pl.pallas_call(
            hand_over,
            out_shape=shapes,
            in_specs=[any_spec] * 9,
            out_specs=tuple([any_spec] * 9),
            scratch_shapes=[pltpu.VMEM(s.shape, s.dtype) for s in shapes] + [dma(2, 9)],
        )(*results)
        return tuple(r[None] for r in results[:8]) + (results[8],)

    spec = P("dp", "seq", "tower")
    return jax.shard_map(
        body,
        mesh=mesh,
        in_specs=(spec,) * 8 + (P(None, "tower"), P("dp"), P("dp")),
        out_specs=(spec,) * 8 + (P(None, "tower"),),
        check_vma=False,
    )
```
